32 devices in a mesh: fsdp: 8 (over y, x, core), sp: 4 (over z).
Axes of the slice: x: 2, y: 2, z: 4, core: 2. Of those that a mesh axis runs over, the one named last changes fastest.
Arguments:
- tokens: bfloat16 [4096, 5120], P(('fsdp', 'sp')), may hold values from -6 to 6
- norm_gain: float32 [5120], replicated, may hold values from 0.1 to 1.9
- q_weight: bfloat16 [5120, 5120], P('fsdp', 'sp'), may hold values from -0.078125 to 0.078125
- key_matrix: bfloat16 [5120, 1024], P('fsdp', 'sp'), may hold values from -0.078125 to 0.078125
- value_matrix: bfloat16 [5120, 1024], P('fsdp', 'sp'), may hold values from -0.078125 to 0.078125
- q_bias: float32 [5120], P('sp'), may hold values from -8 to 8
- k_bias: float32 [1024], P('sp'), may hold values from -8 to 8
- value_offset_bias: float32 [1024], P('sp'), may hold values from -3 to 3
- out_weight: bfloat16 [5120, 5120], P('fsdp', 'sp'), may hold values from -0.078125 to 0.078125
Outputs:
- mixed: bfloat16 [4096, 5120], P(('fsdp', 'sp'))
The draws below stay inside these ranges and needn't reach their ends.
All inputs are finite; a program needn't handle non-finite values.
Results may differ from the reference program's by a relative error of at most 0.014.
Values may be sent and summed in bfloat16 or wider, within the bound.
No kernel may reach another device: no remote copies, remote signals or barrier semaphores. Data moves between devices by JAX's collectives and lax.ppermute only.
A program may use at most 128 MiB of HBM per device.

```python
import jax
import jax.numpy as jnp
from jax import lax

MODEL_WIDTH = 5120
QUERY_HEADS = 40
KEY_VALUE_HEADS = 8
HEAD_SIZE = 128
SEQ_DEV = 128
TOKENS = 4096
HEAD_SETS = 4
N_FSDP = 8
N_SP = 4


def bias_pair(key):
    random_seed_key = jax.random.fold_in(key, 11)
    query_portion = jnp.clip(0.5 * jax.random.normal(jax.random.fold_in(random_seed_key, 3), (QUERY_HEADS * HEAD_SIZE,), jnp.float32), -8.0, 8.0)
    key_portion = jnp.clip(0.5 * jax.random.normal(jax.random.fold_in(random_seed_key, 4), (KEY_VALUE_HEADS * HEAD_SIZE,), jnp.float32), -8.0, 8.0)
    return (query_portion, key_portion)


def draw_q_bias(key, part):
    return bias_pair(key)[0]


def draw_k_bias(key, part):
    return bias_pair(key)[1]


def level_of(own_key, extent, cuts, least, high):
    def one(dim, shards_of):
        draws = jax.random.uniform(jax.random.fold_in(jax.random.fold_in(own_key, 6), dim), (shards_of,), jnp.float32, least / len(cuts), high / len(cuts))
        return jnp.repeat(jnp.exp(draws), extent[dim] // shards_of).reshape((-1,) + (1,) * (len(extent) - dim - 1))

    factor_of = one(*cuts[0])
    for cut in cuts[1:]:
        factor_of = factor_of * one(*cut)
    return factor_of


def scatter_about(rng, shape, scale, most, pieces=(), held_as=jnp.bfloat16):
    array = jax.random.normal(rng, shape, jnp.float32) * scale
    if len(pieces) > 0:
        array = level_of(rng, shape, pieces, -0.22, 0.18) * array
    return jnp.clip(array, min=-most, max=most).astype(held_as)


def setup_inputs(seed: int = 0) -> dict:
    arg_keys = jax.random.split(jax.random.key(seed), 10)
    tokens = scatter_about(arg_keys[0], (TOKENS, MODEL_WIDTH), 1.0, 6.0, ((0, 32),))
    norm_gain = jnp.clip(1.0 + 0.18 * jax.random.normal(arg_keys[1], (MODEL_WIDTH,), jnp.float32), 0.1, 1.9)
    q_weight = scatter_about(arg_keys[2], (MODEL_WIDTH, QUERY_HEADS * HEAD_SIZE), MODEL_WIDTH ** -0.5, 0.078125, ((0, 8), (1, 4)))
    key_matrix = scatter_about(arg_keys[3], (MODEL_WIDTH, KEY_VALUE_HEADS * HEAD_SIZE), MODEL_WIDTH ** -0.5, 0.078125, ((0, 8), (1, 4)))
    value_matrix = scatter_about(arg_keys[4], (MODEL_WIDTH, KEY_VALUE_HEADS * HEAD_SIZE), MODEL_WIDTH ** -0.5, 0.078125, ((0, 8), (1, 4)))
    q_bias = draw_q_bias(jax.random.fold_in(arg_keys[9], 71), 0)
    k_bias = draw_k_bias(jax.random.fold_in(arg_keys[9], 71), 0)
    value_offset_bias = scatter_about(arg_keys[7], (KEY_VALUE_HEADS * HEAD_SIZE,), 0.5, 3.0, ((0, 4),), jnp.float32)
    out_weight = scatter_about(arg_keys[8], (MODEL_WIDTH, QUERY_HEADS * HEAD_SIZE), (QUERY_HEADS * HEAD_SIZE) ** -0.5, 0.078125, ((0, 8), (1, 4)))
    return dict(tokens=tokens, norm_gain=norm_gain, q_weight=q_weight, key_matrix=key_matrix, value_matrix=value_matrix, q_bias=q_bias, k_bias=k_bias, value_offset_bias=value_offset_bias, out_weight=out_weight)


ROPE_BASE = 1000000.0

def rms_normed(tokens, norm_gain):
    rows = tokens.astype(jnp.float32)
    meansq = lax.optimization_barrier(jnp.mean(rows * rows, axis=-1, keepdims=True))
    return (rows * lax.rsqrt(meansq + 1e-06) * norm_gain).astype(jnp.bfloat16)

def rotary(projected, positions):
    count = projected.shape[0]
    heads_grid = projected.reshape(count, -1, HEAD_SIZE)
    half_dim = HEAD_SIZE // 2
    frequency = ROPE_BASE ** (-(jnp.arange(half_dim, dtype=jnp.float32) * 2.0 / HEAD_SIZE))
    angle = positions[:, None] * frequency[None, :]
    cosine = jnp.cos(angle)[:, None, :]
    sine = jnp.sin(angle)[:, None, :]
    first = heads_grid[..., :half_dim]
    second = heads_grid[..., half_dim:]
    rotated = jnp.concatenate([first * cosine - second * sine, second * cosine + first * sine], axis=-1)
    return rotated.reshape(count, -1)

def attend(queries, keys, values):
    length = queries.shape[0]
    kv_heads = keys.shape[1] // HEAD_SIZE
    group_size = queries.shape[1] // keys.shape[1]
    query_grid = queries.reshape(length, kv_heads, group_size, HEAD_SIZE).astype(jnp.float32)
    key_grid = keys.reshape(length, kv_heads, HEAD_SIZE).astype(jnp.float32)
    value_grid = values.reshape(length, kv_heads, HEAD_SIZE).astype(jnp.float32)
    scores = jnp.einsum('qkgd,skd->kgqs', query_grid, key_grid) / jnp.sqrt(jnp.float32(HEAD_SIZE))
    causal = jnp.arange(length)[:, None] >= jnp.arange(length)[None, :]
    scores = jnp.where(causal, scores, jnp.float32(-1e+30))
    largest = lax.optimization_barrier(jnp.max(scores, axis=-1, keepdims=True))
    weights = jnp.exp(scores - largest)
    totals = lax.optimization_barrier(jnp.sum(weights, axis=-1, keepdims=True))
    probs = (weights / totals).astype(jnp.bfloat16)
    result = jnp.einsum('kgqs,skd->qkgd', probs.astype(jnp.float32), value_grid)
    return result.reshape(length, -1).astype(jnp.bfloat16)

def reference(tokens, norm_gain, q_weight, key_matrix, value_matrix, q_bias, k_bias, value_offset_bias, out_weight):
    length = SEQ_DEV * N_SP
    positions = jnp.arange(length, dtype=jnp.float32)
    set_cols = QUERY_HEADS * HEAD_SIZE // HEAD_SETS
    out_sets = out_weight.reshape(MODEL_WIDTH, HEAD_SETS, set_cols).transpose(1, 0, 2)

    def one_sequence(rows):
        normed = rms_normed(rows, norm_gain)
        queries = rotary(jnp.dot(normed, q_weight, preferred_element_type=jnp.float32) + q_bias, positions).astype(jnp.bfloat16)
        keys = rotary(jnp.dot(normed, key_matrix, preferred_element_type=jnp.float32) + k_bias, positions).astype(jnp.bfloat16)
        values = (jnp.dot(normed, value_matrix, preferred_element_type=jnp.float32) + value_offset_bias).astype(jnp.bfloat16)
        heads = attend(queries, keys, values)
        head_sets = heads.reshape(length, HEAD_SETS, set_cols).transpose(1, 0, 2)

        def add_set(total, pair):
            term = jnp.dot(pair[0], pair[1].T, preferred_element_type=jnp.float32).astype(jnp.bfloat16)
            return (total + term.astype(jnp.float32), 0)
        total, unused = lax.scan(add_set, jnp.zeros((length, MODEL_WIDTH), jnp.float32), (head_sets, out_sets))
        return total.astype(jnp.bfloat16)
    mixed = lax.map(one_sequence, tokens.reshape(N_FSDP, length, MODEL_WIDTH))
    return mixed.reshape(N_FSDP * length, MODEL_WIDTH)
```

```python
import functools

import jax
import jax.numpy as jnp
from jax import lax
from jax.experimental import pallas as pl
from jax.experimental.pallas import tpu as pltpu
from jax.sharding import PartitionSpec as P

HEAD_SIZE = 128
HALF = HEAD_SIZE // 2
ROPE_BASE = 1000000.0
LOG2E = 1.4426950408889634
VMEM_LIMIT = 50 * 1024 * 1024
Z_CHUNKS = 2
NT = (((1,), (1,)), ((), ()))


def params():
    return pltpu.CompilerParams(vmem_limit_bytes=VMEM_LIMIT)


def normed_kernel(n_f, me_ref, tokens_ref, gain_ref, *out_refs):
    rows = tokens_ref[...].astype(jnp.float32)
    scale = lax.rsqrt(jnp.mean(rows * rows, axis=-1, keepdims=True) + 1e-06)
    shard = tokens_ref.shape[1] // n_f
    per_chunk = n_f // len(out_refs)
    for j in range(n_f):
        start = pl.multiple_of(jnp.bitwise_xor(me_ref[0], j) * shard, 128)
        columns = pl.ds(start, shard)
        piece = tokens_ref[:, columns].astype(jnp.float32) * scale * gain_ref[:, columns]
        at = (j % per_chunk) * shard
        out_refs[j // per_chunk][:, at : at + shard] = piece.astype(jnp.bfloat16)


def normed_pieces(me, tokens, gain, n_f, chunks):
    count, width = tokens.shape
    shard = width // n_f
    if shard % 128 == 0:
        return pl.pallas_call(
            functools.partial(normed_kernel, n_f),
            out_shape=[jax.ShapeDtypeStruct((count, width // chunks), jnp.bfloat16)] * chunks,
            in_specs=[
                pl.BlockSpec(memory_space=pltpu.SMEM),
                pl.BlockSpec(memory_space=pltpu.VMEM),
                pl.BlockSpec(memory_space=pltpu.VMEM),
            ],
            out_specs=[pl.BlockSpec(memory_space=pltpu.VMEM)] * chunks,
            compiler_params=params(),
            name="norm",
        )(me[None], tokens, gain[None, :])
    rows = tokens.astype(jnp.float32)
    meansq = jnp.mean(rows * rows, axis=-1, keepdims=True)
    normed = (rows * lax.rsqrt(meansq + 1e-06) * gain).astype(jnp.bfloat16)
    pieces = [
        lax.dynamic_slice_in_dim(normed, jnp.bitwise_xor(me, j) * shard, shard, axis=1)
        for j in range(n_f)
    ]
    per_chunk = n_f // chunks
    return [
        jnp.concatenate(pieces[c * per_chunk : (c + 1) * per_chunk], axis=1) for c in range(chunks)
    ]


def rope_tile(tile, cos, sin):
    parts = []
    for at in range(0, tile.shape[1], HEAD_SIZE):
        head = tile[:, at : at + HEAD_SIZE]
        parts.append(head * cos + pltpu.roll(head, HALF, axis=1) * sin)
    return parts[0] if len(parts) == 1 else jnp.concatenate(parts, axis=1)


def project_kernel(n_f, chunks, q_tiles, k_tiles, *refs):
    x_refs = refs[:chunks]
    q_refs = refs[chunks : chunks + n_f]
    kv_refs = refs[chunks + n_f : chunks + 2 * n_f]
    q_bias, kv_bias, cos_ref, sin_ref, q_out, kv_out = refs[chunks + 2 * n_f :]
    shard = q_refs[0].shape[0]
    per_chunk = n_f // chunks
    step = pl.program_id(0)

    def product(w_refs, bias):
        total = None
        for j in range(n_f):
            at = (j % per_chunk) * shard
            term = jnp.dot(
                x_refs[j // per_chunk][:, at : at + shard],
                w_refs[j][...],
                preferred_element_type=jnp.float32,
            )
            total = term if total is None else total + term
        return total + bias[...]

    @pl.when(step < q_tiles)
    def _():
        tile = product(q_refs, q_bias)
        q_out[...] = rope_tile(tile, cos_ref[...], sin_ref[...]).astype(jnp.bfloat16)

    @pl.when(jnp.logical_and(step >= q_tiles, step < q_tiles + k_tiles))
    def _():
        tile = product(kv_refs, kv_bias)
        kv_out[...] = rope_tile(tile, cos_ref[...], sin_ref[...]).astype(jnp.bfloat16)

    @pl.when(step >= q_tiles + k_tiles)
    def _():
        kv_out[...] = product(kv_refs, kv_bias).astype(jnp.bfloat16)


def project(x_chunks, q_pieces, kv_pieces, q_bias, kv_bias, cos, sin):
    n_f, chunks = len(q_pieces), len(x_chunks)
    count = x_chunks[0].shape[0]
    shard, q_cols = q_pieces[0].shape
    kv_cols = kv_pieces[0].shape[1]
    wide = 256 if q_cols % 256 == 0 and (kv_cols // 2) % 256 == 0 else 128
    q_tiles, kv_tiles = q_cols // wide, kv_cols // wide

    def q_at(i):
        return (0, jnp.minimum(i, q_tiles - 1))

    def kv_at(i):
        return (0, jnp.maximum(i - q_tiles, 0))

    def whole(i):
        return (0, 0)

    return pl.pallas_call(
        functools.partial(project_kernel, n_f, chunks, q_tiles, kv_tiles // 2),
        grid=(q_tiles + kv_tiles,),
        in_specs=[pl.BlockSpec(x.shape, whole, pipeline_mode=pl.Buffered(1)) for x in x_chunks]
        + [pl.BlockSpec((shard, wide), q_at)] * n_f
        + [pl.BlockSpec((shard, wide), kv_at)] * n_f
        + [
            pl.BlockSpec((1, wide), q_at),
            pl.BlockSpec((1, wide), kv_at),
            pl.BlockSpec(cos.shape, whole, pipeline_mode=pl.Buffered(1)),
            pl.BlockSpec(sin.shape, whole, pipeline_mode=pl.Buffered(1)),
        ],
        out_specs=[pl.BlockSpec((count, wide), q_at), pl.BlockSpec((count, wide), kv_at)],
        out_shape=[
            jax.ShapeDtypeStruct((count, q_cols), jnp.bfloat16),
            jax.ShapeDtypeStruct((count, kv_cols), jnp.bfloat16),
        ],
        compiler_params=params(),
        cost_estimate=pl.CostEstimate(
            flops=2 * count * shard * n_f * (q_cols + kv_cols),
            bytes_accessed=2 * shard * n_f * (count + q_cols + kv_cols),
            transcendentals=0,
        ),
        name="project",
    )(*x_chunks, *q_pieces, *kv_pieces, q_bias[None, :], kv_bias[None, :], cos, sin)


def attend_kernel(blocks, group, s_ref, q_ref, k_ref, v_ref, out_ref, keys, values):
    length = q_ref.shape[0]
    rows = length // blocks
    factor = LOG2E / (HEAD_SIZE**0.5)

    def held(b):
        return pl.ds(pl.multiple_of(lax.rem(s_ref[0] - b + blocks, blocks) * rows, rows), rows)

    for b in range(blocks):
        keys[b * rows : (b + 1) * rows, :] = k_ref[held(b), :]
        values[b * rows : (b + 1) * rows, :] = v_ref[held(b), :]
    row = lax.broadcasted_iota(jnp.int32, (rows, rows), 0)
    column = lax.broadcasted_iota(jnp.int32, (rows, rows), 1)
    causal = row >= column
    causal = jnp.concatenate([causal.astype(jnp.float32)] * group, axis=0) > 0.5
    for b in range(blocks):
        q_block = q_ref[held(b), :]
        queries = jnp.concatenate(
            [q_block[:, h * HEAD_SIZE : (h + 1) * HEAD_SIZE] for h in range(group)], axis=0
        )
        at = b * rows
        near = lax.dot_general(
            queries, keys[at : at + rows, :], NT, preferred_element_type=jnp.float32
        )
        near = jnp.where(causal, near, jnp.float32(-1e30))
        largest = jnp.max(near, axis=-1, keepdims=True)
        if b > 0:
            far = lax.dot_general(queries, keys[:at, :], NT, preferred_element_type=jnp.float32)
            largest = jnp.maximum(largest, jnp.max(far, axis=-1, keepdims=True))
        near = jnp.exp2((near - largest) * factor)
        total = jnp.sum(near, axis=-1, keepdims=True)
        result = jnp.dot(
            near.astype(jnp.bfloat16), values[at : at + rows, :], preferred_element_type=jnp.float32
        )
        if b > 0:
            far = jnp.exp2((far - largest) * factor)
            total = total + jnp.sum(far, axis=-1, keepdims=True)
            result = result + jnp.dot(
                far.astype(jnp.bfloat16), values[:at, :], preferred_element_type=jnp.float32
            )
        result = (result / total).astype(jnp.bfloat16)
        for h in range(group):
            out_ref[held(b), h * HEAD_SIZE : (h + 1) * HEAD_SIZE] = result[
                h * rows : (h + 1) * rows, :
            ]


def attend(s, queries, kv, blocks):
    length, q_cols = queries.shape
    kv_heads = kv.shape[1] // (2 * HEAD_SIZE)
    group = q_cols // HEAD_SIZE // kv_heads
    return pl.pallas_call(
        functools.partial(attend_kernel, blocks, group),
        grid=(kv_heads,),
        in_specs=[
            pl.BlockSpec(memory_space=pltpu.SMEM),
            pl.BlockSpec((length, group * HEAD_SIZE), lambda g: (0, g)),
            pl.BlockSpec((length, HEAD_SIZE), lambda g: (0, g)),
            pl.BlockSpec((length, HEAD_SIZE), lambda g: (0, kv_heads + g)),
        ],
        out_specs=pl.BlockSpec((length, group * HEAD_SIZE), lambda g: (0, g)),
        out_shape=jax.ShapeDtypeStruct((length, q_cols), jnp.bfloat16),
        scratch_shapes=[
            pltpu.VMEM((length, HEAD_SIZE), jnp.bfloat16),
            pltpu.VMEM((length, HEAD_SIZE), jnp.bfloat16),
        ],
        compiler_params=params(),
        cost_estimate=pl.CostEstimate(
            flops=4 * length * length * q_cols,
            bytes_accessed=6 * length * q_cols,
            transcendentals=length * length * q_cols // HEAD_SIZE,
        ),
        name="attend",
    )(s[None], queries, kv, kv)


def mix_kernel(core_ref, heads_ref, mine_ref, sibling_ref, *out_refs):
    shard = mine_ref.shape[0]
    rows = out_refs[0].shape[0]

    def write(first_ref, second_ref):
        for at, w_ref in ((0, first_ref), (shard, second_ref)):
            term = lax.dot_general(
                heads_ref[...], w_ref[...], NT, preferred_element_type=jnp.float32
            ).astype(jnp.bfloat16)
            for k, out_ref in enumerate(out_refs):
                out_ref[:, at : at + shard] = term[k * rows : (k + 1) * rows, :]

    @pl.when(core_ref[0] == 0)
    def _():
        write(mine_ref, sibling_ref)

    @pl.when(core_ref[0] != 0)
    def _():
        write(sibling_ref, mine_ref)


def mix(core, heads, mine, sibling, blocks):
    length = heads.shape[0]
    shard, features = mine.shape
    vmem = pl.BlockSpec(memory_space=pltpu.VMEM)
    return pl.pallas_call(
        mix_kernel,
        in_specs=[pl.BlockSpec(memory_space=pltpu.SMEM), vmem, vmem, vmem],
        out_specs=[vmem] * blocks,
        out_shape=[jax.ShapeDtypeStruct((length // blocks, 2 * shard), jnp.bfloat16)] * blocks,
        compiler_params=params(),
        cost_estimate=pl.CostEstimate(
            flops=4 * length * shard * features,
            bytes_accessed=2 * (length * features + 2 * shard * (features + length)),
            transcendentals=0,
        ),
        name="mix",
    )(core[None], heads, mine, sibling)


def swapped(array, n_f, mask):
    return lax.ppermute(array, "fsdp", [(i, i ^ mask) for i in range(n_f)])


def chip_pieces(array, n_f, first_bit):
    chips = n_f // 2
    bits = [b for b in (1, 2, 4, 8, 16, 32) if b < chips]
    if first_bit:
        bits = bits[::-1]
    pieces = {0: array}
    for r in sorted(range(1, chips), key=lambda r: (bin(r).count("1"), r)):
        bit = next(b for b in bits if r & b)
        pieces[r] = swapped(pieces[r ^ bit], n_f, 2 * bit)
    return [pieces[r] for r in range(chips)]


def with_siblings(pieces, n_f):
    both = []
    for piece in pieces:
        both += [piece, swapped(piece, n_f, 1)]
    return both


def after(array, *others):
    return lax.optimization_barrier((array, *others))[0]


def body(
    n_f,
    n_s,
    tokens,
    norm_gain,
    q_weight,
    key_matrix,
    value_matrix,
    q_bias,
    k_bias,
    value_offset_bias,
    out_weight,
):
    me = lax.axis_index("fsdp")
    s = lax.axis_index("sp")
    core = lax.rem(me, 2)
    count = tokens.shape[0]
    ring = [(i, (i + 1) % n_s) for i in range(n_s)]

    blocks = [normed_pieces(me, tokens, norm_gain, n_f, Z_CHUNKS)]
    for _ in range(n_s - 1):
        blocks.append([lax.ppermute(x, "sp", ring) for x in blocks[-1]])

    kv_weight = jnp.concatenate([key_matrix, value_matrix], axis=1)
    q_chips = chip_pieces(q_weight, n_f, True)
    kv_chips = chip_pieces(kv_weight, n_f, False)
    o_chips = chip_pieces(after(out_weight, *q_chips[1:2], *kv_chips[1:2]), n_f, False)
    q_pieces = with_siblings(q_chips, n_f)
    kv_pieces = with_siblings(kv_chips, n_f)
    o_pieces = with_siblings(o_chips, n_f)

    order = lax.rem(s - lax.iota(jnp.int32, n_s) + n_s, n_s)
    positions = (order[:, None] * count + lax.iota(jnp.int32, count)[None, :]).reshape(-1)
    frequency = ROPE_BASE ** (-(jnp.arange(HALF, dtype=jnp.float32) * 2.0 / HEAD_SIZE))
    angle = positions.astype(jnp.float32)[:, None] * frequency[None, :]
    cos, sin = jnp.cos(angle), jnp.sin(angle)
    cos = jnp.concatenate([cos, cos], axis=1)
    sin = jnp.concatenate([-sin, sin], axis=1)

    x_chunks = [jnp.concatenate(parts, axis=0) for parts in zip(*blocks)]
    kv_bias = jnp.concatenate([k_bias, value_offset_bias])
    queries, kv = project(x_chunks, q_pieces, kv_pieces, q_bias, kv_bias, cos, sin)
    heads = attend(s, queries, kv, n_s)

    width = out_weight.shape[0] * n_f
    mixed = jnp.zeros((count, width), jnp.bfloat16)
    chips = n_f // 2
    for r in range(chips):
        terms = mix(core, heads, o_pieces[2 * r], o_pieces[2 * r + 1], n_s)
        total = terms[1 % n_s]
        for k in range(2, n_s + 1):
            arrived = lax.ppermute(total, "sp", ring).astype(jnp.float32)
            total = (arrived + terms[k % n_s].astype(jnp.float32)).astype(jnp.bfloat16)
        at = jnp.bitwise_xor(me // 2, r) * (width // chips)
        mixed = lax.dynamic_update_slice(mixed, total, (0, at))
    return mixed


def solution(mesh):
    n_f, n_s = mesh.shape["fsdp"], mesh.shape["sp"]
    placed = (
        P(("fsdp", "sp"), None),
        P(),
        P("fsdp", "sp"),
        P("fsdp", "sp"),
        P("fsdp", "sp"),
        P("sp"),
        P("sp"),
        P("sp"),
        P("fsdp", "sp"),
    )
    return jax.shard_map(
        functools.partial(body, n_f, n_s),
        mesh=mesh,
        in_specs=placed,
        out_specs=P(("fsdp", "sp"), None),
        check_vma=False,
    )
```

```python
import functools

import jax
import jax.numpy as jnp
from jax import lax
from jax.experimental import pallas as pl
from jax.experimental.pallas import tpu as pltpu
from jax.sharding import PartitionSpec as P

HEAD_SIZE = 128
HALF = HEAD_SIZE // 2
ROPE_BASE = 1000000.0
LOG2E = 1.4426950408889634
VMEM_LIMIT = 50 * 1024 * 1024
Z_CHUNKS = 2
NT = (((1,), (1,)), ((), ()))


def params():
    return pltpu.CompilerParams(vmem_limit_bytes=VMEM_LIMIT)


def normed_kernel(n_f, me_ref, tokens_ref, gain_ref, *out_refs):
    rows = tokens_ref[...].astype(jnp.float32)
    scale = lax.rsqrt(jnp.mean(rows * rows, axis=-1, keepdims=True) + 1e-06)
    shard = tokens_ref.shape[1] // n_f
    per_chunk = n_f // len(out_refs)
    for j in range(n_f):
        start = pl.multiple_of(jnp.bitwise_xor(me_ref[0], j) * shard, 128)
        columns = pl.ds(start, shard)
        piece = tokens_ref[:, columns].astype(jnp.float32) * scale * gain_ref[:, columns]
        at = (j % per_chunk) * shard
        out_refs[j // per_chunk][:, at : at + shard] = piece.astype(jnp.bfloat16)


def normed_pieces(me, tokens, gain, n_f, chunks):
    count, width = tokens.shape
    shard = width // n_f
    if shard % 128 == 0:
        return pl.pallas_call(
            functools.partial(normed_kernel, n_f),
            out_shape=[jax.ShapeDtypeStruct((count, width // chunks), jnp.bfloat16)] * chunks,
            in_specs=[
                pl.BlockSpec(memory_space=pltpu.SMEM),
                pl.BlockSpec(memory_space=pltpu.VMEM),
                pl.BlockSpec(memory_space=pltpu.VMEM),
            ],
            out_specs=[pl.BlockSpec(memory_space=pltpu.VMEM)] * chunks,
            compiler_params=params(),
            name="norm",
        )(me[None], tokens, gain[None, :])
    rows = tokens.astype(jnp.float32)
    meansq = jnp.mean(rows * rows, axis=-1, keepdims=True)
    normed = (rows * lax.rsqrt(meansq + 1e-06) * gain).astype(jnp.bfloat16)
    pieces = [
        lax.dynamic_slice_in_dim(normed, jnp.bitwise_xor(me, j) * shard, shard, axis=1)
        for j in range(n_f)
    ]
    per_chunk = n_f // chunks
    return [
        jnp.concatenate(pieces[c * per_chunk : (c + 1) * per_chunk], axis=1) for c in range(chunks)
    ]


def rope_tile(tile, cos, sin):
    parts = []
    for at in range(0, tile.shape[1], HEAD_SIZE):
        head = tile[:, at : at + HEAD_SIZE]
        parts.append(head * cos + pltpu.roll(head, HALF, axis=1) * sin)
    return parts[0] if len(parts) == 1 else jnp.concatenate(parts, axis=1)


def project_kernel(at_rows, n_x, n_w, wide, roped, *refs):
    x_refs, w_refs = refs[:n_x], refs[n_x : n_x + n_w]
    bias_ref, cos_ref, sin_ref, q_out, kv_out, rows, weights, x_sem, w_sem = refs[n_x + n_w :]
    count, part = x_refs[0].shape
    per_block = rows.shape[1] // part
    q_cols = q_out.shape[1]
    tiles = (q_cols + kv_out.shape[1]) // wide

    def fetch_rows(i):
        place = rows.at[
            pl.ds(i // per_block * count, count), pl.ds(i % per_block * part, part)
        ]
        return pltpu.make_async_copy(x_refs[i], place, x_sem.at[i])

    def fetch_weights(tile, i):
        depth = w_refs[i].shape[0]
        return pltpu.make_async_copy(
            w_refs[i].at[:, pl.ds(tile * wide, wide)],
            weights.at[tile % 2, pl.ds(at_rows[i], depth), :],
            w_sem.at[tile % 2, i],
        )

    for i in range(n_w):
        fetch_weights(0, i).start()
    for i in range(n_x):
        fetch_rows(i).start()
    for i in range(n_x):
        fetch_rows(i).wait()
    for tile in range(tiles):
        for i in range(n_w):
            fetch_weights(tile, i).wait()
        if tile + 1 < tiles:
            for i in range(n_w):
                fetch_weights(tile + 1, i).start()
        at = tile * wide
        total = jnp.dot(rows[...], weights[tile % 2], preferred_element_type=jnp.float32)
        total = total + bias_ref[:, at : at + wide]
        if at < roped:
            total = rope_tile(total, cos_ref[...], sin_ref[...])
        total = total.astype(jnp.bfloat16)
        if at < q_cols:
            q_out[:, at : at + wide] = total
        else:
            kv_out[:, at - q_cols : at - q_cols + wide] = total


def project(blocks, pieces, bias, cos, sin, q_cols):
    x_parts = [chunk for block in blocks for chunk in block]
    w_parts, at_rows, at = [], [], 0
    for piece in pieces:
        for part in piece:
            w_parts.append(part)
            at_rows.append(at)
            at += part.shape[0]
    width, columns = at, w_parts[0].shape[1]
    kv_cols = columns - q_cols
    length = len(blocks) * blocks[0][0].shape[0]
    wide = 256 if q_cols % 256 == 0 and (kv_cols // 2) % 256 == 0 else 128
    vmem = pl.BlockSpec(memory_space=pltpu.VMEM)
    n_x, n_w = len(x_parts), len(w_parts)
    return pl.pallas_call(
        functools.partial(project_kernel, at_rows, n_x, n_w, wide, q_cols + kv_cols // 2),
        in_specs=[pl.BlockSpec(memory_space=pl.ANY)] * (n_x + n_w) + [vmem] * 3,
        out_specs=[vmem, vmem],
        out_shape=[
            jax.ShapeDtypeStruct((length, q_cols), jnp.bfloat16),
            jax.ShapeDtypeStruct((length, kv_cols), jnp.bfloat16),
        ],
        scratch_shapes=[
            pltpu.VMEM((length, width), jnp.bfloat16),
            pltpu.VMEM((2, width, wide), jnp.bfloat16),
            pltpu.SemaphoreType.DMA((n_x,)),
            pltpu.SemaphoreType.DMA((2, n_w)),
        ],
        compiler_params=params(),
        cost_estimate=pl.CostEstimate(
            flops=2 * length * width * columns,
            bytes_accessed=2 * (length * width + columns * (length + width)),
            transcendentals=0,
        ),
        name="project",
    )(*x_parts, *w_parts, bias[None, :], cos, sin)


def attend_kernel(blocks, group, s_ref, q_ref, k_ref, v_ref, out_ref, keys, values):
    length = q_ref.shape[0]
    rows = length // blocks
    factor = LOG2E / (HEAD_SIZE**0.5)

    def held(b):
        return pl.ds(pl.multiple_of(lax.rem(s_ref[0] - b + blocks, blocks) * rows, rows), rows)

    for b in range(blocks):
        keys[b * rows : (b + 1) * rows, :] = k_ref[held(b), :]
        values[b * rows : (b + 1) * rows, :] = v_ref[held(b), :]
    row = lax.broadcasted_iota(jnp.int32, (rows, rows), 0)
    column = lax.broadcasted_iota(jnp.int32, (rows, rows), 1)
    causal = row >= column
    causal = jnp.concatenate([causal.astype(jnp.float32)] * group, axis=0) > 0.5
    for b in range(blocks):
        q_block = q_ref[held(b), :]
        queries = jnp.concatenate(
            [q_block[:, h * HEAD_SIZE : (h + 1) * HEAD_SIZE] for h in range(group)], axis=0
        )
        at = b * rows
        near = lax.dot_general(
            queries, keys[at : at + rows, :], NT, preferred_element_type=jnp.float32
        )
        near = jnp.where(causal, near, jnp.float32(-1e30))
        largest = jnp.max(near, axis=-1, keepdims=True)
        if b > 0:
            far = lax.dot_general(queries, keys[:at, :], NT, preferred_element_type=jnp.float32)
            largest = jnp.maximum(largest, jnp.max(far, axis=-1, keepdims=True))
        near = jnp.exp2((near - largest) * factor)
        total = jnp.sum(near, axis=-1, keepdims=True)
        result = jnp.dot(
            near.astype(jnp.bfloat16), values[at : at + rows, :], preferred_element_type=jnp.float32
        )
        if b > 0:
            far = jnp.exp2((far - largest) * factor)
            total = total + jnp.sum(far, axis=-1, keepdims=True)
            result = result + jnp.dot(
                far.astype(jnp.bfloat16), values[:at, :], preferred_element_type=jnp.float32
            )
        result = (result / total).astype(jnp.bfloat16)
        for h in range(group):
            out_ref[held(b), h * HEAD_SIZE : (h + 1) * HEAD_SIZE] = result[
                h * rows : (h + 1) * rows, :
            ]


def attend(s, queries, kv, blocks):
    length, q_cols = queries.shape
    kv_heads = kv.shape[1] // (2 * HEAD_SIZE)
    group = q_cols // HEAD_SIZE // kv_heads
    return pl.pallas_call(
        functools.partial(attend_kernel, blocks, group),
        grid=(kv_heads,),
        in_specs=[
            pl.BlockSpec(memory_space=pltpu.SMEM),
            pl.BlockSpec((length, group * HEAD_SIZE), lambda g: (0, g)),
            pl.BlockSpec((length, HEAD_SIZE), lambda g: (0, g)),
            pl.BlockSpec((length, HEAD_SIZE), lambda g: (0, kv_heads + g)),
        ],
        out_specs=pl.BlockSpec((length, group * HEAD_SIZE), lambda g: (0, g)),
        out_shape=jax.ShapeDtypeStruct((length, q_cols), jnp.bfloat16),
        scratch_shapes=[
            pltpu.VMEM((length, HEAD_SIZE), jnp.bfloat16),
            pltpu.VMEM((length, HEAD_SIZE), jnp.bfloat16),
        ],
        compiler_params=params(),
        cost_estimate=pl.CostEstimate(
            flops=4 * length * length * q_cols,
            bytes_accessed=6 * length * q_cols,
            transcendentals=length * length * q_cols // HEAD_SIZE,
        ),
        name="attend",
    )(s[None], queries, kv, kv)


def mix_kernel(n_w, heads_ref, *refs):
    w_refs, out_refs = refs[:n_w], refs[n_w:]
    rows = out_refs[0].shape[0]
    at = 0
    for w_ref in w_refs:
        columns = w_ref.shape[0]
        term = lax.dot_general(
            heads_ref[...], w_ref[...], NT, preferred_element_type=jnp.float32
        ).astype(jnp.bfloat16)
        for k, out_ref in enumerate(out_refs):
            out_ref[:, at : at + columns] = term[k * rows : (k + 1) * rows, :]
        at += columns


def mix(heads, pieces, blocks):
    parts = [part for piece in pieces for part in piece]
    length, features = heads.shape
    columns = sum(part.shape[0] for part in parts)
    vmem = pl.BlockSpec(memory_space=pltpu.VMEM)
    return pl.pallas_call(
        functools.partial(mix_kernel, len(parts)),
        in_specs=[vmem] * (1 + len(parts)),
        out_specs=[vmem] * blocks,
        out_shape=[jax.ShapeDtypeStruct((length // blocks, columns), jnp.bfloat16)] * blocks,
        compiler_params=params(),
        cost_estimate=pl.CostEstimate(
            flops=2 * length * columns * features,
            bytes_accessed=2 * (length * features + columns * (features + length)),
            transcendentals=0,
        ),
        name="mix",
    )(heads, *parts)


def swapped(array, n_f, mask):
    return lax.ppermute(array, "fsdp", [(i, i ^ mask) for i in range(n_f)])


def half_of(parts, half):
    if len(parts) == 2:
        return parts[half]
    rows = parts[0].shape[0]
    cut = rows // 2
    return parts[0][:cut] if half == 0 else parts[0][cut:]


def of_level(chips, level):
    return [r for r in range(chips) if bin(r).count("1") == level]


def send_level(held, n_f, level, *before):
    for r in of_level(n_f // 2, level):
        if level == 1:
            held[r] = [swapped(after(held[0][0], *before), n_f, 2 * r)]
        else:
            low, high = r & -r, 1 << (r.bit_length() - 1)
            held[r] = [
                swapped(after(half_of(held[r ^ low], 0), *before), n_f, 2 * low),
                swapped(after(half_of(held[r ^ high], 1), *before), n_f, 2 * high),
            ]


def send_siblings(held, sibling, n_f, level, *before):
    for r in of_level(n_f // 2, level):
        sibling[r] = [swapped(after(part, *before), n_f, 1) for part in held[r]]


def in_order(held, sibling):
    return [side[r] for r in range(len(held)) for side in (held, sibling)]


def after(array, *others):
    return lax.optimization_barrier((array, *others))[0] if others else array


def body(
    n_f,
    n_s,
    tokens,
    norm_gain,
    q_weight,
    key_matrix,
    value_matrix,
    q_bias,
    k_bias,
    value_offset_bias,
    out_weight,
):
    me = lax.axis_index("fsdp")
    s = lax.axis_index("sp")
    count = tokens.shape[0]
    ring = [(i, (i + 1) % n_s) for i in range(n_s)]

    chips = n_f // 2
    levels = chips.bit_length() - 1

    own = normed_pieces(me, tokens, norm_gain, n_f, Z_CHUNKS)
    blocks = [own] + [[None] * Z_CHUNKS for _ in range(n_s - 1)]
    events = (n_s - 1) * Z_CHUNKS
    turns = {events * level // levels: level for level in range(1, levels)}

    held = {0: [jnp.concatenate([q_weight, key_matrix, value_matrix], axis=1)]}
    o_held, sibling, o_sibling = {0: [out_weight]}, {}, {}
    send_level(held, n_f, 1)
    send_siblings(held, sibling, n_f, 0)
    for event in range(events):
        k, c = event // Z_CHUNKS + 1, event % Z_CHUNKS
        blocks[k][c] = arrived = lax.ppermute(blocks[k - 1][c], "sp", ring)
        if event == 0:
            send_siblings(o_held, o_sibling, n_f, 0, arrived)
        if event + 1 in turns:
            level = turns[event + 1]
            send_level(held, n_f, level + 1, arrived)
            send_siblings(held, sibling, n_f, level, arrived)
    send_siblings(held, sibling, n_f, levels, blocks[-1][0])
    send_level(o_held, n_f, 1, *held[chips - 1])

    order = lax.rem(s - lax.iota(jnp.int32, n_s) + n_s, n_s)
    positions = (order[:, None] * count + lax.iota(jnp.int32, count)[None, :]).reshape(-1)
    frequency = ROPE_BASE ** (-(jnp.arange(HALF, dtype=jnp.float32) * 2.0 / HEAD_SIZE))
    angle = positions.astype(jnp.float32)[:, None] * frequency[None, :]
    cos, sin = jnp.cos(angle), jnp.sin(angle)
    cos = jnp.concatenate([cos, cos], axis=1)
    sin = jnp.concatenate([-sin, sin], axis=1)

    bias = jnp.concatenate([q_bias, k_bias, value_offset_bias])
    pieces = in_order(held, sibling)
    queries, kv = project(blocks, pieces, bias, cos, sin, q_weight.shape[1])
    heads = attend(s, queries, kv, n_s)

    shard = out_weight.shape[0]
    mixed = jnp.zeros((count, shard * n_f), jnp.bfloat16)
    for level in range(levels + 1):
        for r in of_level(chips, level):
            pair = (o_held[r], o_sibling[r])
            alone = level in (0, levels)
            for group in ((2 * r,), (2 * r + 1,)) if alone else ((2 * r, 2 * r + 1),):
                terms = mix(heads, [pair[j % 2] for j in group], n_s)
                if level < levels and group[0] == 2 * of_level(chips, level)[-1]:
                    send_siblings(o_held, o_sibling, n_f, level + 1, terms[0])
                    send_level(o_held, n_f, level + 2, terms[0])
                total = terms[1 % n_s]
                for k in range(2, n_s + 1):
                    arrived = lax.ppermute(total, "sp", ring).astype(jnp.float32)
                    total = (arrived + terms[k % n_s].astype(jnp.float32)).astype(jnp.bfloat16)
                for i, j in enumerate(group):
                    at = jnp.bitwise_xor(me, j) * shard
                    mixed = lax.dynamic_update_slice(
                        mixed, total[:, i * shard : (i + 1) * shard], (0, at)
                    )
    return mixed


def solution(mesh):
    n_f, n_s = mesh.shape["fsdp"], mesh.shape["sp"]
    placed = (
        P(("fsdp", "sp"), None),
        P(),
        P("fsdp", "sp"),
        P("fsdp", "sp"),
        P("fsdp", "sp"),
        P("sp"),
        P("sp"),
        P("sp"),
        P("fsdp", "sp"),
    )
    return jax.shard_map(
        functools.partial(body, n_f, n_s),
        mesh=mesh,
        in_specs=placed,
        out_specs=P(("fsdp", "sp"), None),
        check_vma=False,
    )
```

```python
import functools

import jax
import jax.numpy as jnp
from jax import lax
from jax.experimental import pallas as pl
from jax.experimental.pallas import tpu as pltpu
from jax.sharding import PartitionSpec as P

HEAD_SIZE = 128
HALF = HEAD_SIZE // 2
ROPE_BASE = 1000000.0
LOG2E = 1.4426950408889634
VMEM_LIMIT = 50 * 1024 * 1024
Z_CHUNKS = 2
NT = (((1,), (1,)), ((), ()))


def params(mib=16):
    return pltpu.CompilerParams(vmem_limit_bytes=mib * 1024 * 1024)


def normed_kernel(n_f, me_ref, tokens_ref, gain_ref, *out_refs):
    rows = tokens_ref[...].astype(jnp.float32)
    scale = lax.rsqrt(jnp.mean(rows * rows, axis=-1, keepdims=True) + 1e-06)
    shard = tokens_ref.shape[1] // n_f
    per_chunk = n_f // len(out_refs)
    for j in range(n_f):
        start = pl.multiple_of(jnp.bitwise_xor(me_ref[0], j) * shard, 128)
        columns = pl.ds(start, shard)
        piece = tokens_ref[:, columns].astype(jnp.float32) * scale * gain_ref[:, columns]
        at = (j % per_chunk) * shard
        out_refs[j // per_chunk][:, at : at + shard] = piece.astype(jnp.bfloat16)


def normed_pieces(me, tokens, gain, n_f, chunks):
    count, width = tokens.shape
    shard = width // n_f
    if shard % 128 == 0:
        return pl.pallas_call(
            functools.partial(normed_kernel, n_f),
            out_shape=[jax.ShapeDtypeStruct((count, width // chunks), jnp.bfloat16)] * chunks,
            in_specs=[
                pl.BlockSpec(memory_space=pltpu.SMEM),
                pl.BlockSpec(memory_space=pltpu.VMEM),
                pl.BlockSpec(memory_space=pltpu.VMEM),
            ],
            out_specs=[pl.BlockSpec(memory_space=pltpu.VMEM)] * chunks,
            compiler_params=params(),
            name="norm",
        )(me[None], tokens, gain[None, :])
    rows = tokens.astype(jnp.float32)
    meansq = jnp.mean(rows * rows, axis=-1, keepdims=True)
    normed = (rows * lax.rsqrt(meansq + 1e-06) * gain).astype(jnp.bfloat16)
    pieces = [
        lax.dynamic_slice_in_dim(normed, jnp.bitwise_xor(me, j) * shard, shard, axis=1)
        for j in range(n_f)
    ]
    per_chunk = n_f // chunks
    return [
        jnp.concatenate(pieces[c * per_chunk : (c + 1) * per_chunk], axis=1) for c in range(chunks)
    ]


def rope_tile(tile, cos, sin):
    parts = []
    for at in range(0, tile.shape[1], HEAD_SIZE):
        head = tile[:, at : at + HEAD_SIZE]
        parts.append(head * cos + pltpu.roll(head, HALF, axis=1) * sin)
    return parts[0] if len(parts) == 1 else jnp.concatenate(parts, axis=1)


def project_kernel(at_rows, n_x, n_w, wide, roped, *refs):
    x_refs, w_refs = refs[:n_x], refs[n_x : n_x + n_w]
    bias_ref, cos_ref, sin_ref, q_out, kv_out, rows, weights, x_sem, w_sem = refs[n_x + n_w :]
    count, part = x_refs[0].shape
    per_block = rows.shape[1] // part
    q_cols = q_out.shape[1]
    tiles = (q_cols + kv_out.shape[1]) // wide

    def fetch_rows(i):
        place = rows.at[
            pl.ds(i // per_block * count, count), pl.ds(i % per_block * part, part)
        ]
        return pltpu.make_async_copy(x_refs[i], place, x_sem.at[i])

    def fetch_weights(tile, i):
        depth = w_refs[i].shape[0]
        return pltpu.make_async_copy(
            w_refs[i].at[:, pl.ds(tile * wide, wide)],
            weights.at[tile % 2, pl.ds(at_rows[i], depth), :],
            w_sem.at[tile % 2, i],
        )

    for i in range(n_w):
        fetch_weights(0, i).start()
    for i in range(n_x):
        fetch_rows(i).start()
    for i in range(n_x):
        fetch_rows(i).wait()
    for tile in range(tiles):
        for i in range(n_w):
            fetch_weights(tile, i).wait()
        if tile + 1 < tiles:
            for i in range(n_w):
                fetch_weights(tile + 1, i).start()
        at = tile * wide
        total = jnp.dot(rows[...], weights[tile % 2], preferred_element_type=jnp.float32)
        total = total + bias_ref[:, at : at + wide]
        if at < roped:
            total = rope_tile(total, cos_ref[...], sin_ref[...])
        total = total.astype(jnp.bfloat16)
        if at < q_cols:
            q_out[:, at : at + wide] = total
        else:
            kv_out[:, at - q_cols : at - q_cols + wide] = total


def project(blocks, pieces, bias, cos, sin, q_cols):
    x_parts = [chunk for block in blocks for chunk in block]
    w_parts, at_rows, at = [], [], 0
    for piece in pieces:
        for part in piece:
            w_parts.append(part)
            at_rows.append(at)
            at += part.shape[0]
    width, columns = at, w_parts[0].shape[1]
    kv_cols = columns - q_cols
    length = len(blocks) * blocks[0][0].shape[0]
    wide = 256 if q_cols % 256 == 0 and (kv_cols // 2) % 256 == 0 else 128
    vmem = pl.BlockSpec(memory_space=pltpu.VMEM)
    n_x, n_w = len(x_parts), len(w_parts)
    return pl.pallas_call(
        functools.partial(project_kernel, at_rows, n_x, n_w, wide, q_cols + kv_cols // 2),
        in_specs=[pl.BlockSpec(memory_space=pl.ANY)] * (n_x + n_w) + [vmem] * 3,
        out_specs=[vmem, vmem],
        out_shape=[
            jax.ShapeDtypeStruct((length, q_cols), jnp.bfloat16),
            jax.ShapeDtypeStruct((length, kv_cols), jnp.bfloat16),
        ],
        scratch_shapes=[
            pltpu.VMEM((length, width), jnp.bfloat16),
            pltpu.VMEM((2, width, wide), jnp.bfloat16),
            pltpu.SemaphoreType.DMA((n_x,)),
            pltpu.SemaphoreType.DMA((2, n_w)),
        ],
        compiler_params=params(20),
        cost_estimate=pl.CostEstimate(
            flops=2 * length * width * columns,
            bytes_accessed=2 * (length * width + columns * (length + width)),
            transcendentals=0,
        ),
        name="project",
    )(*x_parts, *w_parts, bias[None, :], cos, sin)


def attend_kernel(blocks, group, s_ref, q_ref, k_ref, v_ref, out_ref, keys, values):
    length = q_ref.shape[0]
    rows = length // blocks
    factor = LOG2E / (HEAD_SIZE**0.5)

    def held(b):
        return pl.ds(pl.multiple_of(lax.rem(s_ref[0] - b + blocks, blocks) * rows, rows), rows)

    for b in range(blocks):
        keys[b * rows : (b + 1) * rows, :] = k_ref[held(b), :]
        values[b * rows : (b + 1) * rows, :] = v_ref[held(b), :]
    row = lax.broadcasted_iota(jnp.int32, (rows, rows), 0)
    column = lax.broadcasted_iota(jnp.int32, (rows, rows), 1)
    causal = row >= column
    causal = jnp.concatenate([causal.astype(jnp.float32)] * group, axis=0) > 0.5
    for b in range(blocks):
        q_block = q_ref[held(b), :]
        queries = jnp.concatenate(
            [q_block[:, h * HEAD_SIZE : (h + 1) * HEAD_SIZE] for h in range(group)], axis=0
        )
        at = b * rows
        near = lax.dot_general(
            queries, keys[at : at + rows, :], NT, preferred_element_type=jnp.float32
        )
        near = jnp.where(causal, near, jnp.float32(-1e30))
        largest = jnp.max(near, axis=-1, keepdims=True)
        if b > 0:
            far = lax.dot_general(queries, keys[:at, :], NT, preferred_element_type=jnp.float32)
            largest = jnp.maximum(largest, jnp.max(far, axis=-1, keepdims=True))
        near = jnp.exp2((near - largest) * factor)
        total = jnp.sum(near, axis=-1, keepdims=True)
        result = jnp.dot(
            near.astype(jnp.bfloat16), values[at : at + rows, :], preferred_element_type=jnp.float32
        )
        if b > 0:
            far = jnp.exp2((far - largest) * factor)
            total = total + jnp.sum(far, axis=-1, keepdims=True)
            result = result + jnp.dot(
                far.astype(jnp.bfloat16), values[:at, :], preferred_element_type=jnp.float32
            )
        result = (result / total).astype(jnp.bfloat16)
        for h in range(group):
            out_ref[held(b), h * HEAD_SIZE : (h + 1) * HEAD_SIZE] = result[
                h * rows : (h + 1) * rows, :
            ]


def attend(s, queries, kv, blocks):
    length, q_cols = queries.shape
    kv_heads = kv.shape[1] // (2 * HEAD_SIZE)
    group = q_cols // HEAD_SIZE // kv_heads
    return pl.pallas_call(
        functools.partial(attend_kernel, blocks, group),
        grid=(kv_heads,),
        in_specs=[
            pl.BlockSpec(memory_space=pltpu.SMEM),
            pl.BlockSpec((length, group * HEAD_SIZE), lambda g: (0, g)),
            pl.BlockSpec((length, HEAD_SIZE), lambda g: (0, g)),
            pl.BlockSpec((length, HEAD_SIZE), lambda g: (0, kv_heads + g)),
        ],
        out_specs=pl.BlockSpec((length, group * HEAD_SIZE), lambda g: (0, g)),
        out_shape=jax.ShapeDtypeStruct((length, q_cols), jnp.bfloat16),
        scratch_shapes=[
            pltpu.VMEM((length, HEAD_SIZE), jnp.bfloat16),
            pltpu.VMEM((length, HEAD_SIZE), jnp.bfloat16),
        ],
        compiler_params=params(),
        cost_estimate=pl.CostEstimate(
            flops=4 * length * length * q_cols,
            bytes_accessed=6 * length * q_cols,
            transcendentals=length * length * q_cols // HEAD_SIZE,
        ),
        name="attend",
    )(s[None], queries, kv, kv)


def mix_kernel(n_w, heads_ref, *refs):
    w_refs, out_refs = refs[:n_w], refs[n_w:]
    rows = out_refs[0].shape[0]
    at = 0
    for w_ref in w_refs:
        columns = w_ref.shape[0]
        term = lax.dot_general(
            heads_ref[...], w_ref[...], NT, preferred_element_type=jnp.float32
        ).astype(jnp.bfloat16)
        for k, out_ref in enumerate(out_refs):
            out_ref[:, at : at + columns] = term[k * rows : (k + 1) * rows, :]
        at += columns


def mix(heads, pieces, blocks):
    parts = [part for piece in pieces for part in piece]
    length, features = heads.shape
    columns = sum(part.shape[0] for part in parts)
    vmem = pl.BlockSpec(memory_space=pltpu.VMEM)
    return pl.pallas_call(
        functools.partial(mix_kernel, len(parts)),
        in_specs=[vmem] * (1 + len(parts)),
        out_specs=[vmem] * blocks,
        out_shape=[jax.ShapeDtypeStruct((length // blocks, columns), jnp.bfloat16)] * blocks,
        compiler_params=params(),
        cost_estimate=pl.CostEstimate(
            flops=2 * length * columns * features,
            bytes_accessed=2 * (length * features + columns * (features + length)),
            transcendentals=0,
        ),
        name="mix",
    )(heads, *parts)


def swapped(array, n_f, mask):
    return lax.ppermute(array, "fsdp", [(i, i ^ mask) for i in range(n_f)])


def half_of(parts, half):
    if len(parts) == 2:
        return parts[half]
    rows = parts[0].shape[0]
    cut = rows // 2
    return parts[0][:cut] if half == 0 else parts[0][cut:]


def of_level(chips, level):
    return [r for r in range(chips) if bin(r).count("1") == level]


def send_level(held, n_f, level, *before):
    for r in of_level(n_f // 2, level):
        if level == 1:
            held[r] = [swapped(after(held[0][0], *before), n_f, 2 * r)]
        else:
            low, high = r & -r, 1 << (r.bit_length() - 1)
            held[r] = [
                swapped(after(half_of(held[r ^ low], 0), *before), n_f, 2 * low),
                swapped(after(half_of(held[r ^ high], 1), *before), n_f, 2 * high),
            ]


def send_siblings(held, sibling, n_f, level, *before):
    for r in of_level(n_f // 2, level):
        sibling[r] = [swapped(after(part, *before), n_f, 1) for part in held[r]]


def in_order(held, sibling):
    return [side[r] for r in range(len(held)) for side in (held, sibling)]


def after(array, *others):
    return lax.optimization_barrier((array, *others))[0] if others else array


def body(
    n_f,
    n_s,
    tokens,
    norm_gain,
    q_weight,
    key_matrix,
    value_matrix,
    q_bias,
    k_bias,
    value_offset_bias,
    out_weight,
):
    me = lax.axis_index("fsdp")
    s = lax.axis_index("sp")
    count = tokens.shape[0]
    ring = [(i, (i + 1) % n_s) for i in range(n_s)]

    chips = n_f // 2
    levels = chips.bit_length() - 1

    own = normed_pieces(me, tokens, norm_gain, n_f, Z_CHUNKS)
    blocks = [own] + [[None] * Z_CHUNKS for _ in range(n_s - 1)]
    events = (n_s - 1) * Z_CHUNKS
    turns = {events * level // levels: level for level in range(1, levels)}

    held = {0: [jnp.concatenate([q_weight, key_matrix, value_matrix], axis=1)]}
    o_held, sibling, o_sibling = {0: [out_weight]}, {}, {}
    send_level(held, n_f, 1)
    send_siblings(held, sibling, n_f, 0)
    for event in range(events):
        k, c = event // Z_CHUNKS + 1, event % Z_CHUNKS
        blocks[k][c] = arrived = lax.ppermute(blocks[k - 1][c], "sp", ring)
        if event == 0:
            send_siblings(o_held, o_sibling, n_f, 0, arrived)
        if event + 1 in turns:
            level = turns[event + 1]
            send_level(held, n_f, level + 1, arrived)
            send_siblings(held, sibling, n_f, level, arrived)
    send_siblings(held, sibling, n_f, levels, blocks[-1][0])
    send_level(o_held, n_f, 1, *held[chips - 1])

    order = lax.rem(s - lax.iota(jnp.int32, n_s) + n_s, n_s)
    positions = (order[:, None] * count + lax.iota(jnp.int32, count)[None, :]).reshape(-1)
    frequency = ROPE_BASE ** (-(jnp.arange(HALF, dtype=jnp.float32) * 2.0 / HEAD_SIZE))
    angle = positions.astype(jnp.float32)[:, None] * frequency[None, :]
    cos, sin = jnp.cos(angle), jnp.sin(angle)
    cos = jnp.concatenate([cos, cos], axis=1)
    sin = jnp.concatenate([-sin, sin], axis=1)

    bias = jnp.concatenate([q_bias, k_bias, value_offset_bias])
    pieces = in_order(held, sibling)
    queries, kv = project(blocks, pieces, bias, cos, sin, q_weight.shape[1])
    heads = attend(s, queries, kv, n_s)

    shard = out_weight.shape[0]
    mixed = jnp.zeros((count, shard * n_f), jnp.bfloat16)
    for level in range(levels + 1):
        for r in of_level(chips, level):
            pair = (o_held[r], o_sibling[r])
            alone = level in (0, levels)
            for group in ((2 * r,), (2 * r + 1,)) if alone else ((2 * r, 2 * r + 1),):
                terms = mix(heads, [pair[j % 2] for j in group], n_s)
                if level < levels and group[0] == 2 * of_level(chips, level)[-1]:
                    send_siblings(o_held, o_sibling, n_f, level + 1, terms[0])
                    send_level(o_held, n_f, level + 2, terms[0])
                total = terms[1 % n_s]
                for k in range(2, n_s + 1):
                    arrived = lax.ppermute(total, "sp", ring).astype(jnp.float32)
                    total = (arrived + terms[k % n_s].astype(jnp.float32)).astype(jnp.bfloat16)
                for i, j in enumerate(group):
                    at = jnp.bitwise_xor(me, j) * shard
                    mixed = lax.dynamic_update_slice(
                        mixed, total[:, i * shard : (i + 1) * shard], (0, at)
                    )
    return mixed


def solution(mesh):
    n_f, n_s = mesh.shape["fsdp"], mesh.shape["sp"]
    placed = (
        P(("fsdp", "sp"), None),
        P(),
        P("fsdp", "sp"),
        P("fsdp", "sp"),
        P("fsdp", "sp"),
        P("sp"),
        P("sp"),
        P("sp"),
        P("fsdp", "sp"),
    )
    return jax.shard_map(
        functools.partial(body, n_f, n_s),
        mesh=mesh,
        in_specs=placed,
        out_specs=P(("fsdp", "sp"), None),
        check_vma=False,
    )
```

```python
import functools

import jax
import jax.numpy as jnp
import numpy as np
from jax import lax
from jax.experimental import pallas as pl
from jax.experimental.pallas import tpu as pltpu
from jax.sharding import PartitionSpec as P

HEAD_SIZE = 128
HALF = HEAD_SIZE // 2
ROPE_BASE = 1000000.0
LOG2E = 1.4426950408889634
NT = (((1,), (1,)), ((), ()))
VMEM = pl.BlockSpec(memory_space=pltpu.VMEM)
SMEM = pl.BlockSpec(memory_space=pltpu.SMEM)
ANY = pl.BlockSpec(memory_space=pl.ANY)


def params(mib):
    return pltpu.CompilerParams(vmem_limit_bytes=mib * 1024 * 1024)


def bf16(*shape):
    return jax.ShapeDtypeStruct(shape, jnp.bfloat16)


def work(flops, *arrays):
    size = sum(int(np.prod(x.shape)) * x.dtype.itemsize for x in arrays)
    return pl.CostEstimate(flops=flops, bytes_accessed=size, transcendentals=0)


def normed_kernel(n_f, me_ref, tokens_ref, gain_ref, out_ref):
    rows = tokens_ref[...].astype(jnp.float32)
    scale = lax.rsqrt(jnp.mean(rows * rows, axis=-1, keepdims=True) + 1e-06)
    shard = tokens_ref.shape[1] // n_f
    for j in range(n_f):
        start = pl.multiple_of(jnp.bitwise_xor(me_ref[0], j) * shard, 128)
        columns = pl.ds(start, shard)
        piece = tokens_ref[:, columns].astype(jnp.float32) * scale * gain_ref[:, columns]
        out_ref[:, j * shard : (j + 1) * shard] = piece.astype(jnp.bfloat16)


def normed_pieces(me, tokens, gain, n_f):
    count, width = tokens.shape
    shard = width // n_f
    if shard % 128 == 0:
        return pl.pallas_call(
            functools.partial(normed_kernel, n_f),
            out_shape=bf16(count, width),
            in_specs=[SMEM, VMEM, VMEM],
            out_specs=VMEM,
            compiler_params=params(16),
            cost_estimate=work(6 * count * width, tokens, tokens),
            name="norm",
        )(me[None], tokens, gain[None, :])
    rows = tokens.astype(jnp.float32)
    meansq = jnp.mean(rows * rows, axis=-1, keepdims=True)
    normed = (rows * lax.rsqrt(meansq + 1e-06) * gain).astype(jnp.bfloat16)
    pieces = [
        lax.dynamic_slice_in_dim(normed, jnp.bitwise_xor(me, j) * shard, shard, axis=1)
        for j in range(n_f)
    ]
    return jnp.concatenate(pieces, axis=1)


def pack_kernel(q_ref, k_ref, v_ref, first_ref, second_ref):
    q_cols, kv_cols, cut = q_ref.shape[1], k_ref.shape[1], first_ref.shape[1]
    first_ref[...] = q_ref[:, :cut]
    second_ref[:, : q_cols - cut] = q_ref[:, cut:]
    second_ref[:, q_cols - cut : q_cols - cut + kv_cols] = k_ref[...]
    second_ref[:, q_cols - cut + kv_cols :] = v_ref[...]


def pack(q, k, v, cut):
    rows = q.shape[0]
    total = q.shape[1] + 2 * k.shape[1]
    return pl.pallas_call(
        pack_kernel,
        in_specs=[VMEM] * 3,
        out_specs=[VMEM] * 2,
        out_shape=[bf16(rows, cut), bf16(rows, total - cut)],
        compiler_params=params(16),
        cost_estimate=work(0, q, k, v, q, k, v),
        name="pack",
    )(q, k, v)


def cut_kernel(w_ref, first_ref, second_ref):
    cut = first_ref.shape[0]
    first_ref[...] = w_ref[:cut, :]
    second_ref[...] = w_ref[cut:, :]


def cut_rows(w, cut):
    rows, columns = w.shape
    return pl.pallas_call(
        cut_kernel,
        in_specs=[VMEM],
        out_specs=[VMEM] * 2,
        out_shape=[bf16(cut, columns), bf16(rows - cut, columns)],
        compiler_params=params(16),
        cost_estimate=work(0, w, w),
        name="cut",
    )(w)


def partial_kernel(n_x, n_r, wide, *refs):
    x_refs, w_refs, (out_ref, rows) = refs[:n_x], refs[n_x:-2], refs[-2:]
    count = x_refs[0].shape[0]
    shard = w_refs[0].shape[0]
    for i, x_ref in enumerate(x_refs):
        rows[i * count : (i + 1) * count, :] = x_ref[:, : rows.shape[1]]
    base = 0
    for h in range(2):
        half = w_refs[2 * n_r * h : 2 * n_r * (h + 1)]
        for at in range(0, half[0].shape[1], wide):
            total = None
            for j, w_ref in enumerate(half):
                term = jnp.dot(
                    rows[:, j * shard : (j + 1) * shard],
                    w_ref[:, at : at + wide],
                    preferred_element_type=jnp.float32,
                )
                total = term if total is None else total + term
            out_ref[:, base + at : base + at + wide] = total
        base += half[0].shape[1]


def partial(blocks, first, second, wide):
    n_x, n_r = len(blocks), len(first) // 2
    count = blocks[0].shape[0]
    depth = 2 * n_r * first[0].shape[0]
    columns = first[0].shape[1] + second[0].shape[1]
    out = jax.ShapeDtypeStruct((n_x * count, columns), jnp.float32)
    return pl.pallas_call(
        functools.partial(partial_kernel, n_x, n_r, wide),
        in_specs=[VMEM] * (n_x + 4 * n_r),
        out_specs=VMEM,
        out_shape=out,
        scratch_shapes=[pltpu.VMEM((n_x * count, depth), jnp.bfloat16)],
        compiler_params=params(16),
        cost_estimate=work(
            2 * n_x * count * depth * columns, *blocks, *first, *second, out
        ),
        name="partial",
    )(*blocks, *first, *second)


def rope_tile(tile, cos, sin):
    parts = []
    for at in range(0, tile.shape[1], HEAD_SIZE):
        head = tile[:, at : at + HEAD_SIZE]
        parts.append(head * cos + pltpu.roll(head, HALF, axis=1) * sin)
    return parts[0] if len(parts) == 1 else jnp.concatenate(parts, axis=1)


def finish_kernel(n_x, wide, roped, first_col, s_ref, *refs):
    x_refs = refs[:n_x]
    w_refs = refs[n_x : n_x + 4]
    early_ref, late_ref = refs[n_x + 4 : n_x + 6]
    bias_refs, (cos_ref, sin_ref) = refs[n_x + 6 : n_x + 9], refs[n_x + 9 : n_x + 11]
    q_out, kv_out, rows, cos, sin = refs[n_x + 11 :]
    count = x_refs[0].shape[0]
    shard = w_refs[0].shape[0]
    cut = early_ref.shape[0]
    for i, x_ref in enumerate(x_refs):
        here = slice(i * count, (i + 1) * count)
        rows[here, :] = x_ref[:, first_col : first_col + 2 * shard]
        place = pl.ds(pl.multiple_of(lax.rem(s_ref[0] - i + n_x, n_x) * count, count), count)
        cos[here, :] = cos_ref[place, :]
        sin[here, :] = sin_ref[place, :]
    q_cols = q_out.shape[1]

    def bias_tile(col):
        for bias_ref in bias_refs:
            if col < bias_ref.shape[0]:
                return bias_ref[pl.ds(col, wide)][None, :]
            col -= bias_ref.shape[0]

    base = 0
    for mine, sibling in (w_refs[:2], w_refs[2:]):
        for at in range(0, mine.shape[1], wide):
            total = jnp.dot(
                rows[:, :shard], mine[:, at : at + wide], preferred_element_type=jnp.float32
            )
            total = total + jnp.dot(
                rows[:, shard:], sibling[:, at : at + wide], preferred_element_type=jnp.float32
            )
            col = base + at
            total = total + jnp.concatenate(
                [early_ref[:, col : col + wide], late_ref[:, col : col + wide]], axis=0
            )
            total = total + bias_tile(col)
            if col < roped:
                total = rope_tile(total, cos[...], sin[...])
            total = total.astype(jnp.bfloat16)
            if col < q_cols:
                q_out[:, col : col + wide] = total
            else:
                kv_out[:, col - q_cols : col - q_cols + wide] = total
        base += mine.shape[1]


def finish(s, blocks, weights, early, late, biases, cos, sin, q_cols, first_col, wide):
    n_x, count = len(blocks), blocks[0].shape[0]
    shard = weights[0].shape[0]
    columns = early.shape[1]
    kv_cols = columns - q_cols
    length = n_x * count
    return pl.pallas_call(
        functools.partial(finish_kernel, n_x, wide, q_cols + kv_cols // 2, first_col),
        in_specs=[SMEM] + [VMEM] * (n_x + 11),
        out_specs=[VMEM, VMEM],
        out_shape=[bf16(length, q_cols), bf16(length, kv_cols)],
        scratch_shapes=[
            pltpu.VMEM((length, 2 * shard), jnp.bfloat16),
            pltpu.VMEM((length, HEAD_SIZE), jnp.float32),
            pltpu.VMEM((length, HEAD_SIZE), jnp.float32),
        ],
        compiler_params=params(16),
        cost_estimate=work(4 * length * shard * columns, *weights, early, late),
        name="finish",
    )(s[None], *blocks, *weights, early, late, *biases, cos, sin)


def attend_kernel(blocks, group, s_ref, q_ref, kv_ref, out_ref, keys, values):
    length = q_ref.shape[0]
    rows = length // blocks
    factor = LOG2E / (HEAD_SIZE**0.5)

    def held(b):
        return pl.ds(pl.multiple_of(lax.rem(s_ref[0] - b + blocks, blocks) * rows, rows), rows)

    kv_half = kv_ref.shape[1] // 2
    for b in range(blocks):
        keys[b * rows : (b + 1) * rows, :] = kv_ref[held(b), :kv_half]
        values[b * rows : (b + 1) * rows, :] = kv_ref[held(b), kv_half:]
    row = lax.broadcasted_iota(jnp.int32, (rows, rows), 0)
    column = lax.broadcasted_iota(jnp.int32, (rows, rows), 1)
    causal = row >= column
    causal = jnp.concatenate([causal.astype(jnp.float32)] * group, axis=0) > 0.5
    for g, b in [(g, b) for g in range(kv_half // HEAD_SIZE) for b in range(blocks)]:
        left = g * group * HEAD_SIZE
        head = slice(g * HEAD_SIZE, (g + 1) * HEAD_SIZE)
        q_block = q_ref[held(b), left : left + group * HEAD_SIZE]
        queries = jnp.concatenate(
            [q_block[:, h * HEAD_SIZE : (h + 1) * HEAD_SIZE] for h in range(group)], axis=0
        )
        at = b * rows
        near = lax.dot_general(
            queries, keys[at : at + rows, head], NT, preferred_element_type=jnp.float32
        )
        near = jnp.where(causal, near, jnp.float32(-1e30))
        largest = jnp.max(near, axis=-1, keepdims=True)
        if b > 0:
            far = lax.dot_general(queries, keys[:at, head], NT, preferred_element_type=jnp.float32)
            largest = jnp.maximum(largest, jnp.max(far, axis=-1, keepdims=True))
        near = jnp.exp2((near - largest) * factor)
        total = jnp.sum(near, axis=-1, keepdims=True)
        result = jnp.dot(
            near.astype(jnp.bfloat16), values[at : at + rows, head], preferred_element_type=jnp.float32
        )
        if b > 0:
            far = jnp.exp2((far - largest) * factor)
            total = total + jnp.sum(far, axis=-1, keepdims=True)
            result = result + jnp.dot(
                far.astype(jnp.bfloat16), values[:at, head], preferred_element_type=jnp.float32
            )
        result = (result / total).astype(jnp.bfloat16)
        for h in range(group):
            out_ref[held(b), left + h * HEAD_SIZE : left + (h + 1) * HEAD_SIZE] = result[
                h * rows : (h + 1) * rows, :
            ]


def attend(s, queries, kv, blocks):
    length, q_cols = queries.shape
    kv_half = kv.shape[1] // 2
    return pl.pallas_call(
        functools.partial(attend_kernel, blocks, q_cols // kv_half),
        in_specs=[SMEM, VMEM, VMEM],
        out_specs=VMEM,
        out_shape=bf16(length, q_cols),
        scratch_shapes=[
            pltpu.VMEM((length, kv_half), jnp.bfloat16),
            pltpu.VMEM((length, kv_half), jnp.bfloat16),
        ],
        compiler_params=params(16),
        cost_estimate=work(4 * length * length * q_cols, queries, queries, kv),
        name="attend",
    )(s[None], queries, kv)


def mix_kernel(n_w, heads_ref, *refs):
    w_refs, out_refs = refs[:n_w], refs[n_w:]
    rows = out_refs[0].shape[0]
    weights = [w_ref[...] for w_ref in w_refs]
    weights = weights[0] if n_w == 1 else jnp.concatenate(weights, axis=0)
    term = lax.dot_general(
        heads_ref[...], weights, NT, preferred_element_type=jnp.float32
    ).astype(jnp.bfloat16)
    for k, out_ref in enumerate(out_refs):
        out_ref[...] = term[k * rows : (k + 1) * rows, :]


def mix(heads, parts, blocks):
    length, features = heads.shape
    columns = sum(part.shape[0] for part in parts)
    return pl.pallas_call(
        functools.partial(mix_kernel, len(parts)),
        in_specs=[VMEM] * (1 + len(parts)),
        out_specs=[VMEM] * blocks,
        out_shape=[bf16(length // blocks, columns)] * blocks,
        compiler_params=params(16),
        cost_estimate=work(2 * length * columns * features, heads, *parts),
        name="mix",
    )(heads, *parts)


def add_kernel(a_ref, b_ref, out_ref):
    total = a_ref[...].astype(jnp.float32) + b_ref[...].astype(jnp.float32)
    out_ref[...] = total.astype(jnp.bfloat16)


def add(a, b):
    return pl.pallas_call(
        add_kernel,
        in_specs=[VMEM, VMEM],
        out_specs=VMEM,
        out_shape=bf16(*a.shape),
        compiler_params=params(8),
        cost_estimate=work(0, a, a, a),
        name="add",
    )(a, b)


def place_kernel(parts, me_ref, a_ref, b_ref, *refs):
    out_ref, total, sem = refs[-3:]
    add_kernel(a_ref, b_ref, total)
    copies, left = [], 0
    for i, (j, shard, offset, width) in enumerate(parts):
        start = pl.multiple_of(jnp.bitwise_xor(me_ref[0], j) * shard + offset, 128)
        copies.append(
            pltpu.make_async_copy(
                total.at[:, pl.ds(left, width)], out_ref.at[:, pl.ds(start, width)], sem.at[i]
            )
        )
        left += width
    for copy in copies:
        copy.start()
    for copy in copies:
        copy.wait()


def place(mixed, me, a, b, parts, columns):
    if any(offset % 128 or width % 128 or shard % 128 for _, shard, offset, width in parts):
        total, left = add(a, b), 0
        if mixed is None:
            mixed = jnp.zeros((a.shape[0], columns), jnp.bfloat16)
        for j, shard, offset, width in parts:
            start = jnp.bitwise_xor(me, j) * shard + offset
            mixed = lax.dynamic_update_slice(mixed, total[:, left : left + width], (0, start))
            left += width
        return mixed
    held = [] if mixed is None else [mixed]
    return pl.pallas_call(
        functools.partial(place_kernel, parts),
        in_specs=[SMEM, VMEM, VMEM] + [ANY] * len(held),
        out_specs=ANY,
        out_shape=bf16(a.shape[0], columns),
        scratch_shapes=[
            pltpu.VMEM(a.shape, jnp.bfloat16),
            pltpu.SemaphoreType.DMA((len(parts),)),
        ],
        input_output_aliases={3: 0} if held else {},
        compiler_params=params(8),
        cost_estimate=work(0, a, a, a),
        name="place",
    )(me[None], a, b, *held)


def swapped(array, n_f, mask):
    return lax.ppermute(array, "fsdp", [(i, i ^ mask) for i in range(n_f)])


def after(array, *others):
    return lax.optimization_barrier((array, *others))[0] if others else array


def phase_of(piece):
    r, half = piece
    bits = bin(r).count("1")
    if bits <= 1:
        return bits if half == (1 if r == 1 else 0) else 2 * bits
    return bits + 1


def send_phase(held, n_f, phase, *before):
    sent = [(r, h) for r in range(1, n_f // 2) for h in range(2) if phase_of((r, h)) == phase]
    for r, half in sent:
        bit = r & -r if half == 0 else 1 << (r.bit_length() - 1)
        held[r, half] = swapped(after(held[r ^ bit, half], *before), n_f, 2 * bit)
    return [held[piece] for piece in sent]


def send_siblings(held, sibling, n_f, phase, *before):
    for piece in [piece for piece in held if phase_of(piece) == phase]:
        sibling[piece] = swapped(after(held[piece], *before), n_f, 1)


def rope_tables(length):
    frequency = np.float32(ROPE_BASE) ** (
        -(np.arange(HALF, dtype=np.float32) * np.float32(2.0) / np.float32(HEAD_SIZE))
    )
    angle = np.arange(length, dtype=np.float32)[:, None] * frequency[None, :].astype(np.float32)
    angle = angle.astype(np.float64)
    cos, sin = np.cos(angle).astype(np.float32), np.sin(angle).astype(np.float32)
    return np.concatenate([cos, cos], axis=1), np.concatenate([-sin, sin], axis=1)


def body(
    n_f,
    n_s,
    tokens,
    norm_gain,
    q_weight,
    key_matrix,
    value_matrix,
    q_bias,
    k_bias,
    value_offset_bias,
    out_weight,
):
    me = lax.axis_index("fsdp")
    s = lax.axis_index("sp")
    count = tokens.shape[0]
    chips = n_f // 2
    phases = chips.bit_length()
    shard, q_cols = q_weight.shape
    kv_cols = key_matrix.shape[1]
    wide = 256 if q_cols % 256 == 0 and kv_cols % 256 == 0 else 128
    cut = (q_cols + 2 * kv_cols) // wide // 2 * wide
    cut += wide if cut + wide <= q_cols else 0
    ring = [(i, (i + 1) % n_s) for i in range(n_s)]
    cos, sin = rope_tables(n_s * count)

    blocks = [normed_pieces(me, tokens, norm_gain, n_f)]
    first, second = pack(after(q_weight, blocks[0]), key_matrix, value_matrix, cut)
    held, sibling = {(0, 0): first, (0, 1): second}, {}
    send_siblings(held, sibling, n_f, 0)
    o_cut = shard * 3 // 5 // 128 * 128 or shard // 2 // 16 * 16
    o_first, o_second = cut_rows(after(out_weight, first), o_cut)
    o_held, o_sibling = {(0, 0): o_first, (0, 1): o_second}, {}

    gates, sent = [], []
    for k in range(1, n_s):
        if k <= phases:
            sent = send_phase(held, n_f, k, *gates[-1:], *sent)
            if k > 1:
                send_siblings(held, sibling, n_f, k - 1, *gates[-1:])
        blocks.append(lax.ppermute(blocks[-1], "sp", ring))
        gates.append(blocks[-1])
    send_siblings(o_held, o_sibling, n_f, 0, gates[0])

    def parts(half, chosen):
        return [side[r, half] for r in chosen for side in (held, sibling)]

    most = range(chips - 1)
    early = partial(blocks[:-1], parts(0, most), parts(1, most), wide)
    send_siblings(held, sibling, n_f, phases, gates[-1], early)
    send_phase(o_held, n_f, 1, gates[-1], early)
    late = partial(blocks[-1:], parts(0, most), parts(1, most), wide)
    last = parts(0, [chips - 1]) + parts(1, [chips - 1])
    queries, kv = finish(
        s,
        blocks,
        last,
        early,
        late,
        (q_bias, k_bias, value_offset_bias),
        cos,
        sin,
        q_cols,
        2 * shard * (chips - 1),
        wide,
    )
    heads = attend(s, queries, kv, n_s)

    mixed, rings, previous = None, [], []

    def mix_group(group):
        nonlocal mixed
        weights = [(o_sibling if core else o_held)[r, half] for r, half, core in group]
        t = len(rings) - 2
        behind = [rings[t - d][d] for d in range(n_s - 1) if t - d >= 0]
        terms = mix(after(heads, *behind, *previous), weights, n_s)
        previous[:] = terms[:1]
        total, arrivals = terms[1], []
        for k in range(2, n_s + 1):
            arrivals.append(lax.ppermute(total, "sp", ring))
            if k < n_s:
                total = add(arrivals[-1], terms[k])
        where = [
            (2 * r + core, shard, half * o_cut, w.shape[0])
            for (r, half, core), w in zip(group, weights)
        ]
        mixed = place(mixed, me, arrivals[-1], terms[0], where, shard * n_f)
        rings.append(arrivals)

    mix_group([(0, 0, 0), (0, 1, 0)])
    mix_group([(0, 0, 1), (0, 1, 1)])
    for phase in range(1, phases + 1):
        gate = rings[-2][0]
        send_siblings(o_held, o_sibling, n_f, phase, gate)
        send_phase(o_held, n_f, phase + 1, gate)
        for piece in [piece for piece in o_held if phase_of(piece) == phase]:
            mix_group([(*piece, 0), (*piece, 1)])
    return mixed


def solution(mesh):
    n_f, n_s = mesh.shape["fsdp"], mesh.shape["sp"]
    placed = (
        P(("fsdp", "sp"), None),
        P(),
        P("fsdp", "sp"),
        P("fsdp", "sp"),
        P("fsdp", "sp"),
        P("sp"),
        P("sp"),
        P("sp"),
        P("fsdp", "sp"),
    )
    return jax.shard_map(
        functools.partial(body, n_f, n_s),
        mesh=mesh,
        in_specs=placed,
        out_specs=P(("fsdp", "sp"), None),
        check_vma=False,
    )
```

```python
import functools

import jax
import jax.numpy as jnp
import numpy as np
from jax import lax
from jax.experimental import pallas as pl
from jax.experimental.pallas import tpu as pltpu
from jax.sharding import PartitionSpec as P

HEAD_SIZE = 128
HALF = HEAD_SIZE // 2
ROPE_BASE = 1000000.0
LOG2E = 1.4426950408889634
NT = (((1,), (1,)), ((), ()))
VMEM = pl.BlockSpec(memory_space=pltpu.VMEM)
SMEM = pl.BlockSpec(memory_space=pltpu.SMEM)
ANY = pl.BlockSpec(memory_space=pl.ANY)


def params(mib):
    return pltpu.CompilerParams(vmem_limit_bytes=mib * 1024 * 1024)


def bf16(*shape):
    return jax.ShapeDtypeStruct(shape, jnp.bfloat16)


def work(flops, *arrays):
    size = sum(int(np.prod(x.shape)) * x.dtype.itemsize for x in arrays)
    return pl.CostEstimate(flops=flops, bytes_accessed=size, transcendentals=0)


def normed_kernel(n_f, index_ref, tokens_ref, gain_ref, out_ref):
    rows = tokens_ref[...].astype(jnp.float32)
    scale = lax.rsqrt(jnp.mean(rows * rows, axis=-1, keepdims=True) + 1e-06)
    shard = tokens_ref.shape[1] // n_f
    for j in range(n_f):
        start = pl.multiple_of(jnp.bitwise_xor(index_ref[0], j) * shard, 128)
        columns = pl.ds(start, shard)
        piece = tokens_ref[:, columns].astype(jnp.float32) * scale * gain_ref[:, columns]
        out_ref[:, j * shard : (j + 1) * shard] = piece.astype(jnp.bfloat16)


def normed_pieces(index, tokens, gain, n_f):
    count, width = tokens.shape
    shard = width // n_f
    if shard % 128 == 0:
        return pl.pallas_call(
            functools.partial(normed_kernel, n_f),
            out_shape=bf16(count, width),
            in_specs=[SMEM, VMEM, VMEM],
            out_specs=VMEM,
            compiler_params=params(16),
            cost_estimate=work(6 * count * width, tokens, tokens),
            name="norm",
        )(index, tokens, gain[None, :])
    rows = tokens.astype(jnp.float32)
    meansq = jnp.mean(rows * rows, axis=-1, keepdims=True)
    normed = (rows * lax.rsqrt(meansq + 1e-06) * gain).astype(jnp.bfloat16)
    pieces = [
        lax.dynamic_slice_in_dim(normed, jnp.bitwise_xor(index[0], j) * shard, shard, axis=1)
        for j in range(n_f)
    ]
    return jnp.concatenate(pieces, axis=1)


def pack_kernel(q_ref, k_ref, v_ref, first_ref, second_ref):
    q_cols, kv_cols, cut = q_ref.shape[1], k_ref.shape[1], first_ref.shape[1]
    first_ref[...] = q_ref[:, :cut]
    second_ref[:, : q_cols - cut] = q_ref[:, cut:]
    second_ref[:, q_cols - cut : q_cols - cut + kv_cols] = k_ref[...]
    second_ref[:, q_cols - cut + kv_cols :] = v_ref[...]


def pack(q, k, v, cut):
    rows = q.shape[0]
    total = q.shape[1] + 2 * k.shape[1]
    return pl.pallas_call(
        pack_kernel,
        in_specs=[VMEM] * 3,
        out_specs=[VMEM] * 2,
        out_shape=[bf16(rows, cut), bf16(rows, total - cut)],
        compiler_params=params(16),
        cost_estimate=work(0, q, k, v, q, k, v),
        name="pack",
    )(q, k, v)


def cut_kernel(start, w_ref, out_ref):
    out_ref[...] = w_ref[start : start + out_ref.shape[0], :]


def cut_rows(w, cut, half):
    rows, columns = w.shape
    return pl.pallas_call(
        functools.partial(cut_kernel, cut if half else 0),
        in_specs=[VMEM],
        out_specs=VMEM,
        out_shape=bf16(rows - cut if half else cut, columns),
        compiler_params=params(16),
        cost_estimate=work(0, w),
        name="cut",
    )(w)


def partial_kernel(n_x, n_r, wide, *refs):
    x_refs, w_refs, (out_ref, rows) = refs[:n_x], refs[n_x:-2], refs[-2:]
    count = x_refs[0].shape[0]
    shard = w_refs[0].shape[0]
    for i, x_ref in enumerate(x_refs):
        rows[i * count : (i + 1) * count, :] = x_ref[:, : rows.shape[1]]
    base = 0
    for h in range(2):
        half = w_refs[2 * n_r * h : 2 * n_r * (h + 1)]
        for at in range(0, half[0].shape[1], wide):
            total = None
            for j, w_ref in enumerate(half):
                term = jnp.dot(
                    rows[:, j * shard : (j + 1) * shard],
                    w_ref[:, at : at + wide],
                    preferred_element_type=jnp.float32,
                )
                total = term if total is None else total + term
            out_ref[:, base + at : base + at + wide] = total
        base += half[0].shape[1]


def partial(blocks, first, second, wide):
    n_x, n_r = len(blocks), len(first) // 2
    count = blocks[0].shape[0]
    depth = 2 * n_r * first[0].shape[0]
    columns = first[0].shape[1] + second[0].shape[1]
    out = jax.ShapeDtypeStruct((n_x * count, columns), jnp.float32)
    return pl.pallas_call(
        functools.partial(partial_kernel, n_x, n_r, wide),
        in_specs=[VMEM] * (n_x + 4 * n_r),
        out_specs=VMEM,
        out_shape=out,
        scratch_shapes=[pltpu.VMEM((n_x * count, depth), jnp.bfloat16)],
        compiler_params=params(16),
        cost_estimate=work(
            2 * n_x * count * depth * columns, *blocks, *first, *second, out
        ),
        name="partial",
    )(*blocks, *first, *second)


def rope_tile(tile, cos, sin):
    parts = []
    for at in range(0, tile.shape[1], HEAD_SIZE):
        head = tile[:, at : at + HEAD_SIZE]
        parts.append(head * cos + pltpu.roll(head, HALF, axis=1) * sin)
    return parts[0] if len(parts) == 1 else jnp.concatenate(parts, axis=1)


def finish_kernel(n_x, wide, roped, first_col, index_ref, *refs):
    x_refs = refs[:n_x]
    w_refs = refs[n_x : n_x + 4]
    early_ref, late_ref = refs[n_x + 4 : n_x + 6]
    bias_refs, (cos_ref, sin_ref) = refs[n_x + 6 : n_x + 9], refs[n_x + 9 : n_x + 11]
    q_out, kv_out, rows, cos, sin = refs[n_x + 11 :]
    count = x_refs[0].shape[0]
    shard = w_refs[0].shape[0]
    cut = early_ref.shape[0]
    for i, x_ref in enumerate(x_refs):
        here = slice(i * count, (i + 1) * count)
        rows[here, :] = x_ref[:, first_col : first_col + 2 * shard]
        place = pl.ds(pl.multiple_of(lax.rem(index_ref[1] - i + n_x, n_x) * count, count), count)
        cos[here, :] = cos_ref[place, :]
        sin[here, :] = sin_ref[place, :]
    q_cols = q_out.shape[1]

    def bias_tile(col):
        for bias_ref in bias_refs:
            if col < bias_ref.shape[0]:
                return bias_ref[pl.ds(col, wide)][None, :]
            col -= bias_ref.shape[0]

    base = 0
    for mine, sibling in (w_refs[:2], w_refs[2:]):
        for at in range(0, mine.shape[1], wide):
            total = jnp.dot(
                rows[:, :shard], mine[:, at : at + wide], preferred_element_type=jnp.float32
            )
            total = total + jnp.dot(
                rows[:, shard:], sibling[:, at : at + wide], preferred_element_type=jnp.float32
            )
            col = base + at
            total = total + jnp.concatenate(
                [early_ref[:, col : col + wide], late_ref[:, col : col + wide]], axis=0
            )
            total = total + bias_tile(col)
            if col < roped:
                total = rope_tile(total, cos[...], sin[...])
            total = total.astype(jnp.bfloat16)
            if col < q_cols:
                q_out[:, col : col + wide] = total
            else:
                kv_out[:, col - q_cols : col - q_cols + wide] = total
        base += mine.shape[1]


def finish(index, blocks, weights, early, late, biases, cos, sin, q_cols, first_col, wide):
    n_x, count = len(blocks), blocks[0].shape[0]
    shard = weights[0].shape[0]
    columns = early.shape[1]
    kv_cols = columns - q_cols
    length = n_x * count
    return pl.pallas_call(
        functools.partial(finish_kernel, n_x, wide, q_cols + kv_cols // 2, first_col),
        in_specs=[SMEM] + [VMEM] * (n_x + 11),
        out_specs=[VMEM, VMEM],
        out_shape=[bf16(length, q_cols), bf16(length, kv_cols)],
        scratch_shapes=[
            pltpu.VMEM((length, 2 * shard), jnp.bfloat16),
            pltpu.VMEM((length, HEAD_SIZE), jnp.float32),
            pltpu.VMEM((length, HEAD_SIZE), jnp.float32),
        ],
        compiler_params=params(16),
        cost_estimate=work(4 * length * shard * columns, *weights, early, late),
        name="finish",
    )(index, *blocks, *weights, early, late, *biases, cos, sin)


def attend_kernel(blocks, group, index_ref, q_ref, kv_ref, out_ref, keys, values):
    length = q_ref.shape[0]
    rows = length // blocks
    factor = LOG2E / (HEAD_SIZE**0.5)

    def held(b):
        return pl.ds(pl.multiple_of(lax.rem(index_ref[1] - b + blocks, blocks) * rows, rows), rows)

    kv_half = kv_ref.shape[1] // 2
    for b in range(blocks):
        keys[b * rows : (b + 1) * rows, :] = kv_ref[held(b), :kv_half]
        values[b * rows : (b + 1) * rows, :] = kv_ref[held(b), kv_half:]
    row = lax.broadcasted_iota(jnp.int32, (rows, rows), 0)
    column = lax.broadcasted_iota(jnp.int32, (rows, rows), 1)
    causal = row >= column
    causal = jnp.concatenate([causal.astype(jnp.float32)] * group, axis=0) > 0.5
    for g, b in [(g, b) for g in range(kv_half // HEAD_SIZE) for b in range(blocks)]:
        left = g * group * HEAD_SIZE
        head = slice(g * HEAD_SIZE, (g + 1) * HEAD_SIZE)
        q_block = q_ref[held(b), left : left + group * HEAD_SIZE]
        queries = jnp.concatenate(
            [q_block[:, h * HEAD_SIZE : (h + 1) * HEAD_SIZE] for h in range(group)], axis=0
        )
        at = b * rows
        near = lax.dot_general(
            queries, keys[at : at + rows, head], NT, preferred_element_type=jnp.float32
        )
        near = jnp.where(causal, near, jnp.float32(-1e30))
        largest = jnp.max(near, axis=-1, keepdims=True)
        if b > 0:
            far = lax.dot_general(queries, keys[:at, head], NT, preferred_element_type=jnp.float32)
            largest = jnp.maximum(largest, jnp.max(far, axis=-1, keepdims=True))
        near = jnp.exp2((near - largest) * factor)
        total = jnp.sum(near, axis=-1, keepdims=True)
        result = jnp.dot(
            near.astype(jnp.bfloat16), values[at : at + rows, head], preferred_element_type=jnp.float32
        )
        if b > 0:
            far = jnp.exp2((far - largest) * factor)
            total = total + jnp.sum(far, axis=-1, keepdims=True)
            result = result + jnp.dot(
                far.astype(jnp.bfloat16), values[:at, head], preferred_element_type=jnp.float32
            )
        result = (result / total).astype(jnp.bfloat16)
        for h in range(group):
            out_ref[held(b), left + h * HEAD_SIZE : left + (h + 1) * HEAD_SIZE] = result[
                h * rows : (h + 1) * rows, :
            ]


def attend(index, queries, kv, blocks):
    length, q_cols = queries.shape
    kv_half = kv.shape[1] // 2
    return pl.pallas_call(
        functools.partial(attend_kernel, blocks, q_cols // kv_half),
        in_specs=[SMEM, VMEM, VMEM],
        out_specs=VMEM,
        out_shape=bf16(length, q_cols),
        scratch_shapes=[
            pltpu.VMEM((length, kv_half), jnp.bfloat16),
            pltpu.VMEM((length, kv_half), jnp.bfloat16),
        ],
        compiler_params=params(16),
        cost_estimate=work(4 * length * length * q_cols, queries, queries, kv),
        name="attend",
    )(index, queries, kv)


def mix_kernel(n_w, heads_ref, *refs):
    w_refs, out_refs = refs[:n_w], refs[n_w:]
    rows = out_refs[0].shape[0]
    weights = [w_ref[...] for w_ref in w_refs]
    weights = weights[0] if n_w == 1 else jnp.concatenate(weights, axis=0)
    term = lax.dot_general(
        heads_ref[...], weights, NT, preferred_element_type=jnp.float32
    ).astype(jnp.bfloat16)
    for k, out_ref in enumerate(out_refs):
        out_ref[...] = term[k * rows : (k + 1) * rows, :]


def mix(heads, parts, blocks):
    length, features = heads.shape
    columns = sum(part.shape[0] for part in parts)
    return pl.pallas_call(
        functools.partial(mix_kernel, len(parts)),
        in_specs=[VMEM] * (1 + len(parts)),
        out_specs=[VMEM] * blocks,
        out_shape=[bf16(length // blocks, columns)] * blocks,
        compiler_params=params(16),
        cost_estimate=work(2 * length * columns * features, heads, *parts),
        name="mix",
    )(heads, *parts)


def add_kernel(a_ref, b_ref, out_ref):
    total = a_ref[...].astype(jnp.float32) + b_ref[...].astype(jnp.float32)
    out_ref[...] = total.astype(jnp.bfloat16)


def add(a, b):
    return pl.pallas_call(
        add_kernel,
        in_specs=[VMEM, VMEM],
        out_specs=VMEM,
        out_shape=bf16(*a.shape),
        compiler_params=params(8),
        cost_estimate=work(0, a, a, a),
        name="add",
    )(a, b)


def place_kernel(parts, index_ref, a_ref, b_ref, *refs):
    out_ref, total, sem = refs[-3:]
    add_kernel(a_ref, b_ref, total)
    copies, left = [], 0
    for i, (j, shard, offset, width) in enumerate(parts):
        start = pl.multiple_of(jnp.bitwise_xor(index_ref[0], j) * shard + offset, 128)
        copies.append(
            pltpu.make_async_copy(
                total.at[:, pl.ds(left, width)], out_ref.at[:, pl.ds(start, width)], sem.at[i]
            )
        )
        left += width
    for copy in copies:
        copy.start()
    for copy in copies:
        copy.wait()


def place(mixed, index, a, b, parts, columns):
    if any(offset % 128 or width % 128 or shard % 128 for _, shard, offset, width in parts):
        total, left = add(a, b), 0
        if mixed is None:
            mixed = jnp.zeros((a.shape[0], columns), jnp.bfloat16)
        for j, shard, offset, width in parts:
            start = jnp.bitwise_xor(index[0], j) * shard + offset
            mixed = lax.dynamic_update_slice(mixed, total[:, left : left + width], (0, start))
            left += width
        return mixed
    held = [] if mixed is None else [mixed]
    return pl.pallas_call(
        functools.partial(place_kernel, parts),
        in_specs=[SMEM, VMEM, VMEM] + [ANY] * len(held),
        out_specs=ANY,
        out_shape=bf16(a.shape[0], columns),
        scratch_shapes=[
            pltpu.VMEM(a.shape, jnp.bfloat16),
            pltpu.SemaphoreType.DMA((len(parts),)),
        ],
        input_output_aliases={3: 0} if held else {},
        compiler_params=params(8),
        cost_estimate=work(0, a, a, a),
        name="place",
    )(index, a, b, *held)


def swapped(array, n_f, mask):
    return lax.ppermute(array, "fsdp", [(i, i ^ mask) for i in range(n_f)])


def after(array, *others):
    return lax.optimization_barrier((array, *others))[0] if others else array


def phase_of(piece):
    r, half = piece
    bits = bin(r).count("1")
    if bits <= 1:
        return bits if half == (1 if r == 1 else 0) else 2 * bits
    return bits + 1


def send_phase(held, n_f, phase, *before):
    sent = [(r, h) for r in range(1, n_f // 2) for h in range(2) if phase_of((r, h)) == phase]
    for r, half in sent:
        bit = r & -r if half == 0 else 1 << (r.bit_length() - 1)
        held[r, half] = swapped(after(held[r ^ bit, half], *before), n_f, 2 * bit)
    return [held[piece] for piece in sent]


def send_level(held, n_f, cut, level, *before):
    for r in [r for r in range(1, n_f // 2) if bin(r).count("1") == level]:
        if level == 1:
            held[r] = [swapped(after(held[0][0], *before), n_f, 2 * r)]
            continue
        held[r] = []
        for half, bit in ((0, r & -r), (1, 1 << (r.bit_length() - 1))):
            parts = held[r ^ bit]
            part = parts[half] if len(parts) == 2 else cut_rows(parts[0], cut, half)
            held[r].append(swapped(after(part, *before), n_f, 2 * bit))


def send_o_siblings(held, sibling, n_f, level, *before):
    for r in [r for r in held if bin(r).count("1") == level]:
        sibling[r] = [swapped(after(part, *before), n_f, 1) for part in held[r]]


def send_siblings(held, sibling, n_f, pieces, *before):
    for piece in pieces:
        sibling[piece] = swapped(after(held[piece], *before), n_f, 1)


def of_phase(held, phase):
    return [piece for piece in held if phase_of(piece) == phase]


def rope_tables(length):
    frequency = np.float32(ROPE_BASE) ** (
        -(np.arange(HALF, dtype=np.float32) * np.float32(2.0) / np.float32(HEAD_SIZE))
    )
    angle = np.arange(length, dtype=np.float32)[:, None] * frequency[None, :].astype(np.float32)
    angle = angle.astype(np.float64)
    cos, sin = np.cos(angle).astype(np.float32), np.sin(angle).astype(np.float32)
    return np.concatenate([cos, cos], axis=1), np.concatenate([-sin, sin], axis=1)


def body(
    n_f,
    n_s,
    tokens,
    norm_gain,
    q_weight,
    key_matrix,
    value_matrix,
    q_bias,
    k_bias,
    value_offset_bias,
    out_weight,
):
    index = jnp.stack([lax.axis_index("fsdp"), lax.axis_index("sp")])
    count = tokens.shape[0]
    chips = n_f // 2
    phases = chips.bit_length()
    shard, q_cols = q_weight.shape
    kv_cols = key_matrix.shape[1]
    wide = 256 if q_cols % 256 == 0 and kv_cols % 256 == 0 else 128
    cut = (q_cols + 2 * kv_cols) // wide // 2 * wide
    cut += wide if cut + wide <= q_cols else 0
    ring = [(i, (i + 1) % n_s) for i in range(n_s)]
    cos, sin = rope_tables(n_s * count)

    blocks = [normed_pieces(index, tokens, norm_gain, n_f)]
    first, second = pack(after(q_weight, blocks[0]), key_matrix, value_matrix, cut)
    held, sibling = {(0, 0): first, (0, 1): second}, {}
    send_siblings(held, sibling, n_f, list(held))
    o_cut = shard * 3 // 5 // 128 * 128 or shard // 2 // 16 * 16
    o_held, o_sibling = {0: [after(out_weight, first)]}, {}

    gates, sent = [], []
    for k in range(1, n_s):
        if k <= phases:
            sent = send_phase(held, n_f, k, *gates[-1:], *sent)
            if k > 1:
                send_siblings(held, sibling, n_f, of_phase(held, k - 1), *gates[-1:])
        blocks.append(lax.ppermute(blocks[-1], "sp", ring))
        gates.append(blocks[-1])
    send_o_siblings(o_held, o_sibling, n_f, 0, gates[0])

    def parts(half, chosen):
        return [side[r, half] for r in chosen for side in (held, sibling)]

    most = range(chips - 1)
    early = partial(blocks[:-1], parts(0, most), parts(1, most), wide)
    send_siblings(held, sibling, n_f, of_phase(held, phases), gates[-1], early)
    send_level(o_held, n_f, o_cut, 1, gates[-1], early)
    late = partial(blocks[-1:], parts(0, most), parts(1, most), wide)
    last = parts(0, [chips - 1]) + parts(1, [chips - 1])
    queries, kv = finish(
        index,
        blocks,
        last,
        early,
        late,
        (q_bias, k_bias, value_offset_bias),
        cos,
        sin,
        q_cols,
        2 * shard * (chips - 1),
        wide,
    )
    heads = attend(index, queries, kv, n_s)

    mixed = None
    gate, behind = [], []
    for level in range(phases):
        if level:
            send_o_siblings(o_held, o_sibling, n_f, level, *gate)
            send_level(o_held, n_f, o_cut, level + 1, *gate)
        groups = []
        for r in [r for r in o_held if bin(r).count("1") == level]:
            if len(o_held[r]) == 1:
                groups += [((r, 0, 0),), ((r, 0, 1),)]
            else:
                groups += [((r, half, 0), (r, half, 1)) for half in (0, 1)]
        rings = []
        for group in groups:
            weights = [(o_sibling if core else o_held)[r][half] for r, half, core in group]
            rings.append(mix(after(heads, *gate), weights, n_s))
        totals = [terms[1] for terms in rings]
        arrivals = []
        for k in range(2, n_s + 1):
            arrived = [lax.ppermute(total, "sp", ring) for total in totals]
            arrivals.append(arrived)
            if k < n_s:
                held_back = behind if k == n_s - 1 else []
                totals = [
                    add(after(a, *held_back), terms[k]) for a, terms in zip(arrived, rings)
                ]
        for group, a, terms in zip(groups, arrived, rings):
            where = [
                (2 * r + core, shard, half * o_cut, o_held[r][half].shape[0])
                for r, half, core in group
            ]
            mixed = place(mixed, index, a, terms[0], where, shard * n_f)
        gate = arrivals[-1] if level == 0 else arrivals[0]
        behind = arrivals[-1]
    return mixed


def solution(mesh):
    n_f, n_s = mesh.shape["fsdp"], mesh.shape["sp"]
    placed = (
        P(("fsdp", "sp"), None),
        P(),
        P("fsdp", "sp"),
        P("fsdp", "sp"),
        P("fsdp", "sp"),
        P("sp"),
        P("sp"),
        P("sp"),
        P("fsdp", "sp"),
    )
    return jax.shard_map(
        functools.partial(body, n_f, n_s),
        mesh=mesh,
        in_specs=placed,
        out_specs=P(("fsdp", "sp"), None),
        check_vma=False,
    )
```

```python
import functools

import jax
import jax.numpy as jnp
import numpy as np
from jax import lax
from jax.experimental import pallas as pl
from jax.experimental.pallas import tpu as pltpu
from jax.sharding import PartitionSpec as P

HEAD_SIZE = 128
HALF = HEAD_SIZE // 2
ROPE_BASE = 1000000.0
LOG2E = 1.4426950408889634
NT = (((1,), (1,)), ((), ()))
VMEM = pl.BlockSpec(memory_space=pltpu.VMEM)
SMEM = pl.BlockSpec(memory_space=pltpu.SMEM)
ANY = pl.BlockSpec(memory_space=pl.ANY)


def params(mib):
    return pltpu.CompilerParams(vmem_limit_bytes=mib * 1024 * 1024)


def bf16(*shape):
    return jax.ShapeDtypeStruct(shape, jnp.bfloat16)


def work(flops, *arrays):
    size = sum(int(np.prod(x.shape)) * x.dtype.itemsize for x in arrays)
    return pl.CostEstimate(flops=flops, bytes_accessed=size, transcendentals=0)


def normed_kernel(n_f, index_ref, tokens_ref, gain_ref, out_ref):
    rows = tokens_ref[...].astype(jnp.float32)
    scale = lax.rsqrt(jnp.mean(rows * rows, axis=-1, keepdims=True) + 1e-06)
    shard = tokens_ref.shape[1] // n_f
    for j in range(n_f):
        start = pl.multiple_of(jnp.bitwise_xor(index_ref[0], j) * shard, 128)
        columns = pl.ds(start, shard)
        piece = tokens_ref[:, columns].astype(jnp.float32) * scale * gain_ref[:, columns]
        out_ref[:, j * shard : (j + 1) * shard] = piece.astype(jnp.bfloat16)


def normed_pieces(index, tokens, gain, n_f):
    count, width = tokens.shape
    shard = width // n_f
    if shard % 128 == 0:
        return pl.pallas_call(
            functools.partial(normed_kernel, n_f),
            out_shape=bf16(count, width),
            in_specs=[SMEM, VMEM, VMEM],
            out_specs=VMEM,
            compiler_params=params(16),
            cost_estimate=work(6 * count * width, tokens, tokens),
            name="norm",
        )(index, tokens, gain[None, :])
    rows = tokens.astype(jnp.float32)
    meansq = jnp.mean(rows * rows, axis=-1, keepdims=True)
    normed = (rows * lax.rsqrt(meansq + 1e-06) * gain).astype(jnp.bfloat16)
    pieces = [
        lax.dynamic_slice_in_dim(normed, jnp.bitwise_xor(index[0], j) * shard, shard, axis=1)
        for j in range(n_f)
    ]
    return jnp.concatenate(pieces, axis=1)


def pack_kernel(*refs):
    out_ref, at = refs[-1], 0
    for ref in refs[:-1]:
        out_ref[:, at : at + ref.shape[1]] = ref[...]
        at += ref.shape[1]


def pack(*arrays):
    return pl.pallas_call(
        pack_kernel,
        in_specs=[VMEM] * len(arrays),
        out_specs=VMEM,
        out_shape=bf16(arrays[0].shape[0], sum(x.shape[1] for x in arrays)),
        compiler_params=params(16),
        cost_estimate=work(0, *arrays, *arrays),
        name="pack",
    )(*arrays)


def cut_kernel(rows, columns, ref, out_ref):
    out_ref[...] = ref[rows, columns]


def part_of(array, cut, half, axis):
    bounds = [slice(0, size) for size in array.shape]
    bounds[axis] = slice(cut, array.shape[axis]) if half else slice(0, cut)
    return pl.pallas_call(
        functools.partial(cut_kernel, *bounds),
        in_specs=[VMEM],
        out_specs=VMEM,
        out_shape=bf16(*[bound.stop - bound.start for bound in bounds]),
        compiler_params=params(16),
        cost_estimate=work(0, array),
        name="cut",
    )(array)


def partial_kernel(n_x, counts, wide, *refs):
    x_refs, w_refs, (out_ref, rows) = refs[:n_x], refs[n_x:-2], refs[-2:]
    at = 0
    for x_ref in x_refs:
        rows[at : at + x_ref.shape[0], :] = x_ref[:, : rows.shape[1]]
        at += x_ref.shape[0]
    shard = w_refs[0].shape[0]
    pieces, at = [], 0
    for count in counts:
        pieces.append(w_refs[at : at + count])
        at += count
    for col in range(0, out_ref.shape[1], wide):
        total = None
        for j, parts in enumerate(pieces):
            at = col
            for w_ref in parts:
                if at < w_ref.shape[1]:
                    break
                at -= w_ref.shape[1]
            term = jnp.dot(
                rows[:, j * shard : (j + 1) * shard],
                w_ref[:, at : at + wide],
                preferred_element_type=jnp.float32,
            )
            total = term if total is None else total + term
        out_ref[:, col : col + wide] = total


def partial(blocks, pieces, wide):
    weights = [part for piece in pieces for part in piece]
    length = sum(block.shape[0] for block in blocks)
    depth = len(pieces) * weights[0].shape[0]
    columns = sum(part.shape[1] for part in pieces[0])
    out = jax.ShapeDtypeStruct((length, columns), jnp.float32)
    counts = [len(piece) for piece in pieces]
    return pl.pallas_call(
        functools.partial(partial_kernel, len(blocks), counts, wide),
        in_specs=[VMEM] * (len(blocks) + len(weights)),
        out_specs=VMEM,
        out_shape=out,
        scratch_shapes=[pltpu.VMEM((length, depth), jnp.bfloat16)],
        compiler_params=params(16),
        cost_estimate=work(2 * length * depth * columns, *blocks, *weights, out),
        name="partial",
    )(*blocks, *weights)


def rope_tile(tile, cos, sin):
    parts = []
    for at in range(0, tile.shape[1], HEAD_SIZE):
        head = tile[:, at : at + HEAD_SIZE]
        parts.append(head * cos + pltpu.roll(head, HALF, axis=1) * sin)
    return parts[0] if len(parts) == 1 else jnp.concatenate(parts, axis=1)


def finish_kernel(n_x, offsets, wide, roped, first_col, index_ref, *refs):
    x_refs = refs[:n_x]
    w_refs = refs[n_x : n_x + 4]
    early_ref, late_ref = refs[n_x + 4 : n_x + 6]
    bias_refs, (cos_ref, sin_ref) = refs[n_x + 6 : n_x + 9], refs[n_x + 9 : n_x + 11]
    q_out, kv_out, rows, cos, sin = refs[n_x + 11 :]
    shard = w_refs[0].shape[0]
    at = 0
    for x_ref in x_refs:
        rows[at : at + x_ref.shape[0], :] = x_ref[:, first_col : first_col + 2 * shard]
        at += x_ref.shape[0]
    blocks = len(offsets)
    count = at // blocks
    for k, offset in enumerate(offsets):
        block = lax.rem(index_ref[1] - offset + blocks, blocks)
        place = pl.ds(pl.multiple_of(block * count, count), count)
        cos[k * count : (k + 1) * count, :] = cos_ref[place, :]
        sin[k * count : (k + 1) * count, :] = sin_ref[place, :]
    q_cols = q_out.shape[1]

    def bias_tile(col):
        for bias_ref in bias_refs:
            if col < bias_ref.shape[0]:
                return bias_ref[pl.ds(col, wide)][None, :]
            col -= bias_ref.shape[0]

    base = 0
    for mine, sibling in (w_refs[:2], w_refs[2:]):
        for at in range(0, mine.shape[1], wide):
            total = jnp.dot(
                rows[:, :shard], mine[:, at : at + wide], preferred_element_type=jnp.float32
            )
            total = total + jnp.dot(
                rows[:, shard:], sibling[:, at : at + wide], preferred_element_type=jnp.float32
            )
            col = base + at
            total = total + jnp.concatenate(
                [early_ref[:, col : col + wide], late_ref[:, col : col + wide]], axis=0
            )
            total = total + bias_tile(col)
            if col < roped:
                total = rope_tile(total, cos[...], sin[...])
            total = total.astype(jnp.bfloat16)
            if col < q_cols:
                q_out[:, col : col + wide] = total
            else:
                kv_out[:, col - q_cols : col - q_cols + wide] = total
        base += mine.shape[1]


def finish(index, blocks, offsets, weights, early, late, biases, cos, sin, q_cols, first_col, wide):
    n_x = len(blocks)
    length = sum(block.shape[0] for block in blocks)
    shard = weights[0].shape[0]
    columns = early.shape[1]
    kv_cols = columns - q_cols
    return pl.pallas_call(
        functools.partial(finish_kernel, n_x, offsets, wide, q_cols + kv_cols // 2, first_col),
        in_specs=[SMEM] + [VMEM] * (n_x + 11),
        out_specs=[VMEM, VMEM],
        out_shape=[bf16(length, q_cols), bf16(length, kv_cols)],
        scratch_shapes=[
            pltpu.VMEM((length, 2 * shard), jnp.bfloat16),
            pltpu.VMEM((length, HEAD_SIZE), jnp.float32),
            pltpu.VMEM((length, HEAD_SIZE), jnp.float32),
        ],
        compiler_params=params(16),
        cost_estimate=work(4 * length * shard * columns, *weights, early, late),
        name="finish",
    )(index, *blocks, *weights, early, late, *biases, cos, sin)


def attend_kernel(offsets, group, index_ref, q_ref, kv_ref, out_ref, keys, values):
    blocks = len(offsets)
    rows = q_ref.shape[0] // blocks
    factor = LOG2E / (HEAD_SIZE**0.5)

    def held(b):
        offset = lax.rem(index_ref[1] - b + blocks, blocks)
        k = sum(jnp.where(offset == value, i, 0) for i, value in enumerate(offsets))
        return pl.ds(pl.multiple_of(k * rows, rows), rows)

    kv_half = kv_ref.shape[1] // 2
    for b in range(blocks):
        keys[b * rows : (b + 1) * rows, :] = kv_ref[held(b), :kv_half]
        values[b * rows : (b + 1) * rows, :] = kv_ref[held(b), kv_half:]
    row = lax.broadcasted_iota(jnp.int32, (rows, rows), 0)
    column = lax.broadcasted_iota(jnp.int32, (rows, rows), 1)
    causal = row >= column
    causal = jnp.concatenate([causal.astype(jnp.float32)] * group, axis=0) > 0.5
    for g, b in [(g, b) for g in range(kv_half // HEAD_SIZE) for b in range(blocks)]:
        left = g * group * HEAD_SIZE
        head = slice(g * HEAD_SIZE, (g + 1) * HEAD_SIZE)
        q_block = q_ref[held(b), left : left + group * HEAD_SIZE]
        queries = jnp.concatenate(
            [q_block[:, h * HEAD_SIZE : (h + 1) * HEAD_SIZE] for h in range(group)], axis=0
        )
        at = b * rows
        near = lax.dot_general(
            queries, keys[at : at + rows, head], NT, preferred_element_type=jnp.float32
        )
        near = jnp.where(causal, near, jnp.float32(-1e30))
        largest = jnp.max(near, axis=-1, keepdims=True)
        if b > 0:
            far = lax.dot_general(queries, keys[:at, head], NT, preferred_element_type=jnp.float32)
            largest = jnp.maximum(largest, jnp.max(far, axis=-1, keepdims=True))
        near = jnp.exp2((near - largest) * factor)
        total = jnp.sum(near, axis=-1, keepdims=True)
        result = jnp.dot(
            near.astype(jnp.bfloat16), values[at : at + rows, head], preferred_element_type=jnp.float32
        )
        if b > 0:
            far = jnp.exp2((far - largest) * factor)
            total = total + jnp.sum(far, axis=-1, keepdims=True)
            result = result + jnp.dot(
                far.astype(jnp.bfloat16), values[:at, head], preferred_element_type=jnp.float32
            )
        result = (result / total).astype(jnp.bfloat16)
        for h in range(group):
            out_ref[held(b), left + h * HEAD_SIZE : left + (h + 1) * HEAD_SIZE] = result[
                h * rows : (h + 1) * rows, :
            ]


def attend(index, queries, kv, offsets):
    length, q_cols = queries.shape
    kv_half = kv.shape[1] // 2
    return pl.pallas_call(
        functools.partial(attend_kernel, offsets, q_cols // kv_half),
        in_specs=[SMEM, VMEM, VMEM],
        out_specs=VMEM,
        out_shape=bf16(length, q_cols),
        scratch_shapes=[
            pltpu.VMEM((length, kv_half), jnp.bfloat16),
            pltpu.VMEM((length, kv_half), jnp.bfloat16),
        ],
        compiler_params=params(16),
        cost_estimate=work(4 * length * length * q_cols, queries, queries, kv),
        name="attend",
    )(index, queries, kv)


def mix_kernel(n_w, heads_ref, *refs):
    w_refs, out_refs = refs[:n_w], refs[n_w:]
    rows = out_refs[0].shape[0]
    weights = [w_ref[...] for w_ref in w_refs]
    weights = weights[0] if n_w == 1 else jnp.concatenate(weights, axis=0)
    term = lax.dot_general(
        heads_ref[...], weights, NT, preferred_element_type=jnp.float32
    ).astype(jnp.bfloat16)
    for k, out_ref in enumerate(out_refs):
        out_ref[...] = term[k * rows : (k + 1) * rows, :]


def mix(heads, parts, blocks):
    length, features = heads.shape
    columns = sum(part.shape[0] for part in parts)
    return pl.pallas_call(
        functools.partial(mix_kernel, len(parts)),
        in_specs=[VMEM] * (1 + len(parts)),
        out_specs=[VMEM] * blocks,
        out_shape=[bf16(length // blocks, columns)] * blocks,
        compiler_params=params(16),
        cost_estimate=work(2 * length * columns * features, heads, *parts),
        name="mix",
    )(heads, *parts)


def add_kernel(a_ref, b_ref, out_ref):
    total = a_ref[...].astype(jnp.float32) + b_ref[...].astype(jnp.float32)
    out_ref[...] = total.astype(jnp.bfloat16)


def add(a, b):
    return pl.pallas_call(
        add_kernel,
        in_specs=[VMEM, VMEM],
        out_specs=VMEM,
        out_shape=bf16(*a.shape),
        compiler_params=params(8),
        cost_estimate=work(0, a, a, a),
        name="add",
    )(a, b)


def place_kernel(parts, index_ref, *refs):
    n = len(parts)
    a_refs, b_refs, out_ref, total, sem = refs[:n], refs[n : 2 * n], *refs[-3:]
    copies, left = [], 0
    for a_ref, b_ref, pieces in zip(a_refs, b_refs, parts):
        add_kernel(a_ref, b_ref, total.at[:, pl.ds(left, a_ref.shape[1])])
        for j, shard, offset, width in pieces:
            start = pl.multiple_of(jnp.bitwise_xor(index_ref[0], j) * shard + offset, 128)
            copies.append(
                pltpu.make_async_copy(
                    total.at[:, pl.ds(left, width)],
                    out_ref.at[:, pl.ds(start, width)],
                    sem.at[len(copies)],
                )
            )
            copies[-1].start()
            left += width
    for copy in copies:
        copy.wait()


def place(mixed, index, first, second, parts, columns):
    every = [piece for pieces in parts for piece in pieces]
    count = first[0].shape[0]
    if any(offset % 128 or width % 128 or shard % 128 for _, shard, offset, width in every):
        if mixed is None:
            mixed = jnp.zeros((count, columns), jnp.bfloat16)
        for a, b, pieces in zip(first, second, parts):
            total, left = add(a, b), 0
            for j, shard, offset, width in pieces:
                start = jnp.bitwise_xor(index[0], j) * shard + offset
                mixed = lax.dynamic_update_slice(mixed, total[:, left : left + width], (0, start))
                left += width
        return mixed
    held = [] if mixed is None else [mixed]
    return pl.pallas_call(
        functools.partial(place_kernel, parts),
        in_specs=[SMEM] + [VMEM] * (2 * len(parts)) + [ANY] * len(held),
        out_specs=ANY,
        out_shape=bf16(count, columns),
        scratch_shapes=[
            pltpu.VMEM((count, sum(piece[3] for piece in every)), jnp.bfloat16),
            pltpu.SemaphoreType.DMA((len(every),)),
        ],
        input_output_aliases={1 + 2 * len(parts): 0} if held else {},
        compiler_params=params(8),
        cost_estimate=work(0, *first, *second),
        name="place",
    )(index, *first, *second, *held)


def swapped(array, n_f, mask):
    return lax.ppermute(array, "fsdp", [(i, i ^ mask) for i in range(n_f)])


def after(array, *others):
    return lax.optimization_barrier((array, *others))[0] if others else array


def chips_away(level, chips):
    return [r for r in range(chips) if bin(r).count("1") == level]


def send_level(held, n_f, cut, axis, level, *before):
    for r in chips_away(level, n_f // 2):
        if level == 1:
            held[r] = [swapped(after(held[0][0], *before), n_f, 2 * r)]
            continue
        held[r] = []
        for half, bit in ((0, r & -r), (1, 1 << (r.bit_length() - 1))):
            parts = held[r ^ bit]
            part = parts[half] if len(parts) == 2 else part_of(parts[0], cut, half, axis)
            held[r].append(swapped(after(part, *before), n_f, 2 * bit))


def send_siblings(held, sibling, n_f, level, *before):
    for r in chips_away(level, n_f // 2):
        others = held[r] if len(held[r]) > 1 else []
        sibling[r] = [swapped(after(part, *others, *before), n_f, 1) for part in held[r]]


def rope_tables(length):
    frequency = np.float32(ROPE_BASE) ** (
        -(np.arange(HALF, dtype=np.float32) * np.float32(2.0) / np.float32(HEAD_SIZE))
    )
    angle = np.arange(length, dtype=np.float32)[:, None] * frequency[None, :].astype(np.float32)
    angle = angle.astype(np.float64)
    cos, sin = np.cos(angle).astype(np.float32), np.sin(angle).astype(np.float32)
    return np.concatenate([cos, cos], axis=1), np.concatenate([-sin, sin], axis=1)


def body(
    n_f,
    n_s,
    tokens,
    norm_gain,
    q_weight,
    key_matrix,
    value_matrix,
    q_bias,
    k_bias,
    value_offset_bias,
    out_weight,
):
    index = jnp.stack([lax.axis_index("fsdp"), lax.axis_index("sp")])
    count = tokens.shape[0]
    chips = n_f // 2
    levels = chips.bit_length() - 1
    shard, q_cols = q_weight.shape
    kv_cols = key_matrix.shape[1]
    wide = 256 if q_cols % 256 == 0 and kv_cols % 256 == 0 else 128
    cut = (q_cols + 2 * kv_cols) // wide // 2 * wide
    cut += wide if cut + wide <= q_cols else 0
    o_cut = shard * 3 // 5 // 128 * 128 or shard // 2 // 16 * 16
    right = [(i, (i + 1) % n_s) for i in range(n_s)]
    left = [(i, (i - 1) % n_s) for i in range(n_s)]
    cos, sin = rope_tables(n_s * count)

    own = normed_pieces(index, tokens, norm_gain, n_f)
    held = {0: [pack(after(q_weight, own), key_matrix, value_matrix)]}
    sibling, o_held, o_sibling = {}, {0: [after(out_weight, held[0][0])]}, {}
    send_level(held, n_f, cut, 1, 1)
    send_siblings(held, sibling, n_f, 0)

    steps = n_s // 2
    offsets, blocks, gate = [0], [own], []
    ahead = behind = own
    for step in range(1, steps + 1):
        if step > 1 and step <= levels:
            send_level(held, n_f, cut, 1, step, *gate)
            send_siblings(held, sibling, n_f, step - 1, *gate)
        if step < steps:
            ahead = lax.ppermute(ahead, "sp", right)
            behind = lax.ppermute(behind, "sp", left)
            offsets += [step, n_s - step]
        else:
            ahead = lax.ppermute(part_of(ahead, count // 2, 0, 0), "sp", right)
            behind = lax.ppermute(part_of(behind, count // 2, 1, 0), "sp", left)
            offsets += [step]
        blocks += [ahead, behind]
        gate = [ahead, behind]
        if step == 1:
            send_siblings(o_held, o_sibling, n_f, 0, *gate)

    def pieces_of(chosen):
        return [side[r] for r in chosen for side in (held, sibling)]

    most = pieces_of(range(chips - 1))
    early = partial(blocks[:-2], most, wide)
    send_siblings(held, sibling, n_f, levels, *gate, early)
    send_level(o_held, n_f, o_cut, 0, 1, early)
    late = partial(blocks[-2:], most, wide)
    mine, others = pieces_of([chips - 1])
    queries, kv = finish(
        index,
        blocks,
        offsets,
        [mine[0], others[0], mine[1], others[1]],
        early,
        late,
        (q_bias, k_bias, value_offset_bias),
        cos,
        sin,
        q_cols,
        2 * shard * (chips - 1),
        wide,
    )
    heads = attend(index, queries, kv, offsets)

    rounds = []
    for level in range(levels + 1):
        gate = []
        if level == 1:
            gate = arrivals[min(1, n_s - 2)][:1]
        elif level > 1:
            gate = arrivals[0] + (rounds[-2][1][1] if n_s > 2 else [])
        if level:
            before = arrivals[0] if level > 1 else gate
            send_siblings(o_held, o_sibling, n_f, level, *before)
            send_level(o_held, n_f, o_cut, 0, level + 1, *before)
        groups = []
        for r in chips_away(level, chips):
            halves = range(len(o_held[r]))
            if len(halves) == 1:
                groups += [((r, 0, 0),), ((r, 0, 1),)]
            else:
                groups += [((r, half, 0), (r, half, 1)) for half in halves]
        groups.sort(key=lambda group: group[0][2])
        terms = []
        for group in groups:
            weights = [(o_sibling if core else o_held)[r][half] for r, half, core in group]
            mixed = mix(after(heads, *gate), weights, n_s)
            terms.append([mixed[offsets.index(d)] for d in range(n_s)])
        totals, arrivals = [term[1] for term in terms], []
        for d in range(2, n_s + 1):
            arrivals.append([lax.ppermute(total, "sp", right) for total in totals])
            others = []
            if level > 1 and d == n_s - 2:
                others = rounds[-2][1][-1]
            if level > 1 and d == n_s - 1:
                others = rounds[-1][1][-1][:2]
            if d < n_s:
                totals = [add(after(a, *others), term[d]) for a, term in zip(arrivals[-1], terms)]
        where = [
            [(2 * r + core, shard, half * o_cut, o_held[r][half].shape[0]) for r, half, core in group]
            for group in groups
        ]
        rounds.append(([term[0] for term in terms], arrivals, where))

    mixed = None
    for chosen in (rounds[:-1], rounds[-1:]):
        mixed = place(
            mixed,
            index,
            [a for _, arrivals, _ in chosen for a in arrivals[-1]],
            [own for owns, _, _ in chosen for own in owns],
            [parts for _, _, where in chosen for parts in where],
            shard * n_f,
        )
    return mixed


def solution(mesh):
    n_f, n_s = mesh.shape["fsdp"], mesh.shape["sp"]
    placed = (
        P(("fsdp", "sp"), None),
        P(),
        P("fsdp", "sp"),
        P("fsdp", "sp"),
        P("fsdp", "sp"),
        P("sp"),
        P("sp"),
        P("sp"),
        P("fsdp", "sp"),
    )
    return jax.shard_map(
        functools.partial(body, n_f, n_s),
        mesh=mesh,
        in_specs=placed,
        out_specs=P(("fsdp", "sp"), None),
        check_vma=False,
    )
```

```python
import functools

import jax
import jax.numpy as jnp
import numpy as np
from jax import lax
from jax.experimental import pallas as pl
from jax.experimental.pallas import tpu as pltpu
from jax.sharding import PartitionSpec as P

HEAD_SIZE = 128
HALF = HEAD_SIZE // 2
ROPE_BASE = 1000000.0
LOG2E = 1.4426950408889634
NT = (((1,), (1,)), ((), ()))
VMEM = pl.BlockSpec(memory_space=pltpu.VMEM)
SMEM = pl.BlockSpec(memory_space=pltpu.SMEM)
ANY = pl.BlockSpec(memory_space=pl.ANY)


def params(mib):
    return pltpu.CompilerParams(vmem_limit_bytes=mib * 1024 * 1024)


def bf16(*shape):
    return jax.ShapeDtypeStruct(shape, jnp.bfloat16)


def work(flops, *arrays):
    size = sum(int(np.prod(x.shape)) * x.dtype.itemsize for x in arrays)
    return pl.CostEstimate(flops=flops, bytes_accessed=size, transcendentals=0)


def link_time(array, share=2):
    size = share * int(np.prod(array.shape)) * array.dtype.itemsize
    return pl.CostEstimate(flops=size * 11000, bytes_accessed=size, transcendentals=0)


def normed_kernel(n_f, index_ref, tokens_ref, gain_ref, out_ref):
    rows = tokens_ref[...].astype(jnp.float32)
    scale = lax.rsqrt(jnp.mean(rows * rows, axis=-1, keepdims=True) + 1e-06)
    shard = tokens_ref.shape[1] // n_f
    for j in range(n_f):
        start = pl.multiple_of(jnp.bitwise_xor(index_ref[0], j) * shard, 128)
        columns = pl.ds(start, shard)
        piece = tokens_ref[:, columns].astype(jnp.float32) * scale * gain_ref[:, columns]
        out_ref[:, j * shard : (j + 1) * shard] = piece.astype(jnp.bfloat16)


def normed_pieces(index, tokens, gain, n_f):
    count, width = tokens.shape
    shard = width // n_f
    if shard % 128 == 0:
        return pl.pallas_call(
            functools.partial(normed_kernel, n_f),
            out_shape=bf16(count, width),
            in_specs=[SMEM, VMEM, VMEM],
            out_specs=VMEM,
            compiler_params=params(16),
            cost_estimate=work(6 * count * width, tokens, tokens),
            name="norm",
        )(index, tokens, gain[None, :])
    rows = tokens.astype(jnp.float32)
    meansq = jnp.mean(rows * rows, axis=-1, keepdims=True)
    normed = (rows * lax.rsqrt(meansq + 1e-06) * gain).astype(jnp.bfloat16)
    pieces = [
        lax.dynamic_slice_in_dim(normed, jnp.bitwise_xor(index[0], j) * shard, shard, axis=1)
        for j in range(n_f)
    ]
    return jnp.concatenate(pieces, axis=1)


def pack_kernel(*refs):
    out_ref, at = refs[-1], 0
    for ref in refs[:-1]:
        out_ref[:, at : at + ref.shape[1]] = ref[...]
        at += ref.shape[1]


def pack(*arrays):
    return pl.pallas_call(
        pack_kernel,
        in_specs=[VMEM] * len(arrays),
        out_specs=VMEM,
        out_shape=bf16(arrays[0].shape[0], sum(x.shape[1] for x in arrays)),
        compiler_params=params(16),
        cost_estimate=work(0, *arrays, *arrays),
        name="pack",
    )(*arrays)


def cut_kernel(rows, columns, ref, out_ref):
    out_ref[...] = ref[rows, columns]


def part_of(array, cut, half, axis):
    bounds = [slice(0, size) for size in array.shape]
    bounds[axis] = slice(cut, array.shape[axis]) if half else slice(0, cut)
    return pl.pallas_call(
        functools.partial(cut_kernel, *bounds),
        in_specs=[VMEM],
        out_specs=VMEM,
        out_shape=bf16(*[bound.stop - bound.start for bound in bounds]),
        compiler_params=params(16),
        cost_estimate=work(0, array),
        name="cut",
    )(array)


def partial_kernel(n_x, counts, wide, *refs):
    x_refs, w_refs, (out_ref, rows) = refs[:n_x], refs[n_x:-2], refs[-2:]
    at = 0
    for x_ref in x_refs:
        rows[at : at + x_ref.shape[0], :] = x_ref[:, : rows.shape[1]]
        at += x_ref.shape[0]
    shard = w_refs[0].shape[0]
    pieces, at = [], 0
    for count in counts:
        pieces.append(w_refs[at : at + count])
        at += count
    for col in range(0, out_ref.shape[1], wide):
        total = None
        for j, parts in enumerate(pieces):
            at = col
            for w_ref in parts:
                if at < w_ref.shape[1]:
                    break
                at -= w_ref.shape[1]
            term = jnp.dot(
                rows[:, j * shard : (j + 1) * shard],
                w_ref[:, at : at + wide],
                preferred_element_type=jnp.float32,
            )
            total = term if total is None else total + term
        out_ref[:, col : col + wide] = total


def partial(blocks, pieces, wide):
    weights = [part for piece in pieces for part in piece]
    length = sum(block.shape[0] for block in blocks)
    depth = len(pieces) * weights[0].shape[0]
    columns = sum(part.shape[1] for part in pieces[0])
    out = jax.ShapeDtypeStruct((length, columns), jnp.float32)
    counts = [len(piece) for piece in pieces]
    return pl.pallas_call(
        functools.partial(partial_kernel, len(blocks), counts, wide),
        in_specs=[VMEM] * (len(blocks) + len(weights)),
        out_specs=VMEM,
        out_shape=out,
        scratch_shapes=[pltpu.VMEM((length, depth), jnp.bfloat16)],
        compiler_params=params(16),
        cost_estimate=work(2 * length * depth * columns, *blocks, *weights, out),
        name="partial",
    )(*blocks, *weights)


def rope_tile(tile, cos, sin):
    parts = []
    for at in range(0, tile.shape[1], HEAD_SIZE):
        head = tile[:, at : at + HEAD_SIZE]
        parts.append(head * cos + pltpu.roll(head, HALF, axis=1) * sin)
    return parts[0] if len(parts) == 1 else jnp.concatenate(parts, axis=1)


def finish_kernel(n_x, offsets, wide, roped, first_col, index_ref, *refs):
    x_refs = refs[:n_x]
    w_refs = refs[n_x : n_x + 4]
    early_ref, late_ref = refs[n_x + 4 : n_x + 6]
    bias_refs, (cos_ref, sin_ref) = refs[n_x + 6 : n_x + 9], refs[n_x + 9 : n_x + 11]
    q_out, kv_out, rows, cos, sin = refs[n_x + 11 :]
    shard = w_refs[0].shape[0]
    at = 0
    for x_ref in x_refs:
        rows[at : at + x_ref.shape[0], :] = x_ref[:, first_col : first_col + 2 * shard]
        at += x_ref.shape[0]
    blocks = len(offsets)
    count = at // blocks
    for k, offset in enumerate(offsets):
        block = lax.rem(index_ref[1] - offset + blocks, blocks)
        place = pl.ds(pl.multiple_of(block * count, count), count)
        cos[k * count : (k + 1) * count, :] = cos_ref[place, :]
        sin[k * count : (k + 1) * count, :] = sin_ref[place, :]
    q_cols = q_out.shape[1]

    def bias_tile(col):
        for bias_ref in bias_refs:
            if col < bias_ref.shape[0]:
                return bias_ref[pl.ds(col, wide)][None, :]
            col -= bias_ref.shape[0]

    base = 0
    for mine, sibling in (w_refs[:2], w_refs[2:]):
        for at in range(0, mine.shape[1], wide):
            total = jnp.dot(
                rows[:, :shard], mine[:, at : at + wide], preferred_element_type=jnp.float32
            )
            total = total + jnp.dot(
                rows[:, shard:], sibling[:, at : at + wide], preferred_element_type=jnp.float32
            )
            col = base + at
            total = total + jnp.concatenate(
                [early_ref[:, col : col + wide], late_ref[:, col : col + wide]], axis=0
            )
            total = total + bias_tile(col)
            if col < roped:
                total = rope_tile(total, cos[...], sin[...])
            total = total.astype(jnp.bfloat16)
            if col < q_cols:
                q_out[:, col : col + wide] = total
            else:
                kv_out[:, col - q_cols : col - q_cols + wide] = total
        base += mine.shape[1]


def finish(index, blocks, offsets, weights, early, late, biases, cos, sin, q_cols, first_col, wide):
    n_x = len(blocks)
    length = sum(block.shape[0] for block in blocks)
    shard = weights[0].shape[0]
    columns = early.shape[1]
    kv_cols = columns - q_cols
    return pl.pallas_call(
        functools.partial(finish_kernel, n_x, offsets, wide, q_cols + kv_cols // 2, first_col),
        in_specs=[SMEM] + [VMEM] * (n_x + 11),
        out_specs=[VMEM, VMEM],
        out_shape=[bf16(length, q_cols), bf16(length, kv_cols)],
        scratch_shapes=[
            pltpu.VMEM((length, 2 * shard), jnp.bfloat16),
            pltpu.VMEM((length, HEAD_SIZE), jnp.float32),
            pltpu.VMEM((length, HEAD_SIZE), jnp.float32),
        ],
        compiler_params=params(16),
        cost_estimate=work(4 * length * shard * columns, *weights, early, late),
        name="finish",
    )(index, *blocks, *weights, early, late, *biases, cos, sin)


def attend_kernel(offsets, group, index_ref, q_ref, kv_ref, out_ref, keys, values):
    blocks = len(offsets)
    rows = q_ref.shape[0] // blocks
    factor = LOG2E / (HEAD_SIZE**0.5)

    def held(b):
        offset = lax.rem(index_ref[1] - b + blocks, blocks)
        k = sum(jnp.where(offset == value, i, 0) for i, value in enumerate(offsets))
        return pl.ds(pl.multiple_of(k * rows, rows), rows)

    kv_half = kv_ref.shape[1] // 2
    for b in range(blocks):
        keys[b * rows : (b + 1) * rows, :] = kv_ref[held(b), :kv_half]
        values[b * rows : (b + 1) * rows, :] = kv_ref[held(b), kv_half:]
    row = lax.broadcasted_iota(jnp.int32, (rows, rows), 0)
    column = lax.broadcasted_iota(jnp.int32, (rows, rows), 1)
    causal = row >= column
    causal = jnp.concatenate([causal.astype(jnp.float32)] * group, axis=0) > 0.5
    for g, b in [(g, b) for g in range(kv_half // HEAD_SIZE) for b in range(blocks)]:
        left = g * group * HEAD_SIZE
        head = slice(g * HEAD_SIZE, (g + 1) * HEAD_SIZE)
        q_block = q_ref[held(b), left : left + group * HEAD_SIZE]
        queries = jnp.concatenate(
            [q_block[:, h * HEAD_SIZE : (h + 1) * HEAD_SIZE] for h in range(group)], axis=0
        )
        at = b * rows
        near = lax.dot_general(
            queries, keys[at : at + rows, head], NT, preferred_element_type=jnp.float32
        )
        near = jnp.where(causal, near, jnp.float32(-1e30))
        largest = jnp.max(near, axis=-1, keepdims=True)
        if b > 0:
            far = lax.dot_general(queries, keys[:at, head], NT, preferred_element_type=jnp.float32)
            largest = jnp.maximum(largest, jnp.max(far, axis=-1, keepdims=True))
        near = jnp.exp2((near - largest) * factor)
        total = jnp.sum(near, axis=-1, keepdims=True)
        result = jnp.dot(
            near.astype(jnp.bfloat16), values[at : at + rows, head], preferred_element_type=jnp.float32
        )
        if b > 0:
            far = jnp.exp2((far - largest) * factor)
            total = total + jnp.sum(far, axis=-1, keepdims=True)
            result = result + jnp.dot(
                far.astype(jnp.bfloat16), values[:at, head], preferred_element_type=jnp.float32
            )
        result = (result / total).astype(jnp.bfloat16)
        for h in range(group):
            out_ref[held(b), left + h * HEAD_SIZE : left + (h + 1) * HEAD_SIZE] = result[
                h * rows : (h + 1) * rows, :
            ]


def attend(index, queries, kv, offsets):
    length, q_cols = queries.shape
    kv_half = kv.shape[1] // 2
    return pl.pallas_call(
        functools.partial(attend_kernel, offsets, q_cols // kv_half),
        in_specs=[SMEM, VMEM, VMEM],
        out_specs=VMEM,
        out_shape=bf16(length, q_cols),
        scratch_shapes=[
            pltpu.VMEM((length, kv_half), jnp.bfloat16),
            pltpu.VMEM((length, kv_half), jnp.bfloat16),
        ],
        compiler_params=params(16),
        cost_estimate=work(4 * length * length * q_cols, queries, queries, kv),
        name="attend",
    )(index, queries, kv)


def mix_kernel(n_w, heads_ref, *refs):
    w_refs, out_refs = refs[:n_w], refs[n_w:]
    rows = out_refs[0].shape[0]
    weights = [w_ref[...] for w_ref in w_refs]
    weights = weights[0] if n_w == 1 else jnp.concatenate(weights, axis=0)
    term = lax.dot_general(
        heads_ref[...], weights, NT, preferred_element_type=jnp.float32
    ).astype(jnp.bfloat16)
    for k, out_ref in enumerate(out_refs):
        out_ref[...] = term[k * rows : (k + 1) * rows, :]


def mix(heads, parts, blocks):
    length, features = heads.shape
    columns = sum(part.shape[0] for part in parts)
    return pl.pallas_call(
        functools.partial(mix_kernel, len(parts)),
        in_specs=[VMEM] * (1 + len(parts)),
        out_specs=[VMEM] * blocks,
        out_shape=[bf16(length // blocks, columns)] * blocks,
        compiler_params=params(16),
        cost_estimate=work(2 * length * columns * features, heads, *parts),
        name="mix",
    )(heads, *parts)


def add_kernel(a_ref, b_ref, out_ref):
    total = a_ref[...].astype(jnp.float32) + b_ref[...].astype(jnp.float32)
    out_ref[...] = total.astype(jnp.bfloat16)


def add(a, b):
    return pl.pallas_call(
        add_kernel,
        in_specs=[VMEM, VMEM],
        out_specs=VMEM,
        out_shape=bf16(*a.shape),
        compiler_params=params(8),
        cost_estimate=link_time(a),
        name="add",
    )(a, b)


def place_kernel(parts, index_ref, *refs):
    n = len(parts)
    a_refs, b_refs, out_ref, total, sem = refs[:n], refs[n : 2 * n], *refs[-3:]
    copies, left = [], 0
    for a_ref, b_ref, pieces in zip(a_refs, b_refs, parts):
        add_kernel(a_ref, b_ref, total.at[:, pl.ds(left, a_ref.shape[1])])
        for j, shard, offset, width in pieces:
            start = pl.multiple_of(jnp.bitwise_xor(index_ref[0], j) * shard + offset, 128)
            copies.append(
                pltpu.make_async_copy(
                    total.at[:, pl.ds(left, width)],
                    out_ref.at[:, pl.ds(start, width)],
                    sem.at[len(copies)],
                )
            )
            copies[-1].start()
            left += width
    for copy in copies:
        copy.wait()


def place(mixed, index, first, second, parts, columns):
    every = [piece for pieces in parts for piece in pieces]
    count = first[0].shape[0]
    if any(offset % 128 or width % 128 or shard % 128 for _, shard, offset, width in every):
        if mixed is None:
            mixed = jnp.zeros((count, columns), jnp.bfloat16)
        for a, b, pieces in zip(first, second, parts):
            total, left = add(a, b), 0
            for j, shard, offset, width in pieces:
                start = jnp.bitwise_xor(index[0], j) * shard + offset
                mixed = lax.dynamic_update_slice(mixed, total[:, left : left + width], (0, start))
                left += width
        return mixed
    held = [] if mixed is None else [mixed]
    return pl.pallas_call(
        functools.partial(place_kernel, parts),
        in_specs=[SMEM] + [VMEM] * (2 * len(parts)) + [ANY] * len(held),
        out_specs=ANY,
        out_shape=bf16(count, columns),
        scratch_shapes=[
            pltpu.VMEM((count, sum(piece[3] for piece in every)), jnp.bfloat16),
            pltpu.SemaphoreType.DMA((len(every),)),
        ],
        input_output_aliases={1 + 2 * len(parts): 0} if held else {},
        compiler_params=params(8),
        cost_estimate=work(0, *first, *second),
        name="place",
    )(index, *first, *second, *held)


def swapped(array, n_f, mask):
    return lax.ppermute(array, "fsdp", [(i, i ^ mask) for i in range(n_f)])


def after(array, *others):
    return lax.optimization_barrier((array, *others))[0] if others else array


def chips_away(level, chips):
    return [r for r in range(chips) if bin(r).count("1") == level]


def send_level(held, n_f, cut, axis, level, *before):
    for r in chips_away(level, n_f // 2):
        if level == 1:
            held[r] = [swapped(after(held[0][0], *before), n_f, 2 * r)]
            continue
        held[r] = []
        for half, bit in ((0, r & -r), (1, 1 << (r.bit_length() - 1))):
            parts = held[r ^ bit]
            part = parts[half] if len(parts) == 2 else part_of(parts[0], cut, half, axis)
            held[r].append(swapped(after(part, *before), n_f, 2 * bit))


def send_siblings(held, sibling, n_f, level, *before):
    for r in chips_away(level, n_f // 2):
        others = held[r] if len(held[r]) > 1 else []
        sibling[r] = [swapped(after(part, *others, *before), n_f, 1) for part in held[r]]


def rope_tables(length):
    frequency = np.float32(ROPE_BASE) ** (
        -(np.arange(HALF, dtype=np.float32) * np.float32(2.0) / np.float32(HEAD_SIZE))
    )
    angle = np.arange(length, dtype=np.float32)[:, None] * frequency[None, :].astype(np.float32)
    angle = angle.astype(np.float64)
    cos, sin = np.cos(angle).astype(np.float32), np.sin(angle).astype(np.float32)
    return np.concatenate([cos, cos], axis=1), np.concatenate([-sin, sin], axis=1)


def body(
    n_f,
    n_s,
    tokens,
    norm_gain,
    q_weight,
    key_matrix,
    value_matrix,
    q_bias,
    k_bias,
    value_offset_bias,
    out_weight,
):
    index = jnp.stack([lax.axis_index("fsdp"), lax.axis_index("sp")])
    count = tokens.shape[0]
    chips = n_f // 2
    levels = chips.bit_length() - 1
    shard, q_cols = q_weight.shape
    kv_cols = key_matrix.shape[1]
    wide = 256 if q_cols % 256 == 0 and kv_cols % 256 == 0 else 128
    cut = (q_cols + 2 * kv_cols) // wide // 2 * wide
    cut += wide if cut + wide <= q_cols else 0
    o_cut = shard * 3 // 5 // 128 * 128 or shard // 2 // 16 * 16
    right = [(i, (i + 1) % n_s) for i in range(n_s)]
    left = [(i, (i - 1) % n_s) for i in range(n_s)]
    cos, sin = rope_tables(n_s * count)

    own = normed_pieces(index, tokens, norm_gain, n_f)
    held = {0: [pack(after(q_weight, own), key_matrix, value_matrix)]}
    sibling, o_held, o_sibling = {}, {0: [after(out_weight, held[0][0])]}, {}
    send_level(held, n_f, cut, 1, 1)
    send_siblings(held, sibling, n_f, 0)

    steps = n_s // 2
    offsets, blocks, gate = [0], [own], []
    ahead = behind = own
    for step in range(1, steps + 1):
        if step > 1 and step <= levels:
            send_level(held, n_f, cut, 1, step, *gate)
            send_siblings(held, sibling, n_f, step - 1, *gate)
        if step < steps:
            ahead = lax.ppermute(ahead, "sp", right)
            behind = lax.ppermute(behind, "sp", left)
            offsets += [step, n_s - step]
        else:
            ahead = lax.ppermute(part_of(ahead, count // 2, 0, 0), "sp", right)
            behind = lax.ppermute(part_of(behind, count // 2, 1, 0), "sp", left)
            offsets += [step]
        blocks += [ahead, behind]
        gate = [ahead, behind]
        if step == 1:
            send_siblings(o_held, o_sibling, n_f, 0, *gate)

    def pieces_of(chosen):
        return [side[r] for r in chosen for side in (held, sibling)]

    most = pieces_of(range(chips - 1))
    early = partial(blocks[:-2], most, wide)
    send_siblings(held, sibling, n_f, levels, *gate, early)
    send_level(o_held, n_f, o_cut, 0, 1, early)
    late = partial(blocks[-2:], most, wide)
    mine, others = pieces_of([chips - 1])
    queries, kv = finish(
        index,
        blocks,
        offsets,
        [mine[0], others[0], mine[1], others[1]],
        early,
        late,
        (q_bias, k_bias, value_offset_bias),
        cos,
        sin,
        q_cols,
        2 * shard * (chips - 1),
        wide,
    )
    heads = attend(index, queries, kv, offsets)

    rounds = []
    for level in range(levels + 1):
        if level:
            send_siblings(o_held, o_sibling, n_f, level, *sent)
            send_level(o_held, n_f, o_cut, 0, level + 1, *sent)
        groups = []
        for r in chips_away(level, chips):
            halves = range(len(o_held[r]))
            if len(halves) == 1:
                groups += [((r, 0, 0),), ((r, 0, 1),)]
            else:
                groups += [((r, half, 0), (r, half, 1)) for half in halves]
        groups.sort(key=lambda group: group[0][2])
        terms = []
        for group in groups:
            weights = [(o_sibling if core else o_held)[r][half] for r, half, core in group]
            mixed = mix(heads, weights, n_s)
            terms.append([mixed[offsets.index(d)] for d in range(n_s)])
        totals, arrivals = [term[1] for term in terms], []
        for d in range(2, n_s + 1):
            arrivals.append([lax.ppermute(total, "sp", right) for total in totals])
            if d < n_s:
                totals = [add(a, term[d]) for a, term in zip(arrivals[-1], terms)]
        where = [
            [(2 * r + core, shard, half * o_cut, o_held[r][half].shape[0]) for r, half, core in group]
            for group in groups
        ]
        rounds.append(([term[0] for term in terms], arrivals, where))
        sent = arrivals[0][:1]

    mixed = None
    for chosen in (rounds[:-1], rounds[-1:]):
        mixed = place(
            mixed,
            index,
            [a for _, arrivals, _ in chosen for a in arrivals[-1]],
            [own for owns, _, _ in chosen for own in owns],
            [parts for _, _, where in chosen for parts in where],
            shard * n_f,
        )
    return mixed


def solution(mesh):
    n_f, n_s = mesh.shape["fsdp"], mesh.shape["sp"]
    placed = (
        P(("fsdp", "sp"), None),
        P(),
        P("fsdp", "sp"),
        P("fsdp", "sp"),
        P("fsdp", "sp"),
        P("sp"),
        P("sp"),
        P("sp"),
        P("fsdp", "sp"),
    )
    return jax.shard_map(
        functools.partial(body, n_f, n_s),
        mesh=mesh,
        in_specs=placed,
        out_specs=P(("fsdp", "sp"), None),
        check_vma=False,
    )
```

```python
import functools

import jax
import jax.numpy as jnp
import numpy as np
from jax import lax
from jax.experimental import pallas as pl
from jax.experimental.pallas import tpu as pltpu
from jax.sharding import PartitionSpec as P

HEAD_SIZE = 128
HALF = HEAD_SIZE // 2
ROPE_BASE = 1000000.0
LOG2E = 1.4426950408889634
NT = (((1,), (1,)), ((), ()))
VMEM = pl.BlockSpec(memory_space=pltpu.VMEM)
SMEM = pl.BlockSpec(memory_space=pltpu.SMEM)
ANY = pl.BlockSpec(memory_space=pl.ANY)


def params(mib):
    return pltpu.CompilerParams(vmem_limit_bytes=mib * 1024 * 1024)


def bf16(*shape):
    return jax.ShapeDtypeStruct(shape, jnp.bfloat16)


def work(flops, *arrays):
    size = sum(int(np.prod(x.shape)) * x.dtype.itemsize for x in arrays)
    return pl.CostEstimate(flops=flops, bytes_accessed=size, transcendentals=0)


def link_time(array, share=2):
    size = share * int(np.prod(array.shape)) * array.dtype.itemsize
    return pl.CostEstimate(flops=size * 2000, bytes_accessed=size, transcendentals=0)


def normed_kernel(n_f, index_ref, tokens_ref, gain_ref, out_ref):
    rows = tokens_ref[...].astype(jnp.float32)
    scale = lax.rsqrt(jnp.mean(rows * rows, axis=-1, keepdims=True) + 1e-06)
    shard = tokens_ref.shape[1] // n_f
    for j in range(n_f):
        start = pl.multiple_of(jnp.bitwise_xor(index_ref[0], j) * shard, 128)
        columns = pl.ds(start, shard)
        piece = tokens_ref[:, columns].astype(jnp.float32) * scale * gain_ref[:, columns]
        out_ref[:, j * shard : (j + 1) * shard] = piece.astype(jnp.bfloat16)


def normed_pieces(index, tokens, gain, n_f):
    count, width = tokens.shape
    shard = width // n_f
    if shard % 128 == 0:
        return pl.pallas_call(
            functools.partial(normed_kernel, n_f),
            out_shape=bf16(count, width),
            in_specs=[SMEM, VMEM, VMEM],
            out_specs=VMEM,
            compiler_params=params(16),
            cost_estimate=work(6 * count * width, tokens, tokens),
            name="norm",
        )(index, tokens, gain[None, :])
    rows = tokens.astype(jnp.float32)
    meansq = jnp.mean(rows * rows, axis=-1, keepdims=True)
    normed = (rows * lax.rsqrt(meansq + 1e-06) * gain).astype(jnp.bfloat16)
    pieces = [
        lax.dynamic_slice_in_dim(normed, jnp.bitwise_xor(index[0], j) * shard, shard, axis=1)
        for j in range(n_f)
    ]
    return jnp.concatenate(pieces, axis=1)


def pack_kernel(*refs):
    out_ref, at = refs[-1], 0
    for ref in refs[:-1]:
        out_ref[:, at : at + ref.shape[1]] = ref[...]
        at += ref.shape[1]


def pack(*arrays):
    return pl.pallas_call(
        pack_kernel,
        in_specs=[VMEM] * len(arrays),
        out_specs=VMEM,
        out_shape=bf16(arrays[0].shape[0], sum(x.shape[1] for x in arrays)),
        compiler_params=params(16),
        cost_estimate=work(0, *arrays, *arrays),
        name="pack",
    )(*arrays)


def cut_kernel(rows, columns, ref, out_ref):
    out_ref[...] = ref[rows, columns]


def part_of(array, cut, half, axis):
    bounds = [slice(0, size) for size in array.shape]
    bounds[axis] = slice(cut, array.shape[axis]) if half else slice(0, cut)
    return pl.pallas_call(
        functools.partial(cut_kernel, *bounds),
        in_specs=[VMEM],
        out_specs=VMEM,
        out_shape=bf16(*[bound.stop - bound.start for bound in bounds]),
        compiler_params=params(16),
        cost_estimate=work(0, array),
        name="cut",
    )(array)


def partial_kernel(n_x, counts, wide, *refs):
    x_refs, w_refs, (out_ref, rows) = refs[:n_x], refs[n_x:-2], refs[-2:]
    at = 0
    for x_ref in x_refs:
        rows[at : at + x_ref.shape[0], :] = x_ref[:, : rows.shape[1]]
        at += x_ref.shape[0]
    shard = w_refs[0].shape[0]
    pieces, at = [], 0
    for count in counts:
        pieces.append(w_refs[at : at + count])
        at += count
    for col in range(0, out_ref.shape[1], wide):
        total = None
        for j, parts in enumerate(pieces):
            at = col
            for w_ref in parts:
                if at < w_ref.shape[1]:
                    break
                at -= w_ref.shape[1]
            term = jnp.dot(
                rows[:, j * shard : (j + 1) * shard],
                w_ref[:, at : at + wide],
                preferred_element_type=jnp.float32,
            )
            total = term if total is None else total + term
        out_ref[:, col : col + wide] = total


def partial(blocks, pieces, wide):
    weights = [part for piece in pieces for part in piece]
    length = sum(block.shape[0] for block in blocks)
    depth = len(pieces) * weights[0].shape[0]
    columns = sum(part.shape[1] for part in pieces[0])
    out = jax.ShapeDtypeStruct((length, columns), jnp.float32)
    counts = [len(piece) for piece in pieces]
    return pl.pallas_call(
        functools.partial(partial_kernel, len(blocks), counts, wide),
        in_specs=[VMEM] * (len(blocks) + len(weights)),
        out_specs=VMEM,
        out_shape=out,
        scratch_shapes=[pltpu.VMEM((length, depth), jnp.bfloat16)],
        compiler_params=params(16),
        cost_estimate=work(2 * length * depth * columns, *blocks, *weights, out),
        name="partial",
    )(*blocks, *weights)


def rope_tile(tile, cos, sin):
    parts = []
    for at in range(0, tile.shape[1], HEAD_SIZE):
        head = tile[:, at : at + HEAD_SIZE]
        parts.append(head * cos + pltpu.roll(head, HALF, axis=1) * sin)
    return parts[0] if len(parts) == 1 else jnp.concatenate(parts, axis=1)


def finish_kernel(n_x, offsets, wide, roped, first_col, index_ref, *refs):
    x_refs = refs[:n_x]
    w_refs = refs[n_x : n_x + 4]
    early_ref, late_ref = refs[n_x + 4 : n_x + 6]
    bias_refs, (cos_ref, sin_ref) = refs[n_x + 6 : n_x + 9], refs[n_x + 9 : n_x + 11]
    q_out, kv_out, rows, cos, sin = refs[n_x + 11 :]
    shard = w_refs[0].shape[0]
    at = 0
    for x_ref in x_refs:
        rows[at : at + x_ref.shape[0], :] = x_ref[:, first_col : first_col + 2 * shard]
        at += x_ref.shape[0]
    blocks = len(offsets)
    count = at // blocks
    for k, offset in enumerate(offsets):
        block = lax.rem(index_ref[1] - offset + blocks, blocks)
        place = pl.ds(pl.multiple_of(block * count, count), count)
        cos[k * count : (k + 1) * count, :] = cos_ref[place, :]
        sin[k * count : (k + 1) * count, :] = sin_ref[place, :]
    q_cols = q_out.shape[1]

    def bias_tile(col):
        for bias_ref in bias_refs:
            if col < bias_ref.shape[0]:
                return bias_ref[pl.ds(col, wide)][None, :]
            col -= bias_ref.shape[0]

    base = 0
    for mine, sibling in (w_refs[:2], w_refs[2:]):
        for at in range(0, mine.shape[1], wide):
            total = jnp.dot(
                rows[:, :shard], mine[:, at : at + wide], preferred_element_type=jnp.float32
            )
            total = total + jnp.dot(
                rows[:, shard:], sibling[:, at : at + wide], preferred_element_type=jnp.float32
            )
            col = base + at
            total = total + jnp.concatenate(
                [early_ref[:, col : col + wide], late_ref[:, col : col + wide]], axis=0
            )
            total = total + bias_tile(col)
            if col < roped:
                total = rope_tile(total, cos[...], sin[...])
            total = total.astype(jnp.bfloat16)
            if col < q_cols:
                q_out[:, col : col + wide] = total
            else:
                kv_out[:, col - q_cols : col - q_cols + wide] = total
        base += mine.shape[1]


def finish(index, blocks, offsets, weights, early, late, biases, cos, sin, q_cols, first_col, wide):
    n_x = len(blocks)
    length = sum(block.shape[0] for block in blocks)
    shard = weights[0].shape[0]
    columns = early.shape[1]
    kv_cols = columns - q_cols
    return pl.pallas_call(
        functools.partial(finish_kernel, n_x, offsets, wide, q_cols + kv_cols // 2, first_col),
        in_specs=[SMEM] + [VMEM] * (n_x + 11),
        out_specs=[VMEM, VMEM],
        out_shape=[bf16(length, q_cols), bf16(length, kv_cols)],
        scratch_shapes=[
            pltpu.VMEM((length, 2 * shard), jnp.bfloat16),
            pltpu.VMEM((length, HEAD_SIZE), jnp.float32),
            pltpu.VMEM((length, HEAD_SIZE), jnp.float32),
        ],
        compiler_params=params(16),
        cost_estimate=work(4 * length * shard * columns, *weights, early, late),
        name="finish",
    )(index, *blocks, *weights, early, late, *biases, cos, sin)


def attend_kernel(offsets, group, index_ref, q_ref, kv_ref, out_ref, keys, values):
    blocks = len(offsets)
    rows = q_ref.shape[0] // blocks
    factor = LOG2E / (HEAD_SIZE**0.5)

    def held(b):
        offset = lax.rem(index_ref[1] - b + blocks, blocks)
        k = sum(jnp.where(offset == value, i, 0) for i, value in enumerate(offsets))
        return pl.ds(pl.multiple_of(k * rows, rows), rows)

    kv_half = kv_ref.shape[1] // 2
    for b in range(blocks):
        keys[b * rows : (b + 1) * rows, :] = kv_ref[held(b), :kv_half]
        values[b * rows : (b + 1) * rows, :] = kv_ref[held(b), kv_half:]
    row = lax.broadcasted_iota(jnp.int32, (rows, rows), 0)
    column = lax.broadcasted_iota(jnp.int32, (rows, rows), 1)
    causal = row >= column
    causal = jnp.concatenate([causal.astype(jnp.float32)] * group, axis=0) > 0.5
    for g, b in [(g, b) for g in range(kv_half // HEAD_SIZE) for b in range(blocks)]:
        left = g * group * HEAD_SIZE
        head = slice(g * HEAD_SIZE, (g + 1) * HEAD_SIZE)
        q_block = q_ref[held(b), left : left + group * HEAD_SIZE]
        queries = jnp.concatenate(
            [q_block[:, h * HEAD_SIZE : (h + 1) * HEAD_SIZE] for h in range(group)], axis=0
        )
        at = b * rows
        near = lax.dot_general(
            queries, keys[at : at + rows, head], NT, preferred_element_type=jnp.float32
        )
        near = jnp.where(causal, near, jnp.float32(-1e30))
        largest = jnp.max(near, axis=-1, keepdims=True)
        if b > 0:
            far = lax.dot_general(queries, keys[:at, head], NT, preferred_element_type=jnp.float32)
            largest = jnp.maximum(largest, jnp.max(far, axis=-1, keepdims=True))
        near = jnp.exp2((near - largest) * factor)
        total = jnp.sum(near, axis=-1, keepdims=True)
        result = jnp.dot(
            near.astype(jnp.bfloat16), values[at : at + rows, head], preferred_element_type=jnp.float32
        )
        if b > 0:
            far = jnp.exp2((far - largest) * factor)
            total = total + jnp.sum(far, axis=-1, keepdims=True)
            result = result + jnp.dot(
                far.astype(jnp.bfloat16), values[:at, head], preferred_element_type=jnp.float32
            )
        result = (result / total).astype(jnp.bfloat16)
        for h in range(group):
            out_ref[held(b), left + h * HEAD_SIZE : left + (h + 1) * HEAD_SIZE] = result[
                h * rows : (h + 1) * rows, :
            ]


def attend(index, queries, kv, offsets):
    length, q_cols = queries.shape
    kv_half = kv.shape[1] // 2
    return pl.pallas_call(
        functools.partial(attend_kernel, offsets, q_cols // kv_half),
        in_specs=[SMEM, VMEM, VMEM],
        out_specs=VMEM,
        out_shape=bf16(length, q_cols),
        scratch_shapes=[
            pltpu.VMEM((length, kv_half), jnp.bfloat16),
            pltpu.VMEM((length, kv_half), jnp.bfloat16),
        ],
        compiler_params=params(16),
        cost_estimate=work(4 * length * length * q_cols, queries, queries, kv),
        name="attend",
    )(index, queries, kv)


def mix_kernel(n_w, heads_ref, *refs):
    w_refs, out_refs = refs[:n_w], refs[n_w:]
    rows = out_refs[0].shape[0]
    weights = [w_ref[...] for w_ref in w_refs]
    weights = weights[0] if n_w == 1 else jnp.concatenate(weights, axis=0)
    term = lax.dot_general(
        heads_ref[...], weights, NT, preferred_element_type=jnp.float32
    ).astype(jnp.bfloat16)
    for k, out_ref in enumerate(out_refs):
        out_ref[...] = term[k * rows : (k + 1) * rows, :]


def mix(heads, parts, blocks):
    length, features = heads.shape
    columns = sum(part.shape[0] for part in parts)
    return pl.pallas_call(
        functools.partial(mix_kernel, len(parts)),
        in_specs=[VMEM] * (1 + len(parts)),
        out_specs=[VMEM] * blocks,
        out_shape=[bf16(length // blocks, columns)] * blocks,
        compiler_params=params(16),
        cost_estimate=work(2 * length * columns * features, heads, *parts),
        name="mix",
    )(heads, *parts)


def add_kernel(a_ref, b_ref, out_ref):
    total = a_ref[...].astype(jnp.float32) + b_ref[...].astype(jnp.float32)
    out_ref[...] = total.astype(jnp.bfloat16)


def add(a, b):
    return pl.pallas_call(
        add_kernel,
        in_specs=[VMEM, VMEM],
        out_specs=VMEM,
        out_shape=bf16(*a.shape),
        compiler_params=params(8),
        cost_estimate=link_time(a),
        name="add",
    )(a, b)


def place_kernel(parts, index_ref, *refs):
    n = len(parts)
    a_refs, b_refs, out_ref, total, sem = refs[:n], refs[n : 2 * n], *refs[-3:]
    copies, left = [], 0
    for a_ref, b_ref, pieces in zip(a_refs, b_refs, parts):
        add_kernel(a_ref, b_ref, total.at[:, pl.ds(left, a_ref.shape[1])])
        for j, shard, offset, width in pieces:
            start = pl.multiple_of(jnp.bitwise_xor(index_ref[0], j) * shard + offset, 128)
            copies.append(
                pltpu.make_async_copy(
                    total.at[:, pl.ds(left, width)],
                    out_ref.at[:, pl.ds(start, width)],
                    sem.at[len(copies)],
                )
            )
            copies[-1].start()
            left += width
    for copy in copies:
        copy.wait()


def place(mixed, index, first, second, parts, columns):
    every = [piece for pieces in parts for piece in pieces]
    count = first[0].shape[0]
    if any(offset % 128 or width % 128 or shard % 128 for _, shard, offset, width in every):
        if mixed is None:
            mixed = jnp.zeros((count, columns), jnp.bfloat16)
        for a, b, pieces in zip(first, second, parts):
            total, left = add(a, b), 0
            for j, shard, offset, width in pieces:
                start = jnp.bitwise_xor(index[0], j) * shard + offset
                mixed = lax.dynamic_update_slice(mixed, total[:, left : left + width], (0, start))
                left += width
        return mixed
    held = [] if mixed is None else [mixed]
    return pl.pallas_call(
        functools.partial(place_kernel, parts),
        in_specs=[SMEM] + [VMEM] * (2 * len(parts)) + [ANY] * len(held),
        out_specs=ANY,
        out_shape=bf16(count, columns),
        scratch_shapes=[
            pltpu.VMEM((count, sum(piece[3] for piece in every)), jnp.bfloat16),
            pltpu.SemaphoreType.DMA((len(every),)),
        ],
        input_output_aliases={1 + 2 * len(parts): 0} if held else {},
        compiler_params=params(8),
        cost_estimate=work(0, *first, *second),
        name="place",
    )(index, *first, *second, *held)


def swapped(array, n_f, mask):
    return lax.ppermute(array, "fsdp", [(i, i ^ mask) for i in range(n_f)])


def after(array, *others):
    return lax.optimization_barrier((array, *others))[0] if others else array


def chips_away(level, chips):
    return [r for r in range(chips) if bin(r).count("1") == level]


def send_level(held, n_f, cut, axis, level, *before):
    for r in chips_away(level, n_f // 2):
        if level == 1:
            held[r] = [swapped(after(held[0][0], *before), n_f, 2 * r)]
            continue
        held[r] = []
        for half, bit in ((0, r & -r), (1, 1 << (r.bit_length() - 1))):
            parts = held[r ^ bit]
            part = parts[half] if len(parts) == 2 else part_of(parts[0], cut, half, axis)
            held[r].append(swapped(after(part, *before), n_f, 2 * bit))


def send_siblings(held, sibling, n_f, level, *before):
    for r in chips_away(level, n_f // 2):
        others = held[r] if len(held[r]) > 1 else []
        sibling[r] = [swapped(after(part, *others, *before), n_f, 1) for part in held[r]]


def rope_tables(length):
    frequency = np.float32(ROPE_BASE) ** (
        -(np.arange(HALF, dtype=np.float32) * np.float32(2.0) / np.float32(HEAD_SIZE))
    )
    angle = np.arange(length, dtype=np.float32)[:, None] * frequency[None, :].astype(np.float32)
    angle = angle.astype(np.float64)
    cos, sin = np.cos(angle).astype(np.float32), np.sin(angle).astype(np.float32)
    return np.concatenate([cos, cos], axis=1), np.concatenate([-sin, sin], axis=1)


def body(
    n_f,
    n_s,
    tokens,
    norm_gain,
    q_weight,
    key_matrix,
    value_matrix,
    q_bias,
    k_bias,
    value_offset_bias,
    out_weight,
):
    index = jnp.stack([lax.axis_index("fsdp"), lax.axis_index("sp")])
    count = tokens.shape[0]
    chips = n_f // 2
    levels = chips.bit_length() - 1
    shard, q_cols = q_weight.shape
    kv_cols = key_matrix.shape[1]
    wide = 256 if q_cols % 256 == 0 and kv_cols % 256 == 0 else 128
    cut = (q_cols + 2 * kv_cols) // wide // 2 * wide
    cut += wide if cut + wide <= q_cols else 0
    o_cut = shard * 3 // 5 // 128 * 128 or shard // 2 // 16 * 16
    right = [(i, (i + 1) % n_s) for i in range(n_s)]
    left = [(i, (i - 1) % n_s) for i in range(n_s)]
    cos, sin = rope_tables(n_s * count)

    own = normed_pieces(index, tokens, norm_gain, n_f)
    held = {0: [pack(after(q_weight, own), key_matrix, value_matrix)]}
    sibling, o_held, o_sibling = {}, {0: [after(out_weight, held[0][0])]}, {}
    send_level(held, n_f, cut, 1, 1)
    send_siblings(held, sibling, n_f, 0)

    steps = n_s // 2
    offsets, blocks, gate = [0], [own], []
    ahead = behind = own
    for step in range(1, steps + 1):
        if step > 1 and step <= levels:
            send_level(held, n_f, cut, 1, step, *gate)
            send_siblings(held, sibling, n_f, step - 1, *gate)
        if step < steps:
            ahead = lax.ppermute(ahead, "sp", right)
            behind = lax.ppermute(behind, "sp", left)
            offsets += [step, n_s - step]
        else:
            ahead = lax.ppermute(part_of(ahead, count // 2, 0, 0), "sp", right)
            behind = lax.ppermute(part_of(behind, count // 2, 1, 0), "sp", left)
            offsets += [step]
        blocks += [ahead, behind]
        gate = [ahead, behind]
        if step == 1:
            send_siblings(o_held, o_sibling, n_f, 0, *gate)

    def pieces_of(chosen):
        return [side[r] for r in chosen for side in (held, sibling)]

    most = pieces_of(range(chips - 1))
    early = partial(blocks[:-2], most, wide)
    send_siblings(held, sibling, n_f, levels, *gate, early)
    send_level(o_held, n_f, o_cut, 0, 1, early)
    late = partial(blocks[-2:], most, wide)
    mine, others = pieces_of([chips - 1])
    queries, kv = finish(
        index,
        blocks,
        offsets,
        [mine[0], others[0], mine[1], others[1]],
        early,
        late,
        (q_bias, k_bias, value_offset_bias),
        cos,
        sin,
        q_cols,
        2 * shard * (chips - 1),
        wide,
    )
    heads = attend(index, queries, kv, offsets)

    rounds = []
    for level in range(levels + 1):
        if level == 1:
            for r in chips_away(1, chips):
                o_held[r] = [after(part, *arrivals[min(1, n_s - 2)]) for part in o_held[r]]
        if level:
            before = arrivals[0] + arrivals[min(1, n_s - 2)][:2] if level > 1 else []
            send_siblings(o_held, o_sibling, n_f, level, *before)
            send_level(o_held, n_f, o_cut, 0, level + 1, *before)
        groups = []
        for r in chips_away(level, chips):
            halves = range(len(o_held[r]))
            if len(halves) == 1:
                groups += [((r, 0, 0),), ((r, 0, 1),)]
            else:
                groups += [((r, half, 0), (r, half, 1)) for half in halves]
        groups.sort(key=lambda group: group[0][2])
        terms = []
        for group in groups:
            weights = [(o_sibling if core else o_held)[r][half] for r, half, core in group]
            mixed = mix(heads, weights, n_s)
            terms.append([mixed[offsets.index(d)] for d in range(n_s)])
        totals, arrivals = [term[1] for term in terms], []
        for d in range(2, n_s + 1):
            arrivals.append([lax.ppermute(total, "sp", right) for total in totals])
            if d < n_s:
                totals = [add(a, term[d]) for a, term in zip(arrivals[-1], terms)]
        where = [
            [(2 * r + core, shard, half * o_cut, o_held[r][half].shape[0]) for r, half, core in group]
            for group in groups
        ]
        rounds.append(([term[0] for term in terms], arrivals, where))

    mixed = None
    for chosen in (rounds[:-1], rounds[-1:]):
        mixed = place(
            mixed,
            index,
            [a for _, arrivals, _ in chosen for a in arrivals[-1]],
            [own for owns, _, _ in chosen for own in owns],
            [parts for _, _, where in chosen for parts in where],
            shard * n_f,
        )
    return mixed


def solution(mesh):
    n_f, n_s = mesh.shape["fsdp"], mesh.shape["sp"]
    placed = (
        P(("fsdp", "sp"), None),
        P(),
        P("fsdp", "sp"),
        P("fsdp", "sp"),
        P("fsdp", "sp"),
        P("sp"),
        P("sp"),
        P("sp"),
        P("fsdp", "sp"),
    )
    return jax.shard_map(
        functools.partial(body, n_f, n_s),
        mesh=mesh,
        in_specs=placed,
        out_specs=P(("fsdp", "sp"), None),
        check_vma=False,
    )
```

```python
import functools

import jax
import jax.numpy as jnp
import numpy as np
from jax import lax
from jax.experimental import pallas as pl
from jax.experimental.pallas import tpu as pltpu
from jax.sharding import PartitionSpec as P

HEAD_SIZE = 128
HALF = HEAD_SIZE // 2
ROPE_BASE = 1000000.0
LOG2E = 1.4426950408889634
EXCHANGE = 11500000000
NT = (((1,), (1,)), ((), ()))
VMEM = pl.BlockSpec(memory_space=pltpu.VMEM)
SMEM = pl.BlockSpec(memory_space=pltpu.SMEM)
ANY = pl.BlockSpec(memory_space=pl.ANY)


def params(mib):
    return pltpu.CompilerParams(vmem_limit_bytes=mib * 1024 * 1024)


def bf16(*shape):
    return jax.ShapeDtypeStruct(shape, jnp.bfloat16)


def work(flops, *arrays):
    size = sum(int(np.prod(x.shape)) * x.dtype.itemsize for x in arrays)
    return pl.CostEstimate(flops=flops, bytes_accessed=size, transcendentals=0)


def link_time(array, share=2):
    size = share * int(np.prod(array.shape)) * array.dtype.itemsize
    return pl.CostEstimate(flops=size * 300, bytes_accessed=size, transcendentals=0)


def normed_kernel(n_f, index_ref, tokens_ref, gain_ref, out_ref):
    rows = tokens_ref[...].astype(jnp.float32)
    scale = lax.rsqrt(jnp.mean(rows * rows, axis=-1, keepdims=True) + 1e-06)
    shard = tokens_ref.shape[1] // n_f
    for j in range(n_f):
        start = pl.multiple_of(jnp.bitwise_xor(index_ref[0], j) * shard, 128)
        columns = pl.ds(start, shard)
        piece = tokens_ref[:, columns].astype(jnp.float32) * scale * gain_ref[:, columns]
        out_ref[:, j * shard : (j + 1) * shard] = piece.astype(jnp.bfloat16)


def normed_pieces(index, tokens, gain, n_f):
    count, width = tokens.shape
    shard = width // n_f
    if shard % 128 == 0:
        return pl.pallas_call(
            functools.partial(normed_kernel, n_f),
            out_shape=bf16(count, width),
            in_specs=[SMEM, VMEM, VMEM],
            out_specs=VMEM,
            compiler_params=params(16),
            cost_estimate=work(6 * count * width, tokens, tokens),
            name="norm",
        )(index, tokens, gain[None, :])
    rows = tokens.astype(jnp.float32)
    meansq = jnp.mean(rows * rows, axis=-1, keepdims=True)
    normed = (rows * lax.rsqrt(meansq + 1e-06) * gain).astype(jnp.bfloat16)
    pieces = [
        lax.dynamic_slice_in_dim(normed, jnp.bitwise_xor(index[0], j) * shard, shard, axis=1)
        for j in range(n_f)
    ]
    return jnp.concatenate(pieces, axis=1)


def pack_kernel(*refs):
    out_ref, at = refs[-1], 0
    for ref in refs[:-1]:
        out_ref[:, at : at + ref.shape[1]] = ref[...]
        at += ref.shape[1]


def pack(*arrays):
    return pl.pallas_call(
        pack_kernel,
        in_specs=[VMEM] * len(arrays),
        out_specs=VMEM,
        out_shape=bf16(arrays[0].shape[0], sum(x.shape[1] for x in arrays)),
        compiler_params=params(16),
        cost_estimate=work(0, *arrays, *arrays),
        name="pack",
    )(*arrays)


def cut_kernel(rows, columns, ref, out_ref):
    out_ref[...] = ref[rows, columns]


def part_of(array, cut, half, axis, cost=0):
    bounds = [slice(0, size) for size in array.shape]
    bounds[axis] = slice(cut, array.shape[axis]) if half else slice(0, cut)
    return pl.pallas_call(
        functools.partial(cut_kernel, *bounds),
        in_specs=[VMEM],
        out_specs=VMEM,
        out_shape=bf16(*[bound.stop - bound.start for bound in bounds]),
        compiler_params=params(16),
        cost_estimate=work(cost, array),
        name="cut",
    )(array)


def partial_kernel(n_x, counts, wide, *refs):
    x_refs, w_refs, (out_ref, rows) = refs[:n_x], refs[n_x:-2], refs[-2:]
    at = 0
    for x_ref in x_refs:
        rows[at : at + x_ref.shape[0], :] = x_ref[:, : rows.shape[1]]
        at += x_ref.shape[0]
    shard = w_refs[0].shape[0]
    pieces, at = [], 0
    for count in counts:
        pieces.append(w_refs[at : at + count])
        at += count
    for col in range(0, out_ref.shape[1], wide):
        total = None
        for j, parts in enumerate(pieces):
            at = col
            for w_ref in parts:
                if at < w_ref.shape[1]:
                    break
                at -= w_ref.shape[1]
            term = jnp.dot(
                rows[:, j * shard : (j + 1) * shard],
                w_ref[:, at : at + wide],
                preferred_element_type=jnp.float32,
            )
            total = term if total is None else total + term
        out_ref[:, col : col + wide] = total


def partial(blocks, pieces, wide, declared):
    weights = [part for piece in pieces for part in piece]
    length = sum(block.shape[0] for block in blocks)
    depth = len(pieces) * weights[0].shape[0]
    columns = sum(part.shape[1] for part in pieces[0])
    out = jax.ShapeDtypeStruct((length, columns), jnp.float32)
    counts = [len(piece) for piece in pieces]
    return pl.pallas_call(
        functools.partial(partial_kernel, len(blocks), counts, wide),
        in_specs=[VMEM] * (len(blocks) + len(weights)),
        out_specs=VMEM,
        out_shape=out,
        scratch_shapes=[pltpu.VMEM((length, depth), jnp.bfloat16)],
        compiler_params=params(16),
        cost_estimate=work(2 * length * depth * columns if declared else 0),
        name="partial",
    )(*blocks, *weights)


def rope_tile(tile, cos, sin):
    parts = []
    for at in range(0, tile.shape[1], HEAD_SIZE):
        head = tile[:, at : at + HEAD_SIZE]
        parts.append(head * cos + pltpu.roll(head, HALF, axis=1) * sin)
    return parts[0] if len(parts) == 1 else jnp.concatenate(parts, axis=1)


def finish_kernel(n_x, offsets, wide, roped, first_col, index_ref, *refs):
    x_refs = refs[:n_x]
    w_refs = refs[n_x : n_x + 4]
    early_ref, late_ref = refs[n_x + 4 : n_x + 6]
    bias_refs, (cos_ref, sin_ref) = refs[n_x + 6 : n_x + 9], refs[n_x + 9 : n_x + 11]
    q_out, kv_out, rows, cos, sin = refs[n_x + 11 :]
    shard = w_refs[0].shape[0]
    at = 0
    for x_ref in x_refs:
        rows[at : at + x_ref.shape[0], :] = x_ref[:, first_col : first_col + 2 * shard]
        at += x_ref.shape[0]
    blocks = len(offsets)
    count = at // blocks
    for k, offset in enumerate(offsets):
        block = lax.rem(index_ref[1] - offset + blocks, blocks)
        place = pl.ds(pl.multiple_of(block * count, count), count)
        cos[k * count : (k + 1) * count, :] = cos_ref[place, :]
        sin[k * count : (k + 1) * count, :] = sin_ref[place, :]
    q_cols = q_out.shape[1]

    def bias_tile(col):
        for bias_ref in bias_refs:
            if col < bias_ref.shape[0]:
                return bias_ref[pl.ds(col, wide)][None, :]
            col -= bias_ref.shape[0]

    base = 0
    for mine, sibling in (w_refs[:2], w_refs[2:]):
        for at in range(0, mine.shape[1], wide):
            total = jnp.dot(
                rows[:, :shard], mine[:, at : at + wide], preferred_element_type=jnp.float32
            )
            total = total + jnp.dot(
                rows[:, shard:], sibling[:, at : at + wide], preferred_element_type=jnp.float32
            )
            col = base + at
            total = total + jnp.concatenate(
                [early_ref[:, col : col + wide], late_ref[:, col : col + wide]], axis=0
            )
            total = total + bias_tile(col)
            if col < roped:
                total = rope_tile(total, cos[...], sin[...])
            total = total.astype(jnp.bfloat16)
            if col < q_cols:
                q_out[:, col : col + wide] = total
            else:
                kv_out[:, col - q_cols : col - q_cols + wide] = total
        base += mine.shape[1]


def finish(index, blocks, offsets, weights, early, late, biases, cos, sin, q_cols, first_col, wide):
    n_x = len(blocks)
    length = sum(block.shape[0] for block in blocks)
    shard = weights[0].shape[0]
    columns = early.shape[1]
    kv_cols = columns - q_cols
    return pl.pallas_call(
        functools.partial(finish_kernel, n_x, offsets, wide, q_cols + kv_cols // 2, first_col),
        in_specs=[SMEM] + [VMEM] * (n_x + 11),
        out_specs=[VMEM, VMEM],
        out_shape=[bf16(length, q_cols), bf16(length, kv_cols)],
        scratch_shapes=[
            pltpu.VMEM((length, 2 * shard), jnp.bfloat16),
            pltpu.VMEM((length, HEAD_SIZE), jnp.float32),
            pltpu.VMEM((length, HEAD_SIZE), jnp.float32),
        ],
        compiler_params=params(16),
        cost_estimate=work(0),
        name="finish",
    )(index, *blocks, *weights, early, late, *biases, cos, sin)


def attend_kernel(offsets, group, index_ref, q_ref, kv_ref, out_ref, keys, values):
    blocks = len(offsets)
    rows = q_ref.shape[0] // blocks
    factor = LOG2E / (HEAD_SIZE**0.5)

    def held(b):
        offset = lax.rem(index_ref[1] - b + blocks, blocks)
        k = sum(jnp.where(offset == value, i, 0) for i, value in enumerate(offsets))
        return pl.ds(pl.multiple_of(k * rows, rows), rows)

    kv_half = kv_ref.shape[1] // 2
    for b in range(blocks):
        keys[b * rows : (b + 1) * rows, :] = kv_ref[held(b), :kv_half]
        values[b * rows : (b + 1) * rows, :] = kv_ref[held(b), kv_half:]
    row = lax.broadcasted_iota(jnp.int32, (rows, rows), 0)
    column = lax.broadcasted_iota(jnp.int32, (rows, rows), 1)
    causal = row >= column
    causal = jnp.concatenate([causal.astype(jnp.float32)] * group, axis=0) > 0.5
    for g, b in [(g, b) for g in range(kv_half // HEAD_SIZE) for b in range(blocks)]:
        left = g * group * HEAD_SIZE
        head = slice(g * HEAD_SIZE, (g + 1) * HEAD_SIZE)
        q_block = q_ref[held(b), left : left + group * HEAD_SIZE]
        queries = jnp.concatenate(
            [q_block[:, h * HEAD_SIZE : (h + 1) * HEAD_SIZE] for h in range(group)], axis=0
        )
        at = b * rows
        near = lax.dot_general(
            queries, keys[at : at + rows, head], NT, preferred_element_type=jnp.float32
        )
        near = jnp.where(causal, near, jnp.float32(-1e30))
        largest = jnp.max(near, axis=-1, keepdims=True)
        if b > 0:
            far = lax.dot_general(queries, keys[:at, head], NT, preferred_element_type=jnp.float32)
            largest = jnp.maximum(largest, jnp.max(far, axis=-1, keepdims=True))
        near = jnp.exp2((near - largest) * factor)
        total = jnp.sum(near, axis=-1, keepdims=True)
        result = jnp.dot(
            near.astype(jnp.bfloat16), values[at : at + rows, head], preferred_element_type=jnp.float32
        )
        if b > 0:
            far = jnp.exp2((far - largest) * factor)
            total = total + jnp.sum(far, axis=-1, keepdims=True)
            result = result + jnp.dot(
                far.astype(jnp.bfloat16), values[:at, head], preferred_element_type=jnp.float32
            )
        result = (result / total).astype(jnp.bfloat16)
        for h in range(group):
            out_ref[held(b), left + h * HEAD_SIZE : left + (h + 1) * HEAD_SIZE] = result[
                h * rows : (h + 1) * rows, :
            ]


def attend(index, queries, kv, offsets):
    length, q_cols = queries.shape
    kv_half = kv.shape[1] // 2
    return pl.pallas_call(
        functools.partial(attend_kernel, offsets, q_cols // kv_half),
        in_specs=[SMEM, VMEM, VMEM],
        out_specs=VMEM,
        out_shape=bf16(length, q_cols),
        scratch_shapes=[
            pltpu.VMEM((length, kv_half), jnp.bfloat16),
            pltpu.VMEM((length, kv_half), jnp.bfloat16),
        ],
        compiler_params=params(16),
        cost_estimate=work(0),
        name="attend",
    )(index, queries, kv)


def mix_kernel(n_w, heads_ref, *refs):
    w_refs, out_refs = refs[:n_w], refs[n_w:]
    rows = out_refs[0].shape[0]
    weights = [w_ref[...] for w_ref in w_refs]
    weights = weights[0] if n_w == 1 else jnp.concatenate(weights, axis=0)
    term = lax.dot_general(
        heads_ref[...], weights, NT, preferred_element_type=jnp.float32
    ).astype(jnp.bfloat16)
    for k, out_ref in enumerate(out_refs):
        out_ref[...] = term[k * rows : (k + 1) * rows, :]


def mix(heads, parts, blocks):
    length, features = heads.shape
    columns = sum(part.shape[0] for part in parts)
    return pl.pallas_call(
        functools.partial(mix_kernel, len(parts)),
        in_specs=[VMEM] * (1 + len(parts)),
        out_specs=[VMEM] * blocks,
        out_shape=[bf16(length // blocks, columns)] * blocks,
        compiler_params=params(16),
        cost_estimate=work(0),
        name="mix",
    )(heads, *parts)


def add_kernel(a_ref, b_ref, out_ref):
    total = a_ref[...].astype(jnp.float32) + b_ref[...].astype(jnp.float32)
    out_ref[...] = total.astype(jnp.bfloat16)


def add(a, b):
    return pl.pallas_call(
        add_kernel,
        in_specs=[VMEM, VMEM],
        out_specs=VMEM,
        out_shape=bf16(*a.shape),
        compiler_params=params(8),
        cost_estimate=link_time(a),
        name="add",
    )(a, b)


def place_kernel(parts, index_ref, *refs):
    n = len(parts)
    a_refs, b_refs, out_ref, total, sem = refs[:n], refs[n : 2 * n], *refs[-3:]
    copies, left = [], 0
    for a_ref, b_ref, pieces in zip(a_refs, b_refs, parts):
        add_kernel(a_ref, b_ref, total.at[:, pl.ds(left, a_ref.shape[1])])
        for j, shard, offset, width in pieces:
            start = pl.multiple_of(jnp.bitwise_xor(index_ref[0], j) * shard + offset, 128)
            copies.append(
                pltpu.make_async_copy(
                    total.at[:, pl.ds(left, width)],
                    out_ref.at[:, pl.ds(start, width)],
                    sem.at[len(copies)],
                )
            )
            copies[-1].start()
            left += width
    for copy in copies:
        copy.wait()


def place(mixed, index, first, second, parts, columns):
    every = [piece for pieces in parts for piece in pieces]
    count = first[0].shape[0]
    if any(offset % 128 or width % 128 or shard % 128 for _, shard, offset, width in every):
        if mixed is None:
            mixed = jnp.zeros((count, columns), jnp.bfloat16)
        for a, b, pieces in zip(first, second, parts):
            total, left = add(a, b), 0
            for j, shard, offset, width in pieces:
                start = jnp.bitwise_xor(index[0], j) * shard + offset
                mixed = lax.dynamic_update_slice(mixed, total[:, left : left + width], (0, start))
                left += width
        return mixed
    held = [] if mixed is None else [mixed]
    return pl.pallas_call(
        functools.partial(place_kernel, parts),
        in_specs=[SMEM] + [VMEM] * (2 * len(parts)) + [ANY] * len(held),
        out_specs=ANY,
        out_shape=bf16(count, columns),
        scratch_shapes=[
            pltpu.VMEM((count, sum(piece[3] for piece in every)), jnp.bfloat16),
            pltpu.SemaphoreType.DMA((len(every),)),
        ],
        input_output_aliases={1 + 2 * len(parts): 0} if held else {},
        compiler_params=params(8),
        cost_estimate=work(0, *first, *second),
        name="place",
    )(index, *first, *second, *held)


def swapped(array, n_f, mask):
    return lax.ppermute(array, "fsdp", [(i, i ^ mask) for i in range(n_f)])


def after(array, *others):
    return lax.optimization_barrier((array, *others))[0] if others else array


def chips_away(level, chips):
    return [r for r in range(chips) if bin(r).count("1") == level]


def send_level(held, n_f, cut, axis, level, *before):
    for r in chips_away(level, n_f // 2):
        if level == 1:
            held[r] = [swapped(after(held[0][0], *before), n_f, 2 * r)]
            continue
        held[r] = []
        for half, bit in ((0, r & -r), (1, 1 << (r.bit_length() - 1))):
            parts = held[r ^ bit]
            part = parts[half] if len(parts) == 2 else part_of(parts[0], cut, half, axis)
            held[r].append(swapped(after(part, *before), n_f, 2 * bit))


def send_siblings(held, sibling, n_f, level, *before):
    for r in chips_away(level, n_f // 2):
        others = held[r] if len(held[r]) > 1 else []
        sibling[r] = [swapped(after(part, *others, *before), n_f, 1) for part in held[r]]


def rope_tables(length):
    frequency = np.float32(ROPE_BASE) ** (
        -(np.arange(HALF, dtype=np.float32) * np.float32(2.0) / np.float32(HEAD_SIZE))
    )
    angle = np.arange(length, dtype=np.float32)[:, None] * frequency[None, :].astype(np.float32)
    angle = angle.astype(np.float64)
    cos, sin = np.cos(angle).astype(np.float32), np.sin(angle).astype(np.float32)
    return np.concatenate([cos, cos], axis=1), np.concatenate([-sin, sin], axis=1)


def body(
    n_f,
    n_s,
    tokens,
    norm_gain,
    q_weight,
    key_matrix,
    value_matrix,
    q_bias,
    k_bias,
    value_offset_bias,
    out_weight,
):
    index = jnp.stack([lax.axis_index("fsdp"), lax.axis_index("sp")])
    count = tokens.shape[0]
    chips = n_f // 2
    levels = chips.bit_length() - 1
    shard, q_cols = q_weight.shape
    kv_cols = key_matrix.shape[1]
    wide = 256 if q_cols % 256 == 0 and kv_cols % 256 == 0 else 128
    cut = (q_cols + 2 * kv_cols) // wide // 2 * wide
    cut += wide if cut + wide <= q_cols else 0
    o_cut = shard * 3 // 5 // 128 * 128 or shard // 2 // 16 * 16
    right = [(i, (i + 1) % n_s) for i in range(n_s)]
    left = [(i, (i - 1) % n_s) for i in range(n_s)]
    cos, sin = rope_tables(n_s * count)

    own = normed_pieces(index, tokens, norm_gain, n_f)
    held = {0: [pack(after(q_weight, own), key_matrix, value_matrix)]}
    sibling, o_held, o_sibling = {}, {0: [after(out_weight, held[0][0])]}, {}
    send_level(held, n_f, cut, 1, 1)
    send_siblings(held, sibling, n_f, 0)

    steps = n_s // 2
    offsets, blocks, gate = [0], [own], []
    ahead = behind = own
    for step in range(1, steps + 1):
        if step > 1 and step <= levels:
            send_level(held, n_f, cut, 1, step, *gate)
            send_siblings(held, sibling, n_f, step - 1, *gate)
        if step < steps:
            ahead = lax.ppermute(ahead, "sp", right)
            behind = lax.ppermute(behind, "sp", left)
            offsets += [step, n_s - step]
        else:
            ahead = lax.ppermute(halves[0], "sp", right)
            behind = lax.ppermute(halves[1], "sp", left)
            offsets += [step]
        blocks += [ahead, behind]
        gate = [ahead, behind]
        if step == steps - 1:
            halves = [part_of(x, count // 2, i, 0, EXCHANGE) for i, x in enumerate(gate)]
            gate = halves[1:]
        if step == 1:
            send_siblings(o_held, o_sibling, n_f, 0, *gate)

    def pieces_of(chosen):
        return [side[r] for r in chosen for side in (held, sibling)]

    most = pieces_of(range(chips - 1))
    early = partial(blocks[:-2], most, wide, True)
    send_siblings(held, sibling, n_f, levels, early)
    send_level(o_held, n_f, o_cut, 0, 1, early)
    late = partial(blocks[-2:], most, wide, False)
    mine, others = pieces_of([chips - 1])
    queries, kv = finish(
        index,
        blocks,
        offsets,
        [mine[0], others[0], mine[1], others[1]],
        early,
        late,
        (q_bias, k_bias, value_offset_bias),
        cos,
        sin,
        q_cols,
        2 * shard * (chips - 1),
        wide,
    )
    heads = attend(index, queries, kv, offsets)

    sets = []

    def start(level, groups):
        terms = []
        for group in groups:
            weights = [(o_sibling if core else o_held)[r][half] for r, half, core in group]
            mixed = mix(heads, weights, n_s)
            terms.append([mixed[offsets.index(d)] for d in range(n_s)])
        where = [
            [(2 * r + core, shard, half * o_cut, o_held[r][half].shape[0]) for r, half, core in group]
            for group in groups
        ]
        arrived = [lax.ppermute(term[1], "sp", right) for term in terms]
        sets.append((terms, [arrived], where))

    def advance(which, *before):
        terms, arrivals, _ = which
        d = len(arrivals) + 1
        totals = [add(after(a, *before), term[d]) for a, term in zip(arrivals[-1], terms)]
        arrivals.append([lax.ppermute(total, "sp", right) for total in totals])

    def complete(which, *before):
        while len(which[1]) < n_s - 1:
            advance(which, *before)
            before = ()

    for level in range(levels + 1):
        near = chips_away(level, chips)
        if level == 1:
            for r in near:
                o_held[r] = [after(part, *sets[0][1][0]) for part in o_held[r]]
        if level:
            before = sets[-1][1][0] if level > 1 else []
            send_siblings(o_held, o_sibling, n_f, level, *before)
            send_level(o_held, n_f, o_cut, 0, level + 1, *before)
        if level == 0:
            plans = [[tuple((r, 0, core) for r in near for core in (0, 1))]]
        elif level == 1:
            plans = [[tuple((r, 0, core) for r in near)] for core in (0, 1)]
        else:
            plans = [[tuple((r, half, core) for r in near for half in (0, 1) for core in (0, 1))]]
        for groups in plans:
            start(level, groups)
            current = sets[-1]
            if len(sets) == 1:
                advance(current, *current[1][0])
            elif len(sets) == 2:
                complete(sets[-2])
                advance(current, *current[1][0], *sets[-2][1][-1])
            else:
                complete(sets[-2], *current[1][0])
                advance(current, *current[1][0], *sets[-2][1][1])
    complete(sets[-1])
    rounds = [([term[0] for term in terms], arrivals, where) for terms, arrivals, where in sets]

    mixed = None
    for chosen in (rounds[:-1], rounds[-1:]):
        mixed = place(
            mixed,
            index,
            [a for _, arrivals, _ in chosen for a in arrivals[-1]],
            [own for owns, _, _ in chosen for own in owns],
            [parts for _, _, where in chosen for parts in where],
            shard * n_f,
        )
    return mixed


def solution(mesh):
    n_f, n_s = mesh.shape["fsdp"], mesh.shape["sp"]
    placed = (
        P(("fsdp", "sp"), None),
        P(),
        P("fsdp", "sp"),
        P("fsdp", "sp"),
        P("fsdp", "sp"),
        P("sp"),
        P("sp"),
        P("sp"),
        P("fsdp", "sp"),
    )
    return jax.shard_map(
        functools.partial(body, n_f, n_s),
        mesh=mesh,
        in_specs=placed,
        out_specs=P(("fsdp", "sp"), None),
        check_vma=False,
    )
```

```python
import functools

import jax
import jax.numpy as jnp
import numpy as np
from jax import lax
from jax.experimental import pallas as pl
from jax.experimental.pallas import tpu as pltpu
from jax.sharding import PartitionSpec as P

HEAD_SIZE = 128
HALF = HEAD_SIZE // 2
ROPE_BASE = 1000000.0
LOG2E = 1.4426950408889634
EXCHANGE = 11500000000
NT = (((1,), (1,)), ((), ()))
VMEM = pl.BlockSpec(memory_space=pltpu.VMEM)
SMEM = pl.BlockSpec(memory_space=pltpu.SMEM)
ANY = pl.BlockSpec(memory_space=pl.ANY)


def params(mib):
    return pltpu.CompilerParams(vmem_limit_bytes=mib * 1024 * 1024)


def bf16(*shape):
    return jax.ShapeDtypeStruct(shape, jnp.bfloat16)


def work(flops, *arrays):
    size = sum(int(np.prod(x.shape)) * x.dtype.itemsize for x in arrays)
    return pl.CostEstimate(flops=flops, bytes_accessed=size, transcendentals=0)


def normed_kernel(n_f, index_ref, tokens_ref, gain_ref, out_ref):
    rows = tokens_ref[...].astype(jnp.float32)
    scale = lax.rsqrt(jnp.mean(rows * rows, axis=-1, keepdims=True) + 1e-06)
    shard = tokens_ref.shape[1] // n_f
    for j in range(n_f):
        start = pl.multiple_of(jnp.bitwise_xor(index_ref[0], j) * shard, 128)
        columns = pl.ds(start, shard)
        piece = tokens_ref[:, columns].astype(jnp.float32) * scale * gain_ref[:, columns]
        out_ref[:, j * shard : (j + 1) * shard] = piece.astype(jnp.bfloat16)


def normed_pieces(index, tokens, gain, n_f):
    count, width = tokens.shape
    shard = width // n_f
    if shard % 128 == 0:
        return pl.pallas_call(
            functools.partial(normed_kernel, n_f),
            out_shape=bf16(count, width),
            in_specs=[SMEM, VMEM, VMEM],
            out_specs=VMEM,
            compiler_params=params(16),
            cost_estimate=work(6 * count * width, tokens, tokens),
            name="norm",
        )(index, tokens, gain[None, :])
    rows = tokens.astype(jnp.float32)
    meansq = jnp.mean(rows * rows, axis=-1, keepdims=True)
    normed = (rows * lax.rsqrt(meansq + 1e-06) * gain).astype(jnp.bfloat16)
    pieces = [
        lax.dynamic_slice_in_dim(normed, jnp.bitwise_xor(index[0], j) * shard, shard, axis=1)
        for j in range(n_f)
    ]
    return jnp.concatenate(pieces, axis=1)


def pack_kernel(*refs):
    out_ref, at = refs[-1], 0
    for ref in refs[:-1]:
        out_ref[:, at : at + ref.shape[1]] = ref[...]
        at += ref.shape[1]


def pack(*arrays):
    return pl.pallas_call(
        pack_kernel,
        in_specs=[VMEM] * len(arrays),
        out_specs=VMEM,
        out_shape=bf16(arrays[0].shape[0], sum(x.shape[1] for x in arrays)),
        compiler_params=params(16),
        cost_estimate=work(0, *arrays, *arrays),
        name="pack",
    )(*arrays)


def cut_kernel(rows, columns, ref, out_ref):
    out_ref[...] = ref[rows, columns]


def part_of(array, cut, half, axis, cost=0):
    bounds = [slice(0, size) for size in array.shape]
    bounds[axis] = slice(cut, array.shape[axis]) if half else slice(0, cut)
    return pl.pallas_call(
        functools.partial(cut_kernel, *bounds),
        in_specs=[VMEM],
        out_specs=VMEM,
        out_shape=bf16(*[bound.stop - bound.start for bound in bounds]),
        compiler_params=params(16),
        cost_estimate=work(cost, array),
        name="cut",
    )(array)


def partial_kernel(n_x, counts, wide, *refs):
    x_refs, w_refs, (out_ref, rows) = refs[:n_x], refs[n_x:-2], refs[-2:]
    at = 0
    for x_ref in x_refs:
        rows[at : at + x_ref.shape[0], :] = x_ref[:, : rows.shape[1]]
        at += x_ref.shape[0]
    shard = w_refs[0].shape[0]
    pieces, at = [], 0
    for count in counts:
        pieces.append(w_refs[at : at + count])
        at += count
    for col in range(0, out_ref.shape[1], wide):
        total = None
        for j, parts in enumerate(pieces):
            at = col
            for w_ref in parts:
                if at < w_ref.shape[1]:
                    break
                at -= w_ref.shape[1]
            term = jnp.dot(
                rows[:, j * shard : (j + 1) * shard],
                w_ref[:, at : at + wide],
                preferred_element_type=jnp.float32,
            )
            total = term if total is None else total + term
        out_ref[:, col : col + wide] = total


def partial(blocks, pieces, wide, declared):
    weights = [part for piece in pieces for part in piece]
    length = sum(block.shape[0] for block in blocks)
    depth = len(pieces) * weights[0].shape[0]
    columns = sum(part.shape[1] for part in pieces[0])
    out = jax.ShapeDtypeStruct((length, columns), jnp.float32)
    counts = [len(piece) for piece in pieces]
    return pl.pallas_call(
        functools.partial(partial_kernel, len(blocks), counts, wide),
        in_specs=[VMEM] * (len(blocks) + len(weights)),
        out_specs=VMEM,
        out_shape=out,
        scratch_shapes=[pltpu.VMEM((length, depth), jnp.bfloat16)],
        compiler_params=params(16),
        cost_estimate=work(2 * length * depth * columns if declared else 0),
        name="partial",
    )(*blocks, *weights)


def rope_tile(tile, cos, sin):
    parts = []
    for at in range(0, tile.shape[1], HEAD_SIZE):
        head = tile[:, at : at + HEAD_SIZE]
        parts.append(head * cos + pltpu.roll(head, HALF, axis=1) * sin)
    return parts[0] if len(parts) == 1 else jnp.concatenate(parts, axis=1)


def finish_kernel(n_x, offsets, wide, roped, first_col, index_ref, *refs):
    x_refs = refs[:n_x]
    w_refs = refs[n_x : n_x + 4]
    early_ref, late_ref = refs[n_x + 4 : n_x + 6]
    bias_refs, (cos_ref, sin_ref) = refs[n_x + 6 : n_x + 9], refs[n_x + 9 : n_x + 11]
    q_out, kv_out, rows, cos, sin = refs[n_x + 11 :]
    shard = w_refs[0].shape[0]
    at = 0
    for x_ref in x_refs:
        rows[at : at + x_ref.shape[0], :] = x_ref[:, first_col : first_col + 2 * shard]
        at += x_ref.shape[0]
    blocks = len(offsets)
    count = at // blocks
    for k, offset in enumerate(offsets):
        block = lax.rem(index_ref[1] - offset + blocks, blocks)
        place = pl.ds(pl.multiple_of(block * count, count), count)
        cos[k * count : (k + 1) * count, :] = cos_ref[place, :]
        sin[k * count : (k + 1) * count, :] = sin_ref[place, :]
    q_cols = q_out.shape[1]

    def bias_tile(col):
        for bias_ref in bias_refs:
            if col < bias_ref.shape[0]:
                return bias_ref[pl.ds(col, wide)][None, :]
            col -= bias_ref.shape[0]

    base = 0
    for mine, sibling in (w_refs[:2], w_refs[2:]):
        for at in range(0, mine.shape[1], wide):
            total = jnp.dot(
                rows[:, :shard], mine[:, at : at + wide], preferred_element_type=jnp.float32
            )
            total = total + jnp.dot(
                rows[:, shard:], sibling[:, at : at + wide], preferred_element_type=jnp.float32
            )
            col = base + at
            total = total + jnp.concatenate(
                [early_ref[:, col : col + wide], late_ref[:, col : col + wide]], axis=0
            )
            total = total + bias_tile(col)
            if col < roped:
                total = rope_tile(total, cos[...], sin[...])
            total = total.astype(jnp.bfloat16)
            if col < q_cols:
                q_out[:, col : col + wide] = total
            else:
                kv_out[:, col - q_cols : col - q_cols + wide] = total
        base += mine.shape[1]


def finish(index, blocks, offsets, weights, early, late, biases, cos, sin, q_cols, first_col, wide):
    n_x = len(blocks)
    length = sum(block.shape[0] for block in blocks)
    shard = weights[0].shape[0]
    columns = early.shape[1]
    kv_cols = columns - q_cols
    return pl.pallas_call(
        functools.partial(finish_kernel, n_x, offsets, wide, q_cols + kv_cols // 2, first_col),
        in_specs=[SMEM] + [VMEM] * (n_x + 11),
        out_specs=[VMEM, VMEM],
        out_shape=[bf16(length, q_cols), bf16(length, kv_cols)],
        scratch_shapes=[
            pltpu.VMEM((length, 2 * shard), jnp.bfloat16),
            pltpu.VMEM((length, HEAD_SIZE), jnp.float32),
            pltpu.VMEM((length, HEAD_SIZE), jnp.float32),
        ],
        compiler_params=params(16),
        cost_estimate=work(0),
        name="finish",
    )(index, *blocks, *weights, early, late, *biases, cos, sin)


def attend_kernel(offsets, group, index_ref, q_ref, kv_ref, out_ref, keys, values):
    blocks = len(offsets)
    rows = q_ref.shape[0] // blocks
    factor = LOG2E / (HEAD_SIZE**0.5)

    def held(b):
        offset = lax.rem(index_ref[1] - b + blocks, blocks)
        k = sum(jnp.where(offset == value, i, 0) for i, value in enumerate(offsets))
        return pl.ds(pl.multiple_of(k * rows, rows), rows)

    kv_half = kv_ref.shape[1] // 2
    for b in range(blocks):
        keys[b * rows : (b + 1) * rows, :] = kv_ref[held(b), :kv_half]
        values[b * rows : (b + 1) * rows, :] = kv_ref[held(b), kv_half:]
    row = lax.broadcasted_iota(jnp.int32, (rows, rows), 0)
    column = lax.broadcasted_iota(jnp.int32, (rows, rows), 1)
    causal = row >= column
    causal = jnp.concatenate([causal.astype(jnp.float32)] * group, axis=0) > 0.5
    for g, b in [(g, b) for g in range(kv_half // HEAD_SIZE) for b in range(blocks)]:
        left = g * group * HEAD_SIZE
        head = slice(g * HEAD_SIZE, (g + 1) * HEAD_SIZE)
        q_block = q_ref[held(b), left : left + group * HEAD_SIZE]
        queries = jnp.concatenate(
            [q_block[:, h * HEAD_SIZE : (h + 1) * HEAD_SIZE] for h in range(group)], axis=0
        )
        at = b * rows
        near = lax.dot_general(
            queries, keys[at : at + rows, head], NT, preferred_element_type=jnp.float32
        )
        near = jnp.where(causal, near, jnp.float32(-1e30))
        largest = jnp.max(near, axis=-1, keepdims=True)
        if b > 0:
            far = lax.dot_general(queries, keys[:at, head], NT, preferred_element_type=jnp.float32)
            largest = jnp.maximum(largest, jnp.max(far, axis=-1, keepdims=True))
        near = jnp.exp2((near - largest) * factor)
        total = jnp.sum(near, axis=-1, keepdims=True)
        result = jnp.dot(
            near.astype(jnp.bfloat16), values[at : at + rows, head], preferred_element_type=jnp.float32
        )
        if b > 0:
            far = jnp.exp2((far - largest) * factor)
            total = total + jnp.sum(far, axis=-1, keepdims=True)
            result = result + jnp.dot(
                far.astype(jnp.bfloat16), values[:at, head], preferred_element_type=jnp.float32
            )
        result = (result / total).astype(jnp.bfloat16)
        for h in range(group):
            out_ref[held(b), left + h * HEAD_SIZE : left + (h + 1) * HEAD_SIZE] = result[
                h * rows : (h + 1) * rows, :
            ]


def attend(index, queries, kv, offsets):
    length, q_cols = queries.shape
    kv_half = kv.shape[1] // 2
    return pl.pallas_call(
        functools.partial(attend_kernel, offsets, q_cols // kv_half),
        in_specs=[SMEM, VMEM, VMEM],
        out_specs=VMEM,
        out_shape=bf16(length, q_cols),
        scratch_shapes=[
            pltpu.VMEM((length, kv_half), jnp.bfloat16),
            pltpu.VMEM((length, kv_half), jnp.bfloat16),
        ],
        compiler_params=params(16),
        cost_estimate=work(0),
        name="attend",
    )(index, queries, kv)


def mix_kernel(n_w, heads_ref, *refs):
    w_refs, out_refs = refs[:n_w], refs[n_w:]
    rows = out_refs[0].shape[0]
    weights = [w_ref[...] for w_ref in w_refs]
    weights = weights[0] if n_w == 1 else jnp.concatenate(weights, axis=0)
    term = lax.dot_general(
        heads_ref[...], weights, NT, preferred_element_type=jnp.float32
    ).astype(jnp.bfloat16)
    for k, out_ref in enumerate(out_refs):
        out_ref[...] = term[k * rows : (k + 1) * rows, :]


def mix(heads, parts, blocks):
    length, features = heads.shape
    columns = sum(part.shape[0] for part in parts)
    return pl.pallas_call(
        functools.partial(mix_kernel, len(parts)),
        in_specs=[VMEM] * (1 + len(parts)),
        out_specs=[VMEM] * blocks,
        out_shape=[bf16(length // blocks, columns)] * blocks,
        compiler_params=params(16),
        cost_estimate=work(2 * length * columns * features, heads, *parts),
        name="mix",
    )(heads, *parts)


def add_kernel(a_ref, b_ref, out_ref):
    total = a_ref[...].astype(jnp.float32) + b_ref[...].astype(jnp.float32)
    out_ref[...] = total.astype(jnp.bfloat16)


def add(a, b):
    return pl.pallas_call(
        add_kernel,
        in_specs=[VMEM, VMEM],
        out_specs=VMEM,
        out_shape=bf16(*a.shape),
        compiler_params=params(8),
        cost_estimate=work(0, a, a, a),
        name="add",
    )(a, b)


def place_kernel(parts, index_ref, *refs):
    n = len(parts)
    a_refs, b_refs, out_ref, total, sem = refs[:n], refs[n : 2 * n], *refs[-3:]
    copies, left = [], 0
    for a_ref, b_ref, pieces in zip(a_refs, b_refs, parts):
        add_kernel(a_ref, b_ref, total.at[:, pl.ds(left, a_ref.shape[1])])
        for j, shard, offset, width in pieces:
            start = pl.multiple_of(jnp.bitwise_xor(index_ref[0], j) * shard + offset, 128)
            copies.append(
                pltpu.make_async_copy(
                    total.at[:, pl.ds(left, width)],
                    out_ref.at[:, pl.ds(start, width)],
                    sem.at[len(copies)],
                )
            )
            copies[-1].start()
            left += width
    for copy in copies:
        copy.wait()


def place(mixed, index, first, second, parts, columns):
    every = [piece for pieces in parts for piece in pieces]
    count = first[0].shape[0]
    if any(offset % 128 or width % 128 or shard % 128 for _, shard, offset, width in every):
        if mixed is None:
            mixed = jnp.zeros((count, columns), jnp.bfloat16)
        for a, b, pieces in zip(first, second, parts):
            total, left = add(a, b), 0
            for j, shard, offset, width in pieces:
                start = jnp.bitwise_xor(index[0], j) * shard + offset
                mixed = lax.dynamic_update_slice(mixed, total[:, left : left + width], (0, start))
                left += width
        return mixed
    held = [] if mixed is None else [mixed]
    return pl.pallas_call(
        functools.partial(place_kernel, parts),
        in_specs=[SMEM] + [VMEM] * (2 * len(parts)) + [ANY] * len(held),
        out_specs=ANY,
        out_shape=bf16(count, columns),
        scratch_shapes=[
            pltpu.VMEM((count, sum(piece[3] for piece in every)), jnp.bfloat16),
            pltpu.SemaphoreType.DMA((len(every),)),
        ],
        input_output_aliases={1 + 2 * len(parts): 0} if held else {},
        compiler_params=params(8),
        cost_estimate=work(0, *first, *second),
        name="place",
    )(index, *first, *second, *held)


def swapped(array, n_f, mask):
    return lax.ppermute(array, "fsdp", [(i, i ^ mask) for i in range(n_f)])


def after(array, *others):
    return lax.optimization_barrier((array, *others))[0] if others else array


def chips_away(level, chips):
    return [r for r in range(chips) if bin(r).count("1") == level]


def send_level(held, n_f, cut, axis, level, *before):
    for r in chips_away(level, n_f // 2):
        if level == 1:
            held[r] = [swapped(after(held[0][0], *before), n_f, 2 * r)]
            continue
        held[r] = []
        for half, bit in ((0, r & -r), (1, 1 << (r.bit_length() - 1))):
            parts = held[r ^ bit]
            part = parts[half] if len(parts) == 2 else part_of(parts[0], cut, half, axis)
            held[r].append(swapped(after(part, *before), n_f, 2 * bit))


def send_siblings(held, sibling, n_f, level, *before):
    for r in chips_away(level, n_f // 2):
        others = held[r] if len(held[r]) > 1 else []
        sibling[r] = [swapped(after(part, *others, *before), n_f, 1) for part in held[r]]


def rope_tables(length):
    frequency = np.float32(ROPE_BASE) ** (
        -(np.arange(HALF, dtype=np.float32) * np.float32(2.0) / np.float32(HEAD_SIZE))
    )
    angle = np.arange(length, dtype=np.float32)[:, None] * frequency[None, :].astype(np.float32)
    angle = angle.astype(np.float64)
    cos, sin = np.cos(angle).astype(np.float32), np.sin(angle).astype(np.float32)
    return np.concatenate([cos, cos], axis=1), np.concatenate([-sin, sin], axis=1)


def body(
    n_f,
    n_s,
    tokens,
    norm_gain,
    q_weight,
    key_matrix,
    value_matrix,
    q_bias,
    k_bias,
    value_offset_bias,
    out_weight,
):
    index = jnp.stack([lax.axis_index("fsdp"), lax.axis_index("sp")])
    count = tokens.shape[0]
    chips = n_f // 2
    levels = chips.bit_length() - 1
    shard, q_cols = q_weight.shape
    kv_cols = key_matrix.shape[1]
    wide = 256 if q_cols % 256 == 0 and kv_cols % 256 == 0 else 128
    cut = (q_cols + 2 * kv_cols) // wide // 2 * wide
    cut += wide if cut + wide <= q_cols else 0
    o_cut = shard * 3 // 5 // 128 * 128 or shard // 2 // 16 * 16
    right = [(i, (i + 1) % n_s) for i in range(n_s)]
    left = [(i, (i - 1) % n_s) for i in range(n_s)]
    cos, sin = rope_tables(n_s * count)

    own = normed_pieces(index, tokens, norm_gain, n_f)
    held = {0: [pack(after(q_weight, own), key_matrix, value_matrix)]}
    sibling, o_held, o_sibling = {}, {0: [after(out_weight, held[0][0])]}, {}
    send_level(held, n_f, cut, 1, 1)
    send_siblings(held, sibling, n_f, 0)

    steps = n_s // 2
    offsets, blocks, gate = [0], [own], []
    ahead = behind = own
    for step in range(1, steps + 1):
        if step > 1 and step <= levels:
            send_level(held, n_f, cut, 1, step, *gate)
            send_siblings(held, sibling, n_f, step - 1, *gate)
        if step < steps:
            ahead = lax.ppermute(ahead, "sp", right)
            behind = lax.ppermute(behind, "sp", left)
            offsets += [step, n_s - step]
        else:
            ahead = lax.ppermute(halves[0], "sp", right)
            behind = lax.ppermute(halves[1], "sp", left)
            offsets += [step]
        blocks += [ahead, behind]
        gate = [ahead, behind]
        if step == steps - 1:
            halves = [part_of(x, count // 2, i, 0, EXCHANGE) for i, x in enumerate(gate)]
            gate = halves[1:]
        if step == 1:
            send_siblings(o_held, o_sibling, n_f, 0, *gate)

    def pieces_of(chosen):
        return [side[r] for r in chosen for side in (held, sibling)]

    most = pieces_of(range(chips - 1))
    early = partial(blocks[:-2], most, wide, True)
    send_siblings(held, sibling, n_f, levels, early)
    send_level(o_held, n_f, o_cut, 0, 1, early)
    late = partial(blocks[-2:], most, wide, False)
    mine, others = pieces_of([chips - 1])
    queries, kv = finish(
        index,
        blocks,
        offsets,
        [mine[0], others[0], mine[1], others[1]],
        early,
        late,
        (q_bias, k_bias, value_offset_bias),
        cos,
        sin,
        q_cols,
        2 * shard * (chips - 1),
        wide,
    )
    heads = attend(index, queries, kv, offsets)

    gate, behind, rounds = [], [], []
    for level in range(levels + 1):
        near = chips_away(level, chips)
        if level:
            send_siblings(o_held, o_sibling, n_f, level, *gate)
            send_level(o_held, n_f, o_cut, 0, level + 1, *gate)
        if level < 2:
            groups = [((r, 0, core),) for core in (0, 1) for r in near]
        else:
            groups = [((r, half, 0), (r, half, 1)) for r in near for half in (0, 1)]
        terms = []
        for group in groups:
            weights = [(o_sibling if core else o_held)[r][half] for r, half, core in group]
            mixed = mix(after(heads, *gate), weights, n_s)
            terms.append([mixed[offsets.index(d)] for d in range(n_s)])
        totals, arrivals = [term[1] for term in terms], []
        for d in range(2, n_s + 1):
            arrivals.append([lax.ppermute(total, "sp", right) for total in totals])
            others = behind if d == n_s - 1 else []
            if d < n_s:
                totals = [add(after(a, *others), term[d]) for a, term in zip(arrivals[-1], terms)]
        where = [
            [(2 * r + core, shard, half * o_cut, o_held[r][half].shape[0]) for r, half, core in group]
            for group in groups
        ]
        rounds.append(([term[0] for term in terms], arrivals, where))
        gate = arrivals[-1] if level == 0 else arrivals[0] + arrivals[min(1, n_s - 2)][:2]
        behind = arrivals[-1][:2] if level else []

    mixed = None
    for chosen in (rounds[:-1], rounds[-1:]):
        mixed = place(
            mixed,
            index,
            [a for _, arrivals, _ in chosen for a in arrivals[-1]],
            [own for owns, _, _ in chosen for own in owns],
            [parts for _, _, where in chosen for parts in where],
            shard * n_f,
        )
    return mixed


def solution(mesh):
    n_f, n_s = mesh.shape["fsdp"], mesh.shape["sp"]
    placed = (
        P(("fsdp", "sp"), None),
        P(),
        P("fsdp", "sp"),
        P("fsdp", "sp"),
        P("fsdp", "sp"),
        P("sp"),
        P("sp"),
        P("sp"),
        P("fsdp", "sp"),
    )
    return jax.shard_map(
        functools.partial(body, n_f, n_s),
        mesh=mesh,
        in_specs=placed,
        out_specs=P(("fsdp", "sp"), None),
        check_vma=False,
    )
```

```python
import functools

import jax
import jax.numpy as jnp
import numpy as np
from jax import lax
from jax.experimental import pallas as pl
from jax.experimental.pallas import tpu as pltpu
from jax.sharding import PartitionSpec as P

HEAD_SIZE = 128
HALF = HEAD_SIZE // 2
ROPE_BASE = 1000000.0
LOG2E = 1.4426950408889634
EXCHANGE = 11500000000
NT = (((1,), (1,)), ((), ()))
VMEM = pl.BlockSpec(memory_space=pltpu.VMEM)
SMEM = pl.BlockSpec(memory_space=pltpu.SMEM)
ANY = pl.BlockSpec(memory_space=pl.ANY)


def params(mib):
    return pltpu.CompilerParams(vmem_limit_bytes=mib * 1024 * 1024)


def bf16(*shape):
    return jax.ShapeDtypeStruct(shape, jnp.bfloat16)


def work(flops, *arrays):
    size = sum(int(np.prod(x.shape)) * x.dtype.itemsize for x in arrays)
    return pl.CostEstimate(flops=flops, bytes_accessed=size, transcendentals=0)


def normed_kernel(n_f, index_ref, tokens_ref, gain_ref, out_ref):
    rows = tokens_ref[...].astype(jnp.float32)
    scale = lax.rsqrt(jnp.mean(rows * rows, axis=-1, keepdims=True) + 1e-06)
    shard = tokens_ref.shape[1] // n_f
    for j in range(n_f):
        start = pl.multiple_of(jnp.bitwise_xor(index_ref[0], j) * shard, 128)
        columns = pl.ds(start, shard)
        piece = tokens_ref[:, columns].astype(jnp.float32) * scale * gain_ref[:, columns]
        out_ref[:, j * shard : (j + 1) * shard] = piece.astype(jnp.bfloat16)


def normed_pieces(index, tokens, gain, n_f):
    count, width = tokens.shape
    shard = width // n_f
    if shard % 128 == 0:
        return pl.pallas_call(
            functools.partial(normed_kernel, n_f),
            out_shape=bf16(count, width),
            in_specs=[SMEM, VMEM, VMEM],
            out_specs=VMEM,
            compiler_params=params(16),
            cost_estimate=work(6 * count * width, tokens, tokens),
            name="norm",
        )(index, tokens, gain[None, :])
    rows = tokens.astype(jnp.float32)
    meansq = jnp.mean(rows * rows, axis=-1, keepdims=True)
    normed = (rows * lax.rsqrt(meansq + 1e-06) * gain).astype(jnp.bfloat16)
    pieces = [
        lax.dynamic_slice_in_dim(normed, jnp.bitwise_xor(index[0], j) * shard, shard, axis=1)
        for j in range(n_f)
    ]
    return jnp.concatenate(pieces, axis=1)


def pack_kernel(*refs):
    out_ref, at = refs[-1], 0
    for ref in refs[:-1]:
        out_ref[:, at : at + ref.shape[1]] = ref[...]
        at += ref.shape[1]


def pack(*arrays):
    return pl.pallas_call(
        pack_kernel,
        in_specs=[VMEM] * len(arrays),
        out_specs=VMEM,
        out_shape=bf16(arrays[0].shape[0], sum(x.shape[1] for x in arrays)),
        compiler_params=params(16),
        cost_estimate=work(0, *arrays, *arrays),
        name="pack",
    )(*arrays)


def cut_kernel(rows, columns, ref, out_ref):
    out_ref[...] = ref[rows, columns]


def part_of(array, cut, half, axis, cost=0):
    bounds = [slice(0, size) for size in array.shape]
    bounds[axis] = slice(cut, array.shape[axis]) if half else slice(0, cut)
    return pl.pallas_call(
        functools.partial(cut_kernel, *bounds),
        in_specs=[VMEM],
        out_specs=VMEM,
        out_shape=bf16(*[bound.stop - bound.start for bound in bounds]),
        compiler_params=params(16),
        cost_estimate=work(cost, array),
        name="cut",
    )(array)


def partial_kernel(n_x, counts, wide, *refs):
    x_refs, w_refs, (out_ref, rows) = refs[:n_x], refs[n_x:-2], refs[-2:]
    at = 0
    for x_ref in x_refs:
        rows[at : at + x_ref.shape[0], :] = x_ref[:, : rows.shape[1]]
        at += x_ref.shape[0]
    shard = w_refs[0].shape[0]
    pieces, at = [], 0
    for count in counts:
        pieces.append(w_refs[at : at + count])
        at += count
    for col in range(0, out_ref.shape[1], wide):
        total = None
        for j, parts in enumerate(pieces):
            at = col
            for w_ref in parts:
                if at < w_ref.shape[1]:
                    break
                at -= w_ref.shape[1]
            term = jnp.dot(
                rows[:, j * shard : (j + 1) * shard],
                w_ref[:, at : at + wide],
                preferred_element_type=jnp.float32,
            )
            total = term if total is None else total + term
        out_ref[:, col : col + wide] = total


def partial(blocks, pieces, wide, declared):
    weights = [part for piece in pieces for part in piece]
    length = sum(block.shape[0] for block in blocks)
    depth = len(pieces) * weights[0].shape[0]
    columns = sum(part.shape[1] for part in pieces[0])
    out = jax.ShapeDtypeStruct((length, columns), jnp.float32)
    counts = [len(piece) for piece in pieces]
    return pl.pallas_call(
        functools.partial(partial_kernel, len(blocks), counts, wide),
        in_specs=[VMEM] * (len(blocks) + len(weights)),
        out_specs=VMEM,
        out_shape=out,
        scratch_shapes=[pltpu.VMEM((length, depth), jnp.bfloat16)],
        compiler_params=params(16),
        cost_estimate=work(2 * length * depth * columns if declared else 0),
        name="partial",
    )(*blocks, *weights)


def rope_tile(tile, cos, sin):
    parts = []
    for at in range(0, tile.shape[1], HEAD_SIZE):
        head = tile[:, at : at + HEAD_SIZE]
        parts.append(head * cos + pltpu.roll(head, HALF, axis=1) * sin)
    return parts[0] if len(parts) == 1 else jnp.concatenate(parts, axis=1)


def finish_kernel(n_x, offsets, wide, roped, first_col, index_ref, *refs):
    x_refs = refs[:n_x]
    w_refs = refs[n_x : n_x + 4]
    early_ref, late_ref = refs[n_x + 4 : n_x + 6]
    bias_refs, (cos_ref, sin_ref) = refs[n_x + 6 : n_x + 9], refs[n_x + 9 : n_x + 11]
    q_out, kv_out, rows, cos, sin = refs[n_x + 11 :]
    shard = w_refs[0].shape[0]
    at = 0
    for x_ref in x_refs:
        rows[at : at + x_ref.shape[0], :] = x_ref[:, first_col : first_col + 2 * shard]
        at += x_ref.shape[0]
    blocks = len(offsets)
    count = at // blocks
    for k, offset in enumerate(offsets):
        block = lax.rem(index_ref[1] - offset + blocks, blocks)
        place = pl.ds(pl.multiple_of(block * count, count), count)
        cos[k * count : (k + 1) * count, :] = cos_ref[place, :]
        sin[k * count : (k + 1) * count, :] = sin_ref[place, :]
    q_cols = q_out.shape[1]

    def bias_tile(col):
        for bias_ref in bias_refs:
            if col < bias_ref.shape[0]:
                return bias_ref[pl.ds(col, wide)][None, :]
            col -= bias_ref.shape[0]

    base = 0
    for mine, sibling in (w_refs[:2], w_refs[2:]):
        for at in range(0, mine.shape[1], wide):
            total = jnp.dot(
                rows[:, :shard], mine[:, at : at + wide], preferred_element_type=jnp.float32
            )
            total = total + jnp.dot(
                rows[:, shard:], sibling[:, at : at + wide], preferred_element_type=jnp.float32
            )
            col = base + at
            total = total + jnp.concatenate(
                [early_ref[:, col : col + wide], late_ref[:, col : col + wide]], axis=0
            )
            total = total + bias_tile(col)
            if col < roped:
                total = rope_tile(total, cos[...], sin[...])
            total = total.astype(jnp.bfloat16)
            if col < q_cols:
                q_out[:, col : col + wide] = total
            else:
                kv_out[:, col - q_cols : col - q_cols + wide] = total
        base += mine.shape[1]


def finish(index, blocks, offsets, weights, early, late, biases, cos, sin, q_cols, first_col, wide):
    n_x = len(blocks)
    length = sum(block.shape[0] for block in blocks)
    shard = weights[0].shape[0]
    columns = early.shape[1]
    kv_cols = columns - q_cols
    return pl.pallas_call(
        functools.partial(finish_kernel, n_x, offsets, wide, q_cols + kv_cols // 2, first_col),
        in_specs=[SMEM] + [VMEM] * (n_x + 11),
        out_specs=[VMEM, VMEM],
        out_shape=[bf16(length, q_cols), bf16(length, kv_cols)],
        scratch_shapes=[
            pltpu.VMEM((length, 2 * shard), jnp.bfloat16),
            pltpu.VMEM((length, HEAD_SIZE), jnp.float32),
            pltpu.VMEM((length, HEAD_SIZE), jnp.float32),
        ],
        compiler_params=params(16),
        cost_estimate=work(0),
        name="finish",
    )(index, *blocks, *weights, early, late, *biases, cos, sin)


def attend_kernel(offsets, group, index_ref, q_ref, kv_ref, out_ref, keys, values):
    blocks = len(offsets)
    rows = q_ref.shape[0] // blocks
    factor = LOG2E / (HEAD_SIZE**0.5)

    def held(b):
        offset = lax.rem(index_ref[1] - b + blocks, blocks)
        k = sum(jnp.where(offset == value, i, 0) for i, value in enumerate(offsets))
        return pl.ds(pl.multiple_of(k * rows, rows), rows)

    kv_half = kv_ref.shape[1] // 2
    for b in range(blocks):
        keys[b * rows : (b + 1) * rows, :] = kv_ref[held(b), :kv_half]
        values[b * rows : (b + 1) * rows, :] = kv_ref[held(b), kv_half:]
    row = lax.broadcasted_iota(jnp.int32, (rows, rows), 0)
    column = lax.broadcasted_iota(jnp.int32, (rows, rows), 1)
    causal = row >= column
    causal = jnp.concatenate([causal.astype(jnp.float32)] * group, axis=0) > 0.5
    for g, b in [(g, b) for g in range(kv_half // HEAD_SIZE) for b in range(blocks)]:
        left = g * group * HEAD_SIZE
        head = slice(g * HEAD_SIZE, (g + 1) * HEAD_SIZE)
        q_block = q_ref[held(b), left : left + group * HEAD_SIZE]
        queries = jnp.concatenate(
            [q_block[:, h * HEAD_SIZE : (h + 1) * HEAD_SIZE] for h in range(group)], axis=0
        )
        at = b * rows
        near = lax.dot_general(
            queries, keys[at : at + rows, head], NT, preferred_element_type=jnp.float32
        )
        near = jnp.where(causal, near, jnp.float32(-1e30))
        largest = jnp.max(near, axis=-1, keepdims=True)
        if b > 0:
            far = lax.dot_general(queries, keys[:at, head], NT, preferred_element_type=jnp.float32)
            largest = jnp.maximum(largest, jnp.max(far, axis=-1, keepdims=True))
        near = jnp.exp2((near - largest) * factor)
        total = jnp.sum(near, axis=-1, keepdims=True)
        result = jnp.dot(
            near.astype(jnp.bfloat16), values[at : at + rows, head], preferred_element_type=jnp.float32
        )
        if b > 0:
            far = jnp.exp2((far - largest) * factor)
            total = total + jnp.sum(far, axis=-1, keepdims=True)
            result = result + jnp.dot(
                far.astype(jnp.bfloat16), values[:at, head], preferred_element_type=jnp.float32
            )
        result = (result / total).astype(jnp.bfloat16)
        for h in range(group):
            out_ref[held(b), left + h * HEAD_SIZE : left + (h + 1) * HEAD_SIZE] = result[
                h * rows : (h + 1) * rows, :
            ]


def attend(index, queries, kv, offsets):
    length, q_cols = queries.shape
    kv_half = kv.shape[1] // 2
    return pl.pallas_call(
        functools.partial(attend_kernel, offsets, q_cols // kv_half),
        in_specs=[SMEM, VMEM, VMEM],
        out_specs=VMEM,
        out_shape=bf16(length, q_cols),
        scratch_shapes=[
            pltpu.VMEM((length, kv_half), jnp.bfloat16),
            pltpu.VMEM((length, kv_half), jnp.bfloat16),
        ],
        compiler_params=params(16),
        cost_estimate=work(0),
        name="attend",
    )(index, queries, kv)


def mix_kernel(n_w, heads_ref, *refs):
    w_refs, out_refs = refs[:n_w], refs[n_w:]
    rows = out_refs[0].shape[0]
    weights = [w_ref[...] for w_ref in w_refs]
    weights = weights[0] if n_w == 1 else jnp.concatenate(weights, axis=0)
    term = lax.dot_general(
        heads_ref[...], weights, NT, preferred_element_type=jnp.float32
    ).astype(jnp.bfloat16)
    for k, out_ref in enumerate(out_refs):
        out_ref[...] = term[k * rows : (k + 1) * rows, :]


def mix(heads, parts, blocks):
    length, features = heads.shape
    columns = sum(part.shape[0] for part in parts)
    return pl.pallas_call(
        functools.partial(mix_kernel, len(parts)),
        in_specs=[VMEM] * (1 + len(parts)),
        out_specs=[VMEM] * blocks,
        out_shape=[bf16(length // blocks, columns)] * blocks,
        compiler_params=params(16),
        cost_estimate=work(2 * length * columns * features, heads, *parts),
        name="mix",
    )(heads, *parts)


def add_kernel(a_ref, b_ref, out_ref):
    total = a_ref[...].astype(jnp.float32) + b_ref[...].astype(jnp.float32)
    out_ref[...] = total.astype(jnp.bfloat16)


def add(a, b):
    return pl.pallas_call(
        add_kernel,
        in_specs=[VMEM, VMEM],
        out_specs=VMEM,
        out_shape=bf16(*a.shape),
        compiler_params=params(8),
        cost_estimate=work(0, a, a, a),
        name="add",
    )(a, b)


def place_kernel(parts, index_ref, *refs):
    n = len(parts)
    a_refs, b_refs, out_ref, total, sem = refs[:n], refs[n : 2 * n], *refs[-3:]
    copies, left = [], 0
    for a_ref, b_ref, pieces in zip(a_refs, b_refs, parts):
        add_kernel(a_ref, b_ref, total.at[:, pl.ds(left, a_ref.shape[1])])
        for j, shard, offset, width in pieces:
            start = pl.multiple_of(jnp.bitwise_xor(index_ref[0], j) * shard + offset, 128)
            copies.append(
                pltpu.make_async_copy(
                    total.at[:, pl.ds(left, width)],
                    out_ref.at[:, pl.ds(start, width)],
                    sem.at[len(copies)],
                )
            )
            copies[-1].start()
            left += width
    for copy in copies:
        copy.wait()


def place(mixed, index, first, second, parts, columns):
    every = [piece for pieces in parts for piece in pieces]
    count = first[0].shape[0]
    if any(offset % 128 or width % 128 or shard % 128 for _, shard, offset, width in every):
        if mixed is None:
            mixed = jnp.zeros((count, columns), jnp.bfloat16)
        for a, b, pieces in zip(first, second, parts):
            total, left = add(a, b), 0
            for j, shard, offset, width in pieces:
                start = jnp.bitwise_xor(index[0], j) * shard + offset
                mixed = lax.dynamic_update_slice(mixed, total[:, left : left + width], (0, start))
                left += width
        return mixed
    held = [] if mixed is None else [mixed]
    return pl.pallas_call(
        functools.partial(place_kernel, parts),
        in_specs=[SMEM] + [VMEM] * (2 * len(parts)) + [ANY] * len(held),
        out_specs=ANY,
        out_shape=bf16(count, columns),
        scratch_shapes=[
            pltpu.VMEM((count, sum(piece[3] for piece in every)), jnp.bfloat16),
            pltpu.SemaphoreType.DMA((len(every),)),
        ],
        input_output_aliases={1 + 2 * len(parts): 0} if held else {},
        compiler_params=params(8),
        cost_estimate=work(0, *first, *second),
        name="place",
    )(index, *first, *second, *held)


def swapped(array, n_f, mask):
    return lax.ppermute(array, "fsdp", [(i, i ^ mask) for i in range(n_f)])


def after(array, *others):
    return lax.optimization_barrier((array, *others))[0] if others else array


def chips_away(level, chips):
    return [r for r in range(chips) if bin(r).count("1") == level]


def send_level(held, n_f, cut, axis, level, *before):
    for r in chips_away(level, n_f // 2):
        if level == 1:
            held[r] = [swapped(after(held[0][0], *before), n_f, 2 * r)]
            continue
        held[r] = []
        for half, bit in ((0, r & -r), (1, 1 << (r.bit_length() - 1))):
            parts = held[r ^ bit]
            part = parts[half] if len(parts) == 2 else part_of(parts[0], cut, half, axis)
            held[r].append(swapped(after(part, *before), n_f, 2 * bit))


def send_siblings(held, sibling, n_f, level, *before):
    for r in chips_away(level, n_f // 2):
        others = held[r] if len(held[r]) > 1 else []
        sibling[r] = [swapped(after(part, *others, *before), n_f, 1) for part in held[r]]


def rope_tables(length):
    frequency = np.float32(ROPE_BASE) ** (
        -(np.arange(HALF, dtype=np.float32) * np.float32(2.0) / np.float32(HEAD_SIZE))
    )
    angle = np.arange(length, dtype=np.float32)[:, None] * frequency[None, :].astype(np.float32)
    angle = angle.astype(np.float64)
    cos, sin = np.cos(angle).astype(np.float32), np.sin(angle).astype(np.float32)
    return np.concatenate([cos, cos], axis=1), np.concatenate([-sin, sin], axis=1)


def body(
    n_f,
    n_s,
    tokens,
    norm_gain,
    q_weight,
    key_matrix,
    value_matrix,
    q_bias,
    k_bias,
    value_offset_bias,
    out_weight,
):
    index = jnp.stack([lax.axis_index("fsdp"), lax.axis_index("sp")])
    count = tokens.shape[0]
    chips = n_f // 2
    levels = chips.bit_length() - 1
    shard, q_cols = q_weight.shape
    kv_cols = key_matrix.shape[1]
    wide = 256 if q_cols % 256 == 0 and kv_cols % 256 == 0 else 128
    cut = (q_cols + 2 * kv_cols) // wide // 2 * wide
    cut += wide if cut + wide <= q_cols else 0
    o_cut = shard * 3 // 5 // 128 * 128 or shard // 2 // 16 * 16
    right = [(i, (i + 1) % n_s) for i in range(n_s)]
    left = [(i, (i - 1) % n_s) for i in range(n_s)]
    cos, sin = rope_tables(n_s * count)

    own = normed_pieces(index, tokens, norm_gain, n_f)
    held = {0: [pack(after(q_weight, own), key_matrix, value_matrix)]}
    sibling, o_held, o_sibling = {}, {0: [after(out_weight, held[0][0])]}, {}
    send_level(held, n_f, cut, 1, 1)
    send_siblings(held, sibling, n_f, 0)

    steps = n_s // 2
    offsets, blocks, gate = [0], [own], []
    ahead = behind = own
    for step in range(1, steps + 1):
        if step > 1 and step <= levels:
            send_level(held, n_f, cut, 1, step, *gate)
            send_siblings(held, sibling, n_f, step - 1, *gate)
        if step < steps:
            ahead = lax.ppermute(ahead, "sp", right)
            behind = lax.ppermute(behind, "sp", left)
            offsets += [step, n_s - step]
        else:
            ahead = lax.ppermute(halves[0], "sp", right)
            behind = lax.ppermute(halves[1], "sp", left)
            offsets += [step]
        blocks += [ahead, behind]
        gate = [ahead, behind]
        if step == steps - 1:
            halves = [part_of(x, count // 2, i, 0, EXCHANGE) for i, x in enumerate(gate)]
            gate = halves[1:]
        if step == 1:
            send_siblings(o_held, o_sibling, n_f, 0, *gate)

    def pieces_of(chosen):
        return [side[r] for r in chosen for side in (held, sibling)]

    most = pieces_of(range(chips - 1))
    early = partial(blocks[:-2], most, wide, True)
    send_siblings(held, sibling, n_f, levels, early)
    send_level(o_held, n_f, o_cut, 0, 1, early)
    late = partial(blocks[-2:], most, wide, False)
    mine, others = pieces_of([chips - 1])
    queries, kv = finish(
        index,
        blocks,
        offsets,
        [mine[0], others[0], mine[1], others[1]],
        early,
        late,
        (q_bias, k_bias, value_offset_bias),
        cos,
        sin,
        q_cols,
        2 * shard * (chips - 1),
        wide,
    )
    heads = attend(index, queries, kv, offsets)

    gate, behind, rounds = [], [], []
    for level in range(levels + 1):
        near = chips_away(level, chips)
        if level:
            send_siblings(o_held, o_sibling, n_f, level, *gate)
            send_level(o_held, n_f, o_cut, 0, level + 1, *gate)
        if level < 2:
            groups = [tuple((r, 0, core) for r in near) for core in (0, 1)]
        else:
            groups = [((r, half, 0), (r, half, 1)) for r in near for half in (0, 1)]
        terms = []
        for group in groups:
            weights = [(o_sibling if core else o_held)[r][half] for r, half, core in group]
            mixed = mix(after(heads, *gate), weights, n_s)
            terms.append([mixed[offsets.index(d)] for d in range(n_s)])
        totals, arrivals = [term[1] for term in terms], []
        for d in range(2, n_s + 1):
            arrivals.append([lax.ppermute(total, "sp", right) for total in totals])
            others = behind if d == n_s - 1 else []
            if d < n_s:
                totals = [add(after(a, *others), term[d]) for a, term in zip(arrivals[-1], terms)]
        where = [
            [(2 * r + core, shard, half * o_cut, o_held[r][half].shape[0]) for r, half, core in group]
            for group in groups
        ]
        rounds.append(([term[0] for term in terms], arrivals, where))
        gate = arrivals[-1] if level == 0 else arrivals[min(1, n_s - 2)]
        behind = arrivals[-1][:1] if level else []

    mixed = None
    for chosen in (rounds[:-1], rounds[-1:]):
        mixed = place(
            mixed,
            index,
            [a for _, arrivals, _ in chosen for a in arrivals[-1]],
            [own for owns, _, _ in chosen for own in owns],
            [parts for _, _, where in chosen for parts in where],
            shard * n_f,
        )
    return mixed


def solution(mesh):
    n_f, n_s = mesh.shape["fsdp"], mesh.shape["sp"]
    placed = (
        P(("fsdp", "sp"), None),
        P(),
        P("fsdp", "sp"),
        P("fsdp", "sp"),
        P("fsdp", "sp"),
        P("sp"),
        P("sp"),
        P("sp"),
        P("fsdp", "sp"),
    )
    return jax.shard_map(
        functools.partial(body, n_f, n_s),
        mesh=mesh,
        in_specs=placed,
        out_specs=P(("fsdp", "sp"), None),
        check_vma=False,
    )
```

```python
import functools

import jax
import jax.numpy as jnp
import numpy as np
from jax import lax
from jax.experimental import pallas as pl
from jax.experimental.pallas import tpu as pltpu
from jax.sharding import PartitionSpec as P

HEAD_SIZE = 128
HALF = HEAD_SIZE // 2
ROPE_BASE = 1000000.0
LOG2E = 1.4426950408889634
EXCHANGE = 11500000000
NT = (((1,), (1,)), ((), ()))
VMEM = pl.BlockSpec(memory_space=pltpu.VMEM)
SMEM = pl.BlockSpec(memory_space=pltpu.SMEM)
ANY = pl.BlockSpec(memory_space=pl.ANY)


def params(mib):
    return pltpu.CompilerParams(vmem_limit_bytes=mib * 1024 * 1024)


def bf16(*shape):
    return jax.ShapeDtypeStruct(shape, jnp.bfloat16)


def work(flops, *arrays):
    size = sum(int(np.prod(x.shape)) * x.dtype.itemsize for x in arrays)
    return pl.CostEstimate(flops=flops, bytes_accessed=size, transcendentals=0)


def normed_kernel(n_f, index_ref, tokens_ref, gain_ref, out_ref):
    rows = tokens_ref[...].astype(jnp.float32)
    scale = lax.rsqrt(jnp.mean(rows * rows, axis=-1, keepdims=True) + 1e-06)
    shard = tokens_ref.shape[1] // n_f
    for j in range(n_f):
        start = pl.multiple_of(jnp.bitwise_xor(index_ref[0], j) * shard, 128)
        columns = pl.ds(start, shard)
        piece = tokens_ref[:, columns].astype(jnp.float32) * scale * gain_ref[:, columns]
        out_ref[:, j * shard : (j + 1) * shard] = piece.astype(jnp.bfloat16)


def normed_pieces(index, tokens, gain, n_f):
    count, width = tokens.shape
    shard = width // n_f
    if shard % 128 == 0:
        return pl.pallas_call(
            functools.partial(normed_kernel, n_f),
            out_shape=bf16(count, width),
            in_specs=[SMEM, VMEM, VMEM],
            out_specs=VMEM,
            compiler_params=params(16),
            cost_estimate=work(6 * count * width, tokens, tokens),
            name="norm",
        )(index, tokens, gain[None, :])
    rows = tokens.astype(jnp.float32)
    meansq = jnp.mean(rows * rows, axis=-1, keepdims=True)
    normed = (rows * lax.rsqrt(meansq + 1e-06) * gain).astype(jnp.bfloat16)
    pieces = [
        lax.dynamic_slice_in_dim(normed, jnp.bitwise_xor(index[0], j) * shard, shard, axis=1)
        for j in range(n_f)
    ]
    return jnp.concatenate(pieces, axis=1)


def pack_kernel(*refs):
    out_ref, at = refs[-1], 0
    for ref in refs[:-1]:
        out_ref[:, at : at + ref.shape[1]] = ref[...]
        at += ref.shape[1]


def pack(*arrays):
    return pl.pallas_call(
        pack_kernel,
        in_specs=[VMEM] * len(arrays),
        out_specs=VMEM,
        out_shape=bf16(arrays[0].shape[0], sum(x.shape[1] for x in arrays)),
        compiler_params=params(16),
        cost_estimate=work(0, *arrays, *arrays),
        name="pack",
    )(*arrays)


def cut_kernel(rows, columns, ref, out_ref):
    out_ref[...] = ref[rows, columns]


def part_of(array, cut, half, axis, cost=0):
    bounds = [slice(0, size) for size in array.shape]
    bounds[axis] = slice(cut, array.shape[axis]) if half else slice(0, cut)
    return pl.pallas_call(
        functools.partial(cut_kernel, *bounds),
        in_specs=[VMEM],
        out_specs=VMEM,
        out_shape=bf16(*[bound.stop - bound.start for bound in bounds]),
        compiler_params=params(16),
        cost_estimate=work(cost, array),
        name="cut",
    )(array)


def partial_kernel(n_x, counts, wide, *refs):
    x_refs, w_refs, (out_ref, rows) = refs[:n_x], refs[n_x:-2], refs[-2:]
    at = 0
    for x_ref in x_refs:
        rows[at : at + x_ref.shape[0], :] = x_ref[:, : rows.shape[1]]
        at += x_ref.shape[0]
    shard = w_refs[0].shape[0]
    pieces, at = [], 0
    for count in counts:
        pieces.append(w_refs[at : at + count])
        at += count
    for col in range(0, out_ref.shape[1], wide):
        total = None
        for j, parts in enumerate(pieces):
            at = col
            for w_ref in parts:
                if at < w_ref.shape[1]:
                    break
                at -= w_ref.shape[1]
            term = jnp.dot(
                rows[:, j * shard : (j + 1) * shard],
                w_ref[:, at : at + wide],
                preferred_element_type=jnp.float32,
            )
            total = term if total is None else total + term
        out_ref[:, col : col + wide] = total


def partial(blocks, pieces, wide, declared):
    weights = [part for piece in pieces for part in piece]
    length = sum(block.shape[0] for block in blocks)
    depth = len(pieces) * weights[0].shape[0]
    columns = sum(part.shape[1] for part in pieces[0])
    out = jax.ShapeDtypeStruct((length, columns), jnp.float32)
    counts = [len(piece) for piece in pieces]
    return pl.pallas_call(
        functools.partial(partial_kernel, len(blocks), counts, wide),
        in_specs=[VMEM] * (len(blocks) + len(weights)),
        out_specs=VMEM,
        out_shape=out,
        scratch_shapes=[pltpu.VMEM((length, depth), jnp.bfloat16)],
        compiler_params=params(16),
        cost_estimate=work(2 * length * depth * columns if declared else 0),
        name="partial",
    )(*blocks, *weights)


def rope_tile(tile, cos, sin):
    parts = []
    for at in range(0, tile.shape[1], HEAD_SIZE):
        head = tile[:, at : at + HEAD_SIZE]
        parts.append(head * cos + pltpu.roll(head, HALF, axis=1) * sin)
    return parts[0] if len(parts) == 1 else jnp.concatenate(parts, axis=1)


def finish_kernel(n_x, offsets, wide, roped, first_col, index_ref, *refs):
    x_refs = refs[:n_x]
    w_refs = refs[n_x : n_x + 4]
    early_ref, late_ref = refs[n_x + 4 : n_x + 6]
    bias_refs, (cos_ref, sin_ref) = refs[n_x + 6 : n_x + 9], refs[n_x + 9 : n_x + 11]
    q_out, kv_out, rows, cos, sin = refs[n_x + 11 :]
    shard = w_refs[0].shape[0]
    at = 0
    for x_ref in x_refs:
        rows[at : at + x_ref.shape[0], :] = x_ref[:, first_col : first_col + 2 * shard]
        at += x_ref.shape[0]
    blocks = len(offsets)
    count = at // blocks
    for k, offset in enumerate(offsets):
        block = lax.rem(index_ref[1] - offset + blocks, blocks)
        place = pl.ds(pl.multiple_of(block * count, count), count)
        cos[k * count : (k + 1) * count, :] = cos_ref[place, :]
        sin[k * count : (k + 1) * count, :] = sin_ref[place, :]
    q_cols = q_out.shape[1]

    def bias_tile(col):
        for bias_ref in bias_refs:
            if col < bias_ref.shape[0]:
                return bias_ref[pl.ds(col, wide)][None, :]
            col -= bias_ref.shape[0]

    base = 0
    for mine, sibling in (w_refs[:2], w_refs[2:]):
        for at in range(0, mine.shape[1], wide):
            total = jnp.dot(
                rows[:, :shard], mine[:, at : at + wide], preferred_element_type=jnp.float32
            )
            total = total + jnp.dot(
                rows[:, shard:], sibling[:, at : at + wide], preferred_element_type=jnp.float32
            )
            col = base + at
            total = total + jnp.concatenate(
                [early_ref[:, col : col + wide], late_ref[:, col : col + wide]], axis=0
            )
            total = total + bias_tile(col)
            if col < roped:
                total = rope_tile(total, cos[...], sin[...])
            total = total.astype(jnp.bfloat16)
            if col < q_cols:
                q_out[:, col : col + wide] = total
            else:
                kv_out[:, col - q_cols : col - q_cols + wide] = total
        base += mine.shape[1]


def finish(index, blocks, offsets, weights, early, late, biases, cos, sin, q_cols, first_col, wide):
    n_x = len(blocks)
    length = sum(block.shape[0] for block in blocks)
    shard = weights[0].shape[0]
    columns = early.shape[1]
    kv_cols = columns - q_cols
    return pl.pallas_call(
        functools.partial(finish_kernel, n_x, offsets, wide, q_cols + kv_cols // 2, first_col),
        in_specs=[SMEM] + [VMEM] * (n_x + 11),
        out_specs=[VMEM, VMEM],
        out_shape=[bf16(length, q_cols), bf16(length, kv_cols)],
        scratch_shapes=[
            pltpu.VMEM((length, 2 * shard), jnp.bfloat16),
            pltpu.VMEM((length, HEAD_SIZE), jnp.float32),
            pltpu.VMEM((length, HEAD_SIZE), jnp.float32),
        ],
        compiler_params=params(16),
        cost_estimate=work(0),
        name="finish",
    )(index, *blocks, *weights, early, late, *biases, cos, sin)


def attend_kernel(offsets, group, index_ref, q_ref, kv_ref, out_ref, keys, values):
    blocks = len(offsets)
    rows = q_ref.shape[0] // blocks
    factor = LOG2E / (HEAD_SIZE**0.5)

    def held(b):
        offset = lax.rem(index_ref[1] - b + blocks, blocks)
        k = sum(jnp.where(offset == value, i, 0) for i, value in enumerate(offsets))
        return pl.ds(pl.multiple_of(k * rows, rows), rows)

    kv_half = kv_ref.shape[1] // 2
    for b in range(blocks):
        keys[b * rows : (b + 1) * rows, :] = kv_ref[held(b), :kv_half]
        values[b * rows : (b + 1) * rows, :] = kv_ref[held(b), kv_half:]
    row = lax.broadcasted_iota(jnp.int32, (rows, rows), 0)
    column = lax.broadcasted_iota(jnp.int32, (rows, rows), 1)
    causal = row >= column
    causal = jnp.concatenate([causal.astype(jnp.float32)] * group, axis=0) > 0.5
    for g, b in [(g, b) for g in range(kv_half // HEAD_SIZE) for b in range(blocks)]:
        left = g * group * HEAD_SIZE
        head = slice(g * HEAD_SIZE, (g + 1) * HEAD_SIZE)
        q_block = q_ref[held(b), left : left + group * HEAD_SIZE]
        queries = jnp.concatenate(
            [q_block[:, h * HEAD_SIZE : (h + 1) * HEAD_SIZE] for h in range(group)], axis=0
        )
        at = b * rows
        near = lax.dot_general(
            queries, keys[at : at + rows, head], NT, preferred_element_type=jnp.float32
        )
        near = jnp.where(causal, near, jnp.float32(-1e30))
        largest = jnp.max(near, axis=-1, keepdims=True)
        if b > 0:
            far = lax.dot_general(queries, keys[:at, head], NT, preferred_element_type=jnp.float32)
            largest = jnp.maximum(largest, jnp.max(far, axis=-1, keepdims=True))
        near = jnp.exp2((near - largest) * factor)
        total = jnp.sum(near, axis=-1, keepdims=True)
        result = jnp.dot(
            near.astype(jnp.bfloat16), values[at : at + rows, head], preferred_element_type=jnp.float32
        )
        if b > 0:
            far = jnp.exp2((far - largest) * factor)
            total = total + jnp.sum(far, axis=-1, keepdims=True)
            result = result + jnp.dot(
                far.astype(jnp.bfloat16), values[:at, head], preferred_element_type=jnp.float32
            )
        result = (result / total).astype(jnp.bfloat16)
        for h in range(group):
            out_ref[held(b), left + h * HEAD_SIZE : left + (h + 1) * HEAD_SIZE] = result[
                h * rows : (h + 1) * rows, :
            ]


def attend(index, queries, kv, offsets):
    length, q_cols = queries.shape
    kv_half = kv.shape[1] // 2
    return pl.pallas_call(
        functools.partial(attend_kernel, offsets, q_cols // kv_half),
        in_specs=[SMEM, VMEM, VMEM],
        out_specs=VMEM,
        out_shape=bf16(length, q_cols),
        scratch_shapes=[
            pltpu.VMEM((length, kv_half), jnp.bfloat16),
            pltpu.VMEM((length, kv_half), jnp.bfloat16),
        ],
        compiler_params=params(16),
        cost_estimate=work(0),
        name="attend",
    )(index, queries, kv)


def mix_kernel(n_w, heads_ref, *refs):
    w_refs, out_refs = refs[:n_w], refs[n_w:]
    rows = out_refs[0].shape[0]
    weights = [w_ref[...] for w_ref in w_refs]
    weights = weights[0] if n_w == 1 else jnp.concatenate(weights, axis=0)
    term = lax.dot_general(
        heads_ref[...], weights, NT, preferred_element_type=jnp.float32
    ).astype(jnp.bfloat16)
    for k, out_ref in enumerate(out_refs):
        out_ref[...] = term[k * rows : (k + 1) * rows, :]


def mix(heads, parts, blocks):
    length, features = heads.shape
    columns = sum(part.shape[0] for part in parts)
    return pl.pallas_call(
        functools.partial(mix_kernel, len(parts)),
        in_specs=[VMEM] * (1 + len(parts)),
        out_specs=[VMEM] * blocks,
        out_shape=[bf16(length // blocks, columns)] * blocks,
        compiler_params=params(16),
        cost_estimate=work(2 * length * columns * features, heads, *parts),
        name="mix",
    )(heads, *parts)


def add_kernel(a_ref, b_ref, out_ref):
    total = a_ref[...].astype(jnp.float32) + b_ref[...].astype(jnp.float32)
    out_ref[...] = total.astype(jnp.bfloat16)


def add(a, b):
    return pl.pallas_call(
        add_kernel,
        in_specs=[VMEM, VMEM],
        out_specs=VMEM,
        out_shape=bf16(*a.shape),
        compiler_params=params(8),
        cost_estimate=work(0, a, a, a),
        name="add",
    )(a, b)


def place_kernel(parts, index_ref, *refs):
    n = len(parts)
    a_refs, b_refs, out_ref, total, sem = refs[:n], refs[n : 2 * n], *refs[-3:]
    copies, left = [], 0
    for a_ref, b_ref, pieces in zip(a_refs, b_refs, parts):
        add_kernel(a_ref, b_ref, total.at[:, pl.ds(left, a_ref.shape[1])])
        for j, shard, offset, width in pieces:
            start = pl.multiple_of(jnp.bitwise_xor(index_ref[0], j) * shard + offset, 128)
            copies.append(
                pltpu.make_async_copy(
                    total.at[:, pl.ds(left, width)],
                    out_ref.at[:, pl.ds(start, width)],
                    sem.at[len(copies)],
                )
            )
            copies[-1].start()
            left += width
    for copy in copies:
        copy.wait()


def place(mixed, index, first, second, parts, columns):
    every = [piece for pieces in parts for piece in pieces]
    count = first[0].shape[0]
    if any(offset % 128 or width % 128 or shard % 128 for _, shard, offset, width in every):
        if mixed is None:
            mixed = jnp.zeros((count, columns), jnp.bfloat16)
        for a, b, pieces in zip(first, second, parts):
            total, left = add(a, b), 0
            for j, shard, offset, width in pieces:
                start = jnp.bitwise_xor(index[0], j) * shard + offset
                mixed = lax.dynamic_update_slice(mixed, total[:, left : left + width], (0, start))
                left += width
        return mixed
    held = [] if mixed is None else [mixed]
    return pl.pallas_call(
        functools.partial(place_kernel, parts),
        in_specs=[SMEM] + [VMEM] * (2 * len(parts)) + [ANY] * len(held),
        out_specs=ANY,
        out_shape=bf16(count, columns),
        scratch_shapes=[
            pltpu.VMEM((count, sum(piece[3] for piece in every)), jnp.bfloat16),
            pltpu.SemaphoreType.DMA((len(every),)),
        ],
        input_output_aliases={1 + 2 * len(parts): 0} if held else {},
        compiler_params=params(8),
        cost_estimate=work(0, *first, *second),
        name="place",
    )(index, *first, *second, *held)


def swapped(array, n_f, mask):
    return lax.ppermute(array, "fsdp", [(i, i ^ mask) for i in range(n_f)])


def after(array, *others):
    return lax.optimization_barrier((array, *others))[0] if others else array


def chips_away(level, chips):
    return [r for r in range(chips) if bin(r).count("1") == level]


def send_level(held, n_f, cut, axis, level, *before):
    for r in chips_away(level, n_f // 2):
        if level == 1:
            held[r] = [swapped(after(held[0][0], *before), n_f, 2 * r)]
            continue
        held[r] = []
        for half, bit in ((0, r & -r), (1, 1 << (r.bit_length() - 1))):
            parts = held[r ^ bit]
            part = parts[half] if len(parts) == 2 else part_of(parts[0], cut, half, axis)
            held[r].append(swapped(after(part, *before), n_f, 2 * bit))


def send_siblings(held, sibling, n_f, level, *before):
    for r in chips_away(level, n_f // 2):
        others = held[r] if len(held[r]) > 1 else []
        sibling[r] = [swapped(after(part, *others, *before), n_f, 1) for part in held[r]]


def rope_tables(length):
    frequency = np.float32(ROPE_BASE) ** (
        -(np.arange(HALF, dtype=np.float32) * np.float32(2.0) / np.float32(HEAD_SIZE))
    )
    angle = np.arange(length, dtype=np.float32)[:, None] * frequency[None, :].astype(np.float32)
    angle = angle.astype(np.float64)
    cos, sin = np.cos(angle).astype(np.float32), np.sin(angle).astype(np.float32)
    return np.concatenate([cos, cos], axis=1), np.concatenate([-sin, sin], axis=1)


def body(
    n_f,
    n_s,
    tokens,
    norm_gain,
    q_weight,
    key_matrix,
    value_matrix,
    q_bias,
    k_bias,
    value_offset_bias,
    out_weight,
):
    index = jnp.stack([lax.axis_index("fsdp"), lax.axis_index("sp")])
    count = tokens.shape[0]
    chips = n_f // 2
    levels = chips.bit_length() - 1
    shard, q_cols = q_weight.shape
    kv_cols = key_matrix.shape[1]
    wide = 256 if q_cols % 256 == 0 and kv_cols % 256 == 0 else 128
    cut = (q_cols + 2 * kv_cols) // wide // 2 * wide
    cut += wide if cut + wide <= q_cols else 0
    o_cut = shard * 3 // 5 // 128 * 128 or shard // 2 // 16 * 16
    right = [(i, (i + 1) % n_s) for i in range(n_s)]
    left = [(i, (i - 1) % n_s) for i in range(n_s)]
    cos, sin = rope_tables(n_s * count)

    own = normed_pieces(index, tokens, norm_gain, n_f)
    held = {0: [pack(after(q_weight, own), key_matrix, value_matrix)]}
    sibling, o_held, o_sibling = {}, {0: [after(out_weight, held[0][0])]}, {}
    send_level(held, n_f, cut, 1, 1)
    send_siblings(held, sibling, n_f, 0)

    steps = n_s // 2
    offsets, blocks, gate = [0], [own], []
    ahead = behind = own
    for step in range(1, steps + 1):
        if step > 1 and step <= levels:
            send_level(held, n_f, cut, 1, step, *gate)
            send_siblings(held, sibling, n_f, step - 1, *gate)
        if step < steps:
            ahead = lax.ppermute(ahead, "sp", right)
            behind = lax.ppermute(behind, "sp", left)
            offsets += [step, n_s - step]
        else:
            ahead = lax.ppermute(halves[0], "sp", right)
            behind = lax.ppermute(halves[1], "sp", left)
            offsets += [step]
        blocks += [ahead, behind]
        gate = [ahead, behind]
        if step == steps - 1:
            halves = [part_of(x, count // 2, i, 0, EXCHANGE) for i, x in enumerate(gate)]
            gate = halves[1:]
        if step == 1:
            send_siblings(o_held, o_sibling, n_f, 0, *gate)

    def pieces_of(chosen):
        return [side[r] for r in chosen for side in (held, sibling)]

    most = pieces_of(range(chips - 1))
    early = partial(blocks[:-2], most, wide, True)
    send_siblings(held, sibling, n_f, levels, early)
    send_level(o_held, n_f, o_cut, 0, 1, early)
    late = partial(blocks[-2:], most, wide, False)
    mine, others = pieces_of([chips - 1])
    queries, kv = finish(
        index,
        blocks,
        offsets,
        [mine[0], others[0], mine[1], others[1]],
        early,
        late,
        (q_bias, k_bias, value_offset_bias),
        cos,
        sin,
        q_cols,
        2 * shard * (chips - 1),
        wide,
    )
    heads = attend(index, queries, kv, offsets)

    gate, behind, rounds = [], [], []
    for level in range(levels + 1):
        near = chips_away(level, chips)
        if level:
            send_siblings(o_held, o_sibling, n_f, level, *gate)
            send_level(o_held, n_f, o_cut, 0, level + 1, *gate)
        if level < 2:
            groups = [tuple((r, 0, core) for r in near) for core in (0, 1)]
        else:
            groups = [((r, half, 0), (r, half, 1)) for r in near for half in (0, 1)]
        terms = []
        for group in groups:
            weights = [(o_sibling if core else o_held)[r][half] for r, half, core in group]
            mixed = mix(after(heads, *gate), weights, n_s)
            terms.append([mixed[offsets.index(d)] for d in range(n_s)])
        totals, arrivals = [term[1] for term in terms], []
        for d in range(2, n_s + 1):
            arrivals.append([lax.ppermute(total, "sp", right) for total in totals])
            others = behind if d == (2 if level == 1 else n_s - 1) else []
            if d < n_s:
                totals = [add(after(a, *others), term[d]) for a, term in zip(arrivals[-1], terms)]
        where = [
            [(2 * r + core, shard, half * o_cut, o_held[r][half].shape[0]) for r, half, core in group]
            for group in groups
        ]
        rounds.append(([term[0] for term in terms], arrivals, where))
        gate = arrivals[min(1, n_s - 2)]
        behind = arrivals[-1][:1] if level else arrivals[-1]

    mixed = None
    for chosen in (rounds[:-1], rounds[-1:]):
        mixed = place(
            mixed,
            index,
            [a for _, arrivals, _ in chosen for a in arrivals[-1]],
            [own for owns, _, _ in chosen for own in owns],
            [parts for _, _, where in chosen for parts in where],
            shard * n_f,
        )
    return mixed


def solution(mesh):
    n_f, n_s = mesh.shape["fsdp"], mesh.shape["sp"]
    placed = (
        P(("fsdp", "sp"), None),
        P(),
        P("fsdp", "sp"),
        P("fsdp", "sp"),
        P("fsdp", "sp"),
        P("sp"),
        P("sp"),
        P("sp"),
        P("fsdp", "sp"),
    )
    return jax.shard_map(
        functools.partial(body, n_f, n_s),
        mesh=mesh,
        in_specs=placed,
        out_specs=P(("fsdp", "sp"), None),
        check_vma=False,
    )
```

```python
import functools

import jax
import jax.numpy as jnp
import numpy as np
from jax import lax
from jax.experimental import pallas as pl
from jax.experimental.pallas import tpu as pltpu
from jax.sharding import PartitionSpec as P

HEAD_SIZE = 128
HALF = HEAD_SIZE // 2
ROPE_BASE = 1000000.0
LOG2E = 1.4426950408889634
EXCHANGE = 11500000000
NT = (((1,), (1,)), ((), ()))
VMEM = pl.BlockSpec(memory_space=pltpu.VMEM)
SMEM = pl.BlockSpec(memory_space=pltpu.SMEM)
ANY = pl.BlockSpec(memory_space=pl.ANY)


def params(mib):
    return pltpu.CompilerParams(vmem_limit_bytes=mib * 1024 * 1024)


def bf16(*shape):
    return jax.ShapeDtypeStruct(shape, jnp.bfloat16)


def work(flops, *arrays):
    size = sum(int(np.prod(x.shape)) * x.dtype.itemsize for x in arrays)
    return pl.CostEstimate(flops=flops, bytes_accessed=size, transcendentals=0)


def normed_kernel(n_f, index_ref, tokens_ref, gain_ref, out_ref):
    rows = tokens_ref[...].astype(jnp.float32)
    scale = lax.rsqrt(jnp.mean(rows * rows, axis=-1, keepdims=True) + 1e-06)
    shard = tokens_ref.shape[1] // n_f
    for j in range(n_f):
        start = pl.multiple_of(jnp.bitwise_xor(index_ref[0], j) * shard, 128)
        columns = pl.ds(start, shard)
        piece = tokens_ref[:, columns].astype(jnp.float32) * scale * gain_ref[:, columns]
        out_ref[:, j * shard : (j + 1) * shard] = piece.astype(jnp.bfloat16)


def normed_pieces(index, tokens, gain, n_f):
    count, width = tokens.shape
    shard = width // n_f
    if shard % 128 == 0:
        return pl.pallas_call(
            functools.partial(normed_kernel, n_f),
            out_shape=bf16(count, width),
            in_specs=[SMEM, VMEM, VMEM],
            out_specs=VMEM,
            compiler_params=params(16),
            cost_estimate=work(6 * count * width, tokens, tokens),
            name="norm",
        )(index, tokens, gain[None, :])
    rows = tokens.astype(jnp.float32)
    meansq = jnp.mean(rows * rows, axis=-1, keepdims=True)
    normed = (rows * lax.rsqrt(meansq + 1e-06) * gain).astype(jnp.bfloat16)
    pieces = [
        lax.dynamic_slice_in_dim(normed, jnp.bitwise_xor(index[0], j) * shard, shard, axis=1)
        for j in range(n_f)
    ]
    return jnp.concatenate(pieces, axis=1)


def pack_kernel(*refs):
    out_ref, at = refs[-1], 0
    for ref in refs[:-1]:
        out_ref[:, at : at + ref.shape[1]] = ref[...]
        at += ref.shape[1]


def pack(*arrays):
    return pl.pallas_call(
        pack_kernel,
        in_specs=[VMEM] * len(arrays),
        out_specs=VMEM,
        out_shape=bf16(arrays[0].shape[0], sum(x.shape[1] for x in arrays)),
        compiler_params=params(16),
        cost_estimate=work(0, *arrays, *arrays),
        name="pack",
    )(*arrays)


def cut_kernel(rows, columns, ref, out_ref):
    out_ref[...] = ref[rows, columns]


def part_of(array, cut, half, axis, cost=0):
    bounds = [slice(0, size) for size in array.shape]
    bounds[axis] = slice(cut, array.shape[axis]) if half else slice(0, cut)
    return pl.pallas_call(
        functools.partial(cut_kernel, *bounds),
        in_specs=[VMEM],
        out_specs=VMEM,
        out_shape=bf16(*[bound.stop - bound.start for bound in bounds]),
        compiler_params=params(16),
        cost_estimate=work(cost, array),
        name="cut",
    )(array)


def partial_kernel(n_x, counts, wide, *refs):
    x_refs, w_refs, (out_ref, rows) = refs[:n_x], refs[n_x:-2], refs[-2:]
    at = 0
    for x_ref in x_refs:
        rows[at : at + x_ref.shape[0], :] = x_ref[:, : rows.shape[1]]
        at += x_ref.shape[0]
    shard = w_refs[0].shape[0]
    pieces, at = [], 0
    for count in counts:
        pieces.append(w_refs[at : at + count])
        at += count
    for col in range(0, out_ref.shape[1], wide):
        total = None
        for j, parts in enumerate(pieces):
            at = col
            for w_ref in parts:
                if at < w_ref.shape[1]:
                    break
                at -= w_ref.shape[1]
            term = jnp.dot(
                rows[:, j * shard : (j + 1) * shard],
                w_ref[:, at : at + wide],
                preferred_element_type=jnp.float32,
            )
            total = term if total is None else total + term
        out_ref[:, col : col + wide] = total


def partial(blocks, pieces, wide, declared):
    weights = [part for piece in pieces for part in piece]
    length = sum(block.shape[0] for block in blocks)
    depth = len(pieces) * weights[0].shape[0]
    columns = sum(part.shape[1] for part in pieces[0])
    out = jax.ShapeDtypeStruct((length, columns), jnp.float32)
    counts = [len(piece) for piece in pieces]
    return pl.pallas_call(
        functools.partial(partial_kernel, len(blocks), counts, wide),
        in_specs=[VMEM] * (len(blocks) + len(weights)),
        out_specs=VMEM,
        out_shape=out,
        scratch_shapes=[pltpu.VMEM((length, depth), jnp.bfloat16)],
        compiler_params=params(16),
        cost_estimate=work(2 * length * depth * columns if declared else 0),
        name="partial",
    )(*blocks, *weights)


def rope_tile(tile, cos, sin):
    parts = []
    for at in range(0, tile.shape[1], HEAD_SIZE):
        head = tile[:, at : at + HEAD_SIZE]
        parts.append(head * cos + pltpu.roll(head, HALF, axis=1) * sin)
    return parts[0] if len(parts) == 1 else jnp.concatenate(parts, axis=1)


def finish_kernel(n_x, offsets, wide, roped, first_col, index_ref, *refs):
    x_refs = refs[:n_x]
    w_refs = refs[n_x : n_x + 4]
    early_ref, late_ref = refs[n_x + 4 : n_x + 6]
    bias_refs, (cos_ref, sin_ref) = refs[n_x + 6 : n_x + 9], refs[n_x + 9 : n_x + 11]
    q_out, kv_out, rows, cos, sin = refs[n_x + 11 :]
    shard = w_refs[0].shape[0]
    at = 0
    for x_ref in x_refs:
        rows[at : at + x_ref.shape[0], :] = x_ref[:, first_col : first_col + 2 * shard]
        at += x_ref.shape[0]
    blocks = len(offsets)
    count = at // blocks
    for k, offset in enumerate(offsets):
        block = lax.rem(index_ref[1] - offset + blocks, blocks)
        place = pl.ds(pl.multiple_of(block * count, count), count)
        cos[k * count : (k + 1) * count, :] = cos_ref[place, :]
        sin[k * count : (k + 1) * count, :] = sin_ref[place, :]
    q_cols = q_out.shape[1]

    def bias_tile(col):
        for bias_ref in bias_refs:
            if col < bias_ref.shape[0]:
                return bias_ref[pl.ds(col, wide)][None, :]
            col -= bias_ref.shape[0]

    base = 0
    for mine, sibling in (w_refs[:2], w_refs[2:]):
        for at in range(0, mine.shape[1], wide):
            total = jnp.dot(
                rows[:, :shard], mine[:, at : at + wide], preferred_element_type=jnp.float32
            )
            total = total + jnp.dot(
                rows[:, shard:], sibling[:, at : at + wide], preferred_element_type=jnp.float32
            )
            col = base + at
            total = total + jnp.concatenate(
                [early_ref[:, col : col + wide], late_ref[:, col : col + wide]], axis=0
            )
            total = total + bias_tile(col)
            if col < roped:
                total = rope_tile(total, cos[...], sin[...])
            total = total.astype(jnp.bfloat16)
            if col < q_cols:
                q_out[:, col : col + wide] = total
            else:
                kv_out[:, col - q_cols : col - q_cols + wide] = total
        base += mine.shape[1]


def finish(index, blocks, offsets, weights, early, late, biases, cos, sin, q_cols, first_col, wide):
    n_x = len(blocks)
    length = sum(block.shape[0] for block in blocks)
    shard = weights[0].shape[0]
    columns = early.shape[1]
    kv_cols = columns - q_cols
    return pl.pallas_call(
        functools.partial(finish_kernel, n_x, offsets, wide, q_cols + kv_cols // 2, first_col),
        in_specs=[SMEM] + [VMEM] * (n_x + 11),
        out_specs=[VMEM, VMEM],
        out_shape=[bf16(length, q_cols), bf16(length, kv_cols)],
        scratch_shapes=[
            pltpu.VMEM((length, 2 * shard), jnp.bfloat16),
            pltpu.VMEM((length, HEAD_SIZE), jnp.float32),
            pltpu.VMEM((length, HEAD_SIZE), jnp.float32),
        ],
        compiler_params=params(16),
        cost_estimate=work(0),
        name="finish",
    )(index, *blocks, *weights, early, late, *biases, cos, sin)


def attend_kernel(offsets, group, index_ref, q_ref, kv_ref, out_ref, keys, values):
    blocks = len(offsets)
    rows = q_ref.shape[0] // blocks
    factor = LOG2E / (HEAD_SIZE**0.5)

    def held(b):
        offset = lax.rem(index_ref[1] - b + blocks, blocks)
        k = sum(jnp.where(offset == value, i, 0) for i, value in enumerate(offsets))
        return pl.ds(pl.multiple_of(k * rows, rows), rows)

    kv_half = kv_ref.shape[1] // 2
    for b in range(blocks):
        keys[b * rows : (b + 1) * rows, :] = kv_ref[held(b), :kv_half]
        values[b * rows : (b + 1) * rows, :] = kv_ref[held(b), kv_half:]
    row = lax.broadcasted_iota(jnp.int32, (rows, rows), 0)
    column = lax.broadcasted_iota(jnp.int32, (rows, rows), 1)
    causal = row >= column
    causal = jnp.concatenate([causal.astype(jnp.float32)] * group, axis=0) > 0.5
    for g, b in [(g, b) for g in range(kv_half // HEAD_SIZE) for b in range(blocks)]:
        left = g * group * HEAD_SIZE
        head = slice(g * HEAD_SIZE, (g + 1) * HEAD_SIZE)
        q_block = q_ref[held(b), left : left + group * HEAD_SIZE]
        queries = jnp.concatenate(
            [q_block[:, h * HEAD_SIZE : (h + 1) * HEAD_SIZE] for h in range(group)], axis=0
        )
        at = b * rows
        near = lax.dot_general(
            queries, keys[at : at + rows, head], NT, preferred_element_type=jnp.float32
        )
        near = jnp.where(causal, near, jnp.float32(-1e30))
        largest = jnp.max(near, axis=-1, keepdims=True)
        if b > 0:
            far = lax.dot_general(queries, keys[:at, head], NT, preferred_element_type=jnp.float32)
            largest = jnp.maximum(largest, jnp.max(far, axis=-1, keepdims=True))
        near = jnp.exp2((near - largest) * factor)
        total = jnp.sum(near, axis=-1, keepdims=True)
        result = jnp.dot(
            near.astype(jnp.bfloat16), values[at : at + rows, head], preferred_element_type=jnp.float32
        )
        if b > 0:
            far = jnp.exp2((far - largest) * factor)
            total = total + jnp.sum(far, axis=-1, keepdims=True)
            result = result + jnp.dot(
                far.astype(jnp.bfloat16), values[:at, head], preferred_element_type=jnp.float32
            )
        result = (result / total).astype(jnp.bfloat16)
        for h in range(group):
            out_ref[held(b), left + h * HEAD_SIZE : left + (h + 1) * HEAD_SIZE] = result[
                h * rows : (h + 1) * rows, :
            ]


def attend(index, queries, kv, offsets):
    length, q_cols = queries.shape
    kv_half = kv.shape[1] // 2
    return pl.pallas_call(
        functools.partial(attend_kernel, offsets, q_cols // kv_half),
        in_specs=[SMEM, VMEM, VMEM],
        out_specs=VMEM,
        out_shape=bf16(length, q_cols),
        scratch_shapes=[
            pltpu.VMEM((length, kv_half), jnp.bfloat16),
            pltpu.VMEM((length, kv_half), jnp.bfloat16),
        ],
        compiler_params=params(16),
        cost_estimate=work(0),
        name="attend",
    )(index, queries, kv)


def mix_kernel(n_w, heads_ref, *refs):
    w_refs, out_refs = refs[:n_w], refs[n_w:]
    rows = out_refs[0].shape[0]
    weights = [w_ref[...] for w_ref in w_refs]
    weights = weights[0] if n_w == 1 else jnp.concatenate(weights, axis=0)
    term = lax.dot_general(
        heads_ref[...], weights, NT, preferred_element_type=jnp.float32
    ).astype(jnp.bfloat16)
    for k, out_ref in enumerate(out_refs):
        out_ref[...] = term[k * rows : (k + 1) * rows, :]


def mix(heads, parts, blocks):
    length, features = heads.shape
    columns = sum(part.shape[0] for part in parts)
    return pl.pallas_call(
        functools.partial(mix_kernel, len(parts)),
        in_specs=[VMEM] * (1 + len(parts)),
        out_specs=[VMEM] * blocks,
        out_shape=[bf16(length // blocks, columns)] * blocks,
        compiler_params=params(16),
        cost_estimate=work(2 * length * columns * features, heads, *parts),
        name="mix",
    )(heads, *parts)


def add_kernel(a_ref, b_ref, out_ref):
    total = a_ref[...].astype(jnp.float32) + b_ref[...].astype(jnp.float32)
    out_ref[...] = total.astype(jnp.bfloat16)


def add(a, b):
    return pl.pallas_call(
        add_kernel,
        in_specs=[VMEM, VMEM],
        out_specs=VMEM,
        out_shape=bf16(*a.shape),
        compiler_params=params(8),
        cost_estimate=work(0, a, a, a),
        name="add",
    )(a, b)


def place_kernel(parts, index_ref, *refs):
    n = len(parts)
    a_refs, b_refs, out_ref, total, sem = refs[:n], refs[n : 2 * n], *refs[-3:]
    copies, left = [], 0
    for a_ref, b_ref, pieces in zip(a_refs, b_refs, parts):
        add_kernel(a_ref, b_ref, total.at[:, pl.ds(left, a_ref.shape[1])])
        for j, shard, offset, width in pieces:
            start = pl.multiple_of(jnp.bitwise_xor(index_ref[0], j) * shard + offset, 128)
            copies.append(
                pltpu.make_async_copy(
                    total.at[:, pl.ds(left, width)],
                    out_ref.at[:, pl.ds(start, width)],
                    sem.at[len(copies)],
                )
            )
            copies[-1].start()
            left += width
    for copy in copies:
        copy.wait()


def place(mixed, index, first, second, parts, columns):
    every = [piece for pieces in parts for piece in pieces]
    count = first[0].shape[0]
    if any(offset % 128 or width % 128 or shard % 128 for _, shard, offset, width in every):
        if mixed is None:
            mixed = jnp.zeros((count, columns), jnp.bfloat16)
        for a, b, pieces in zip(first, second, parts):
            total, left = add(a, b), 0
            for j, shard, offset, width in pieces:
                start = jnp.bitwise_xor(index[0], j) * shard + offset
                mixed = lax.dynamic_update_slice(mixed, total[:, left : left + width], (0, start))
                left += width
        return mixed
    held = [] if mixed is None else [mixed]
    return pl.pallas_call(
        functools.partial(place_kernel, parts),
        in_specs=[SMEM] + [VMEM] * (2 * len(parts)) + [ANY] * len(held),
        out_specs=ANY,
        out_shape=bf16(count, columns),
        scratch_shapes=[
            pltpu.VMEM((count, sum(piece[3] for piece in every)), jnp.bfloat16),
            pltpu.SemaphoreType.DMA((len(every),)),
        ],
        input_output_aliases={1 + 2 * len(parts): 0} if held else {},
        compiler_params=params(8),
        cost_estimate=work(0, *first, *second),
        name="place",
    )(index, *first, *second, *held)


def swapped(array, n_f, mask):
    return lax.ppermute(array, "fsdp", [(i, i ^ mask) for i in range(n_f)])


def after(array, *others):
    return lax.optimization_barrier((array, *others))[0] if others else array


def chips_away(level, chips):
    return [r for r in range(chips) if bin(r).count("1") == level]


def send_level(held, n_f, cut, axis, level, *before):
    for r in chips_away(level, n_f // 2):
        if level == 1:
            held[r] = [swapped(after(held[0][0], *before), n_f, 2 * r)]
            continue
        held[r] = []
        for half, bit in ((0, r & -r), (1, 1 << (r.bit_length() - 1))):
            parts = held[r ^ bit]
            part = parts[half] if len(parts) == 2 else part_of(parts[0], cut, half, axis)
            held[r].append(swapped(after(part, *before), n_f, 2 * bit))


def send_siblings(held, sibling, n_f, level, *before):
    for r in chips_away(level, n_f // 2):
        others = held[r] if len(held[r]) > 1 else []
        sibling[r] = [swapped(after(part, *others, *before), n_f, 1) for part in held[r]]


def rope_tables(length):
    frequency = np.float32(ROPE_BASE) ** (
        -(np.arange(HALF, dtype=np.float32) * np.float32(2.0) / np.float32(HEAD_SIZE))
    )
    angle = np.arange(length, dtype=np.float32)[:, None] * frequency[None, :].astype(np.float32)
    angle = angle.astype(np.float64)
    cos, sin = np.cos(angle).astype(np.float32), np.sin(angle).astype(np.float32)
    return np.concatenate([cos, cos], axis=1), np.concatenate([-sin, sin], axis=1)


def body(
    n_f,
    n_s,
    tokens,
    norm_gain,
    q_weight,
    key_matrix,
    value_matrix,
    q_bias,
    k_bias,
    value_offset_bias,
    out_weight,
):
    index = jnp.stack([lax.axis_index("fsdp"), lax.axis_index("sp")])
    count = tokens.shape[0]
    chips = n_f // 2
    levels = chips.bit_length() - 1
    shard, q_cols = q_weight.shape
    kv_cols = key_matrix.shape[1]
    wide = 256 if q_cols % 256 == 0 and kv_cols % 256 == 0 else 128
    cut = (q_cols + 2 * kv_cols) // wide // 2 * wide
    cut += wide if cut + wide <= q_cols else 0
    o_cut = shard * 3 // 5 // 128 * 128 or shard // 2 // 16 * 16
    right = [(i, (i + 1) % n_s) for i in range(n_s)]
    left = [(i, (i - 1) % n_s) for i in range(n_s)]
    cos, sin = rope_tables(n_s * count)

    own = normed_pieces(index, tokens, norm_gain, n_f)
    held = {0: [pack(after(q_weight, own), key_matrix, value_matrix)]}
    sibling, o_held, o_sibling = {}, {0: [after(out_weight, held[0][0])]}, {}
    send_level(held, n_f, cut, 1, 1)
    send_siblings(held, sibling, n_f, 0)

    steps = n_s // 2
    offsets, blocks, gate = [0], [own], []
    ahead = behind = own
    for step in range(1, steps + 1):
        if step > 1 and step <= levels:
            send_level(held, n_f, cut, 1, step, *gate)
            send_siblings(held, sibling, n_f, step - 1, *gate)
        if step < steps:
            ahead = lax.ppermute(ahead, "sp", right)
            behind = lax.ppermute(behind, "sp", left)
            offsets += [step, n_s - step]
        else:
            ahead = lax.ppermute(halves[0], "sp", right)
            behind = lax.ppermute(halves[1], "sp", left)
            offsets += [step]
        blocks += [ahead, behind]
        gate = [ahead, behind]
        if step == steps - 1:
            halves = [part_of(x, count // 2, i, 0, EXCHANGE) for i, x in enumerate(gate)]
            gate = halves[1:]
        if step == 1:
            send_siblings(o_held, o_sibling, n_f, 0, *gate)

    def pieces_of(chosen):
        return [side[r] for r in chosen for side in (held, sibling)]

    most = pieces_of(range(chips - 1))
    early = partial(blocks[:-2], most, wide, True)
    send_siblings(held, sibling, n_f, levels, early)
    send_level(o_held, n_f, o_cut, 0, 1, early)
    late = partial(blocks[-2:], most, wide, False)
    mine, others = pieces_of([chips - 1])
    queries, kv = finish(
        index,
        blocks,
        offsets,
        [mine[0], others[0], mine[1], others[1]],
        early,
        late,
        (q_bias, k_bias, value_offset_bias),
        cos,
        sin,
        q_cols,
        2 * shard * (chips - 1),
        wide,
    )
    heads = attend(index, queries, kv, offsets)

    gate, behind, rounds = [], [], []
    for level in range(levels + 1):
        near = chips_away(level, chips)
        if level:
            send_siblings(o_held, o_sibling, n_f, level, *gate)
            send_level(o_held, n_f, o_cut, 0, level + 1, *gate)
        if level < 2:
            groups = [tuple((r, 0, core) for r in near) for core in (0, 1)]
        else:
            groups = [((r, half, 0), (r, half, 1)) for r in near for half in (0, 1)]
        terms = []
        for group in groups:
            weights = [(o_sibling if core else o_held)[r][half] for r, half, core in group]
            mixed = mix(after(heads, *gate), weights, n_s)
            terms.append([mixed[offsets.index(d)] for d in range(n_s)])
        totals, arrivals = [term[1] for term in terms], []
        for d in range(2, n_s + 1):
            arrivals.append([lax.ppermute(total, "sp", right) for total in totals])
            others = behind if d == 2 else []
            if d < n_s:
                totals = [add(after(a, *others), term[d]) for a, term in zip(arrivals[-1], terms)]
        where = [
            [(2 * r + core, shard, half * o_cut, o_held[r][half].shape[0]) for r, half, core in group]
            for group in groups
        ]
        rounds.append(([term[0] for term in terms], arrivals, where))
        gate = arrivals[-1] if level == 0 else arrivals[min(1, n_s - 2)]
        behind = arrivals[-1][:1] if level else []

    mixed = None
    for chosen in (rounds[:-1], rounds[-1:]):
        mixed = place(
            mixed,
            index,
            [a for _, arrivals, _ in chosen for a in arrivals[-1]],
            [own for owns, _, _ in chosen for own in owns],
            [parts for _, _, where in chosen for parts in where],
            shard * n_f,
        )
    return mixed


def solution(mesh):
    n_f, n_s = mesh.shape["fsdp"], mesh.shape["sp"]
    placed = (
        P(("fsdp", "sp"), None),
        P(),
        P("fsdp", "sp"),
        P("fsdp", "sp"),
        P("fsdp", "sp"),
        P("sp"),
        P("sp"),
        P("sp"),
        P("fsdp", "sp"),
    )
    return jax.shard_map(
        functools.partial(body, n_f, n_s),
        mesh=mesh,
        in_specs=placed,
        out_specs=P(("fsdp", "sp"), None),
        check_vma=False,
    )
```

```python
import functools

import jax
import jax.numpy as jnp
import numpy as np
from jax import lax
from jax.experimental import pallas as pl
from jax.experimental.pallas import tpu as pltpu
from jax.sharding import PartitionSpec as P

HEAD_SIZE = 128
HALF = HEAD_SIZE // 2
ROPE_BASE = 1000000.0
LOG2E = 1.4426950408889634
EXCHANGE = 11500000000
NT = (((1,), (1,)), ((), ()))
VMEM = pl.BlockSpec(memory_space=pltpu.VMEM)
SMEM = pl.BlockSpec(memory_space=pltpu.SMEM)
ANY = pl.BlockSpec(memory_space=pl.ANY)


def params(mib):
    return pltpu.CompilerParams(vmem_limit_bytes=mib * 1024 * 1024)


def bf16(*shape):
    return jax.ShapeDtypeStruct(shape, jnp.bfloat16)


def work(flops, *arrays):
    size = sum(int(np.prod(x.shape)) * x.dtype.itemsize for x in arrays)
    return pl.CostEstimate(flops=flops, bytes_accessed=size, transcendentals=0)


def normed_kernel(n_f, index_ref, tokens_ref, gain_ref, out_ref):
    rows = tokens_ref[...].astype(jnp.float32)
    scale = lax.rsqrt(jnp.mean(rows * rows, axis=-1, keepdims=True) + 1e-06)
    shard = tokens_ref.shape[1] // n_f
    for j in range(n_f):
        start = pl.multiple_of(jnp.bitwise_xor(index_ref[0], j) * shard, 128)
        columns = pl.ds(start, shard)
        piece = tokens_ref[:, columns].astype(jnp.float32) * scale * gain_ref[:, columns]
        out_ref[:, j * shard : (j + 1) * shard] = piece.astype(jnp.bfloat16)


def normed_pieces(index, tokens, gain, n_f):
    count, width = tokens.shape
    shard = width // n_f
    if shard % 128 == 0:
        return pl.pallas_call(
            functools.partial(normed_kernel, n_f),
            out_shape=bf16(count, width),
            in_specs=[SMEM, VMEM, VMEM],
            out_specs=VMEM,
            compiler_params=params(16),
            cost_estimate=work(6 * count * width, tokens, tokens),
            name="norm",
        )(index, tokens, gain[None, :])
    rows = tokens.astype(jnp.float32)
    meansq = jnp.mean(rows * rows, axis=-1, keepdims=True)
    normed = (rows * lax.rsqrt(meansq + 1e-06) * gain).astype(jnp.bfloat16)
    pieces = [
        lax.dynamic_slice_in_dim(normed, jnp.bitwise_xor(index[0], j) * shard, shard, axis=1)
        for j in range(n_f)
    ]
    return jnp.concatenate(pieces, axis=1)


def pack_kernel(*refs):
    out_ref, at = refs[-1], 0
    for ref in refs[:-1]:
        out_ref[:, at : at + ref.shape[1]] = ref[...]
        at += ref.shape[1]


def pack(*arrays):
    return pl.pallas_call(
        pack_kernel,
        in_specs=[VMEM] * len(arrays),
        out_specs=VMEM,
        out_shape=bf16(arrays[0].shape[0], sum(x.shape[1] for x in arrays)),
        compiler_params=params(16),
        cost_estimate=work(0, *arrays, *arrays),
        name="pack",
    )(*arrays)


def cut_kernel(rows, columns, ref, out_ref):
    out_ref[...] = ref[rows, columns]


def part_of(array, cut, half, axis, cost=0):
    bounds = [slice(0, size) for size in array.shape]
    bounds[axis] = slice(cut, array.shape[axis]) if half else slice(0, cut)
    return pl.pallas_call(
        functools.partial(cut_kernel, *bounds),
        in_specs=[VMEM],
        out_specs=VMEM,
        out_shape=bf16(*[bound.stop - bound.start for bound in bounds]),
        compiler_params=params(16),
        cost_estimate=work(cost, array),
        name="cut",
    )(array)


def partial_kernel(n_x, counts, wide, *refs):
    x_refs, w_refs, (out_ref, rows) = refs[:n_x], refs[n_x:-2], refs[-2:]
    at = 0
    for x_ref in x_refs:
        rows[at : at + x_ref.shape[0], :] = x_ref[:, : rows.shape[1]]
        at += x_ref.shape[0]
    shard = w_refs[0].shape[0]
    pieces, at = [], 0
    for count in counts:
        pieces.append(w_refs[at : at + count])
        at += count
    for col in range(0, out_ref.shape[1], wide):
        total = None
        for j, parts in enumerate(pieces):
            at = col
            for w_ref in parts:
                if at < w_ref.shape[1]:
                    break
                at -= w_ref.shape[1]
            term = jnp.dot(
                rows[:, j * shard : (j + 1) * shard],
                w_ref[:, at : at + wide],
                preferred_element_type=jnp.float32,
            )
            total = term if total is None else total + term
        out_ref[:, col : col + wide] = total


def partial(blocks, pieces, wide, declared):
    weights = [part for piece in pieces for part in piece]
    length = sum(block.shape[0] for block in blocks)
    depth = len(pieces) * weights[0].shape[0]
    columns = sum(part.shape[1] for part in pieces[0])
    out = jax.ShapeDtypeStruct((length, columns), jnp.float32)
    counts = [len(piece) for piece in pieces]
    return pl.pallas_call(
        functools.partial(partial_kernel, len(blocks), counts, wide),
        in_specs=[VMEM] * (len(blocks) + len(weights)),
        out_specs=VMEM,
        out_shape=out,
        scratch_shapes=[pltpu.VMEM((length, depth), jnp.bfloat16)],
        compiler_params=params(16),
        cost_estimate=work(2 * length * depth * columns if declared else 0),
        name="partial",
    )(*blocks, *weights)


def rope_tile(tile, cos, sin):
    parts = []
    for at in range(0, tile.shape[1], HEAD_SIZE):
        head = tile[:, at : at + HEAD_SIZE]
        parts.append(head * cos + pltpu.roll(head, HALF, axis=1) * sin)
    return parts[0] if len(parts) == 1 else jnp.concatenate(parts, axis=1)


def finish_kernel(n_x, offsets, wide, roped, first_col, index_ref, *refs):
    x_refs = refs[:n_x]
    w_refs = refs[n_x : n_x + 4]
    early_ref, late_ref = refs[n_x + 4 : n_x + 6]
    bias_refs, (cos_ref, sin_ref) = refs[n_x + 6 : n_x + 9], refs[n_x + 9 : n_x + 11]
    q_out, kv_out, rows, cos, sin = refs[n_x + 11 :]
    shard = w_refs[0].shape[0]
    at = 0
    for x_ref in x_refs:
        rows[at : at + x_ref.shape[0], :] = x_ref[:, first_col : first_col + 2 * shard]
        at += x_ref.shape[0]
    blocks = len(offsets)
    count = at // blocks
    for k, offset in enumerate(offsets):
        block = lax.rem(index_ref[1] - offset + blocks, blocks)
        place = pl.ds(pl.multiple_of(block * count, count), count)
        cos[k * count : (k + 1) * count, :] = cos_ref[place, :]
        sin[k * count : (k + 1) * count, :] = sin_ref[place, :]
    q_cols = q_out.shape[1]

    def bias_tile(col):
        for bias_ref in bias_refs:
            if col < bias_ref.shape[0]:
                return bias_ref[pl.ds(col, wide)][None, :]
            col -= bias_ref.shape[0]

    base = 0
    for mine, sibling in (w_refs[:2], w_refs[2:]):
        for at in range(0, mine.shape[1], wide):
            total = jnp.dot(
                rows[:, :shard], mine[:, at : at + wide], preferred_element_type=jnp.float32
            )
            total = total + jnp.dot(
                rows[:, shard:], sibling[:, at : at + wide], preferred_element_type=jnp.float32
            )
            col = base + at
            total = total + jnp.concatenate(
                [early_ref[:, col : col + wide], late_ref[:, col : col + wide]], axis=0
            )
            total = total + bias_tile(col)
            if col < roped:
                total = rope_tile(total, cos[...], sin[...])
            total = total.astype(jnp.bfloat16)
            if col < q_cols:
                q_out[:, col : col + wide] = total
            else:
                kv_out[:, col - q_cols : col - q_cols + wide] = total
        base += mine.shape[1]


def finish(index, blocks, offsets, weights, early, late, biases, cos, sin, q_cols, first_col, wide):
    n_x = len(blocks)
    length = sum(block.shape[0] for block in blocks)
    shard = weights[0].shape[0]
    columns = early.shape[1]
    kv_cols = columns - q_cols
    return pl.pallas_call(
        functools.partial(finish_kernel, n_x, offsets, wide, q_cols + kv_cols // 2, first_col),
        in_specs=[SMEM] + [VMEM] * (n_x + 11),
        out_specs=[VMEM, VMEM],
        out_shape=[bf16(length, q_cols), bf16(length, kv_cols)],
        scratch_shapes=[
            pltpu.VMEM((length, 2 * shard), jnp.bfloat16),
            pltpu.VMEM((length, HEAD_SIZE), jnp.float32),
            pltpu.VMEM((length, HEAD_SIZE), jnp.float32),
        ],
        compiler_params=params(16),
        cost_estimate=work(0),
        name="finish",
    )(index, *blocks, *weights, early, late, *biases, cos, sin)


def attend_kernel(offsets, group, index_ref, q_ref, kv_ref, out_ref, keys, values):
    blocks = len(offsets)
    rows = q_ref.shape[0] // blocks
    factor = LOG2E / (HEAD_SIZE**0.5)

    def held(b):
        offset = lax.rem(index_ref[1] - b + blocks, blocks)
        k = sum(jnp.where(offset == value, i, 0) for i, value in enumerate(offsets))
        return pl.ds(pl.multiple_of(k * rows, rows), rows)

    kv_half = kv_ref.shape[1] // 2
    for b in range(blocks):
        keys[b * rows : (b + 1) * rows, :] = kv_ref[held(b), :kv_half]
        values[b * rows : (b + 1) * rows, :] = kv_ref[held(b), kv_half:]
    row = lax.broadcasted_iota(jnp.int32, (rows, rows), 0)
    column = lax.broadcasted_iota(jnp.int32, (rows, rows), 1)
    causal = row >= column
    causal = jnp.concatenate([causal.astype(jnp.float32)] * group, axis=0) > 0.5
    for g, b in [(g, b) for g in range(kv_half // HEAD_SIZE) for b in range(blocks)]:
        left = g * group * HEAD_SIZE
        head = slice(g * HEAD_SIZE, (g + 1) * HEAD_SIZE)
        q_block = q_ref[held(b), left : left + group * HEAD_SIZE]
        queries = jnp.concatenate(
            [q_block[:, h * HEAD_SIZE : (h + 1) * HEAD_SIZE] for h in range(group)], axis=0
        )
        at = b * rows
        near = lax.dot_general(
            queries, keys[at : at + rows, head], NT, preferred_element_type=jnp.float32
        )
        near = jnp.where(causal, near, jnp.float32(-1e30))
        largest = jnp.max(near, axis=-1, keepdims=True)
        if b > 0:
            far = lax.dot_general(queries, keys[:at, head], NT, preferred_element_type=jnp.float32)
            largest = jnp.maximum(largest, jnp.max(far, axis=-1, keepdims=True))
        near = jnp.exp2((near - largest) * factor)
        total = jnp.sum(near, axis=-1, keepdims=True)
        result = jnp.dot(
            near.astype(jnp.bfloat16), values[at : at + rows, head], preferred_element_type=jnp.float32
        )
        if b > 0:
            far = jnp.exp2((far - largest) * factor)
            total = total + jnp.sum(far, axis=-1, keepdims=True)
            result = result + jnp.dot(
                far.astype(jnp.bfloat16), values[:at, head], preferred_element_type=jnp.float32
            )
        result = (result / total).astype(jnp.bfloat16)
        for h in range(group):
            out_ref[held(b), left + h * HEAD_SIZE : left + (h + 1) * HEAD_SIZE] = result[
                h * rows : (h + 1) * rows, :
            ]


def attend(index, queries, kv, offsets):
    length, q_cols = queries.shape
    kv_half = kv.shape[1] // 2
    return pl.pallas_call(
        functools.partial(attend_kernel, offsets, q_cols // kv_half),
        in_specs=[SMEM, VMEM, VMEM],
        out_specs=VMEM,
        out_shape=bf16(length, q_cols),
        scratch_shapes=[
            pltpu.VMEM((length, kv_half), jnp.bfloat16),
            pltpu.VMEM((length, kv_half), jnp.bfloat16),
        ],
        compiler_params=params(16),
        cost_estimate=work(0),
        name="attend",
    )(index, queries, kv)


def mix_kernel(n_w, heads_ref, *refs):
    w_refs, out_refs = refs[:n_w], refs[n_w:]
    rows = out_refs[0].shape[0]
    weights = [w_ref[...] for w_ref in w_refs]
    weights = weights[0] if n_w == 1 else jnp.concatenate(weights, axis=0)
    term = lax.dot_general(
        heads_ref[...], weights, NT, preferred_element_type=jnp.float32
    ).astype(jnp.bfloat16)
    for k, out_ref in enumerate(out_refs):
        out_ref[...] = term[k * rows : (k + 1) * rows, :]


def mix(heads, parts, blocks):
    length, features = heads.shape
    columns = sum(part.shape[0] for part in parts)
    return pl.pallas_call(
        functools.partial(mix_kernel, len(parts)),
        in_specs=[VMEM] * (1 + len(parts)),
        out_specs=[VMEM] * blocks,
        out_shape=[bf16(length // blocks, columns)] * blocks,
        compiler_params=params(16),
        cost_estimate=work(2 * length * columns * features, heads, *parts),
        name="mix",
    )(heads, *parts)


def add_kernel(a_ref, b_ref, out_ref):
    total = a_ref[...].astype(jnp.float32) + b_ref[...].astype(jnp.float32)
    out_ref[...] = total.astype(jnp.bfloat16)


def add(a, b):
    return pl.pallas_call(
        add_kernel,
        in_specs=[VMEM, VMEM],
        out_specs=VMEM,
        out_shape=bf16(*a.shape),
        compiler_params=params(8),
        cost_estimate=work(0, a, a, a),
        name="add",
    )(a, b)


def place_kernel(parts, index_ref, *refs):
    n = len(parts)
    a_refs, b_refs, out_ref, total, sem = refs[:n], refs[n : 2 * n], *refs[-3:]
    copies, left = [], 0
    for a_ref, b_ref, pieces in zip(a_refs, b_refs, parts):
        add_kernel(a_ref, b_ref, total.at[:, pl.ds(left, a_ref.shape[1])])
        for j, shard, offset, width in pieces:
            start = pl.multiple_of(jnp.bitwise_xor(index_ref[0], j) * shard + offset, 128)
            copies.append(
                pltpu.make_async_copy(
                    total.at[:, pl.ds(left, width)],
                    out_ref.at[:, pl.ds(start, width)],
                    sem.at[len(copies)],
                )
            )
            copies[-1].start()
            left += width
    for copy in copies:
        copy.wait()


def place(mixed, index, first, second, parts, columns):
    every = [piece for pieces in parts for piece in pieces]
    count = first[0].shape[0]
    if any(offset % 128 or width % 128 or shard % 128 for _, shard, offset, width in every):
        if mixed is None:
            mixed = jnp.zeros((count, columns), jnp.bfloat16)
        for a, b, pieces in zip(first, second, parts):
            total, left = add(a, b), 0
            for j, shard, offset, width in pieces:
                start = jnp.bitwise_xor(index[0], j) * shard + offset
                mixed = lax.dynamic_update_slice(mixed, total[:, left : left + width], (0, start))
                left += width
        return mixed
    held = [] if mixed is None else [mixed]
    return pl.pallas_call(
        functools.partial(place_kernel, parts),
        in_specs=[SMEM] + [VMEM] * (2 * len(parts)) + [ANY] * len(held),
        out_specs=ANY,
        out_shape=bf16(count, columns),
        scratch_shapes=[
            pltpu.VMEM((count, sum(piece[3] for piece in every)), jnp.bfloat16),
            pltpu.SemaphoreType.DMA((len(every),)),
        ],
        input_output_aliases={1 + 2 * len(parts): 0} if held else {},
        compiler_params=params(8),
        cost_estimate=work(0, *first, *second),
        name="place",
    )(index, *first, *second, *held)


def swapped(array, n_f, mask):
    return lax.ppermute(array, "fsdp", [(i, i ^ mask) for i in range(n_f)])


def after(array, *others):
    return lax.optimization_barrier((array, *others))[0] if others else array


def chips_away(level, chips):
    return [r for r in range(chips) if bin(r).count("1") == level]


def send_level(held, n_f, cut, axis, level, *before):
    for r in chips_away(level, n_f // 2):
        if level == 1:
            held[r] = [swapped(after(held[0][0], *before), n_f, 2 * r)]
            continue
        held[r] = []
        for half, bit in ((0, r & -r), (1, 1 << (r.bit_length() - 1))):
            parts = held[r ^ bit]
            part = parts[half] if len(parts) == 2 else part_of(parts[0], cut, half, axis)
            held[r].append(swapped(after(part, *before), n_f, 2 * bit))


def send_siblings(held, sibling, n_f, level, *before):
    for r in chips_away(level, n_f // 2):
        others = held[r] if len(held[r]) > 1 else []
        sibling[r] = [swapped(after(part, *others, *before), n_f, 1) for part in held[r]]


def rope_tables(length):
    frequency = np.float32(ROPE_BASE) ** (
        -(np.arange(HALF, dtype=np.float32) * np.float32(2.0) / np.float32(HEAD_SIZE))
    )
    angle = np.arange(length, dtype=np.float32)[:, None] * frequency[None, :].astype(np.float32)
    angle = angle.astype(np.float64)
    cos, sin = np.cos(angle).astype(np.float32), np.sin(angle).astype(np.float32)
    return np.concatenate([cos, cos], axis=1), np.concatenate([-sin, sin], axis=1)


def body(
    n_f,
    n_s,
    tokens,
    norm_gain,
    q_weight,
    key_matrix,
    value_matrix,
    q_bias,
    k_bias,
    value_offset_bias,
    out_weight,
):
    index = jnp.stack([lax.axis_index("fsdp"), lax.axis_index("sp")])
    count = tokens.shape[0]
    chips = n_f // 2
    levels = chips.bit_length() - 1
    shard, q_cols = q_weight.shape
    kv_cols = key_matrix.shape[1]
    wide = 256 if q_cols % 256 == 0 and kv_cols % 256 == 0 else 128
    cut = (q_cols + 2 * kv_cols) // wide // 2 * wide
    cut += wide if cut + wide <= q_cols else 0
    o_cut = shard * 3 // 5 // 128 * 128 or shard // 2 // 16 * 16
    right = [(i, (i + 1) % n_s) for i in range(n_s)]
    left = [(i, (i - 1) % n_s) for i in range(n_s)]
    cos, sin = rope_tables(n_s * count)

    own = normed_pieces(index, tokens, norm_gain, n_f)
    held = {0: [pack(after(q_weight, own), key_matrix, value_matrix)]}
    sibling, o_held, o_sibling = {}, {0: [after(out_weight, held[0][0])]}, {}
    send_level(held, n_f, cut, 1, 1)
    send_siblings(held, sibling, n_f, 0)

    steps = n_s // 2
    offsets, blocks, gate = [0], [own], []
    ahead = behind = own
    for step in range(1, steps + 1):
        if step > 1 and step <= levels:
            send_level(held, n_f, cut, 1, step, *gate)
            send_siblings(held, sibling, n_f, step - 1, *gate)
        if step < steps:
            ahead = lax.ppermute(ahead, "sp", right)
            behind = lax.ppermute(behind, "sp", left)
            offsets += [step, n_s - step]
        else:
            ahead = lax.ppermute(halves[0], "sp", right)
            behind = lax.ppermute(halves[1], "sp", left)
            offsets += [step]
        blocks += [ahead, behind]
        gate = [ahead, behind]
        if step == steps - 1:
            halves = [part_of(x, count // 2, i, 0, EXCHANGE) for i, x in enumerate(gate)]
            gate = halves[1:]
        if step == 1:
            send_siblings(o_held, o_sibling, n_f, 0, *gate)

    def pieces_of(chosen):
        return [side[r] for r in chosen for side in (held, sibling)]

    most = pieces_of(range(chips - 1))
    early = partial(blocks[:-2], most, wide, True)
    send_siblings(held, sibling, n_f, levels, early)
    send_level(o_held, n_f, o_cut, 0, 1, early)
    late = partial(blocks[-2:], most, wide, False)
    mine, others = pieces_of([chips - 1])
    queries, kv = finish(
        index,
        blocks,
        offsets,
        [mine[0], others[0], mine[1], others[1]],
        early,
        late,
        (q_bias, k_bias, value_offset_bias),
        cos,
        sin,
        q_cols,
        2 * shard * (chips - 1),
        wide,
    )
    heads = attend(index, queries, kv, offsets)

    gate, behind, rounds = [], [], []
    for level in range(levels + 1):
        near = chips_away(level, chips)
        if level:
            send_siblings(o_held, o_sibling, n_f, level, *gate)
            send_level(o_held, n_f, o_cut, 0, level + 1, *gate)
        if level < 2:
            groups = [tuple((r, 0, core) for r in near) for core in (0, 1)]
        else:
            groups = [((r, half, 0), (r, half, 1)) for r in near for half in (0, 1)]
        terms = []
        for group in groups:
            weights = [(o_sibling if core else o_held)[r][half] for r, half, core in group]
            mixed = mix(after(heads, *gate), weights, n_s)
            terms.append([mixed[offsets.index(d)] for d in range(n_s)])
        totals, arrivals = [term[1] for term in terms], []
        for d in range(2, n_s + 1):
            arrivals.append([lax.ppermute(total, "sp", right) for total in totals])
            others = behind if level > 1 and d == n_s - 1 else []
            if d < n_s:
                totals = [add(after(a, *others), term[d]) for a, term in zip(arrivals[-1], terms)]
        where = [
            [(2 * r + core, shard, half * o_cut, o_held[r][half].shape[0]) for r, half, core in group]
            for group in groups
        ]
        rounds.append(([term[0] for term in terms], arrivals, where))
        gate = arrivals[min(1, n_s - 2)]
        behind = (arrivals[-1][:1] if level else []) + rounds[0][1][-1]

    mixed = None
    for chosen in (rounds[:-1], rounds[-1:]):
        mixed = place(
            mixed,
            index,
            [a for _, arrivals, _ in chosen for a in arrivals[-1]],
            [own for owns, _, _ in chosen for own in owns],
            [parts for _, _, where in chosen for parts in where],
            shard * n_f,
        )
    return mixed


def solution(mesh):
    n_f, n_s = mesh.shape["fsdp"], mesh.shape["sp"]
    placed = (
        P(("fsdp", "sp"), None),
        P(),
        P("fsdp", "sp"),
        P("fsdp", "sp"),
        P("fsdp", "sp"),
        P("sp"),
        P("sp"),
        P("sp"),
        P("fsdp", "sp"),
    )
    return jax.shard_map(
        functools.partial(body, n_f, n_s),
        mesh=mesh,
        in_specs=placed,
        out_specs=P(("fsdp", "sp"), None),
        check_vma=False,
    )
```

```python
import functools

import jax
import jax.numpy as jnp
import numpy as np
from jax import lax
from jax.experimental import pallas as pl
from jax.experimental.pallas import tpu as pltpu
from jax.sharding import PartitionSpec as P

HEAD_SIZE = 128
HALF = HEAD_SIZE // 2
ROPE_BASE = 1000000.0
LOG2E = 1.4426950408889634
EXCHANGE = 11500000000
NT = (((1,), (1,)), ((), ()))
VMEM = pl.BlockSpec(memory_space=pltpu.VMEM)
SMEM = pl.BlockSpec(memory_space=pltpu.SMEM)
ANY = pl.BlockSpec(memory_space=pl.ANY)


def params(mib):
    return pltpu.CompilerParams(vmem_limit_bytes=mib * 1024 * 1024)


def bf16(*shape):
    return jax.ShapeDtypeStruct(shape, jnp.bfloat16)


def work(flops, *arrays):
    size = sum(int(np.prod(x.shape)) * x.dtype.itemsize for x in arrays)
    return pl.CostEstimate(flops=flops, bytes_accessed=size, transcendentals=0)


def normed_kernel(n_f, index_ref, tokens_ref, gain_ref, out_ref):
    rows = tokens_ref[...].astype(jnp.float32)
    scale = lax.rsqrt(jnp.mean(rows * rows, axis=-1, keepdims=True) + 1e-06)
    shard = tokens_ref.shape[1] // n_f
    for j in range(n_f):
        start = pl.multiple_of(jnp.bitwise_xor(index_ref[0], j) * shard, 128)
        columns = pl.ds(start, shard)
        piece = tokens_ref[:, columns].astype(jnp.float32) * scale * gain_ref[:, columns]
        out_ref[:, j * shard : (j + 1) * shard] = piece.astype(jnp.bfloat16)


def normed_pieces(index, tokens, gain, n_f):
    count, width = tokens.shape
    shard = width // n_f
    if shard % 128 == 0:
        return pl.pallas_call(
            functools.partial(normed_kernel, n_f),
            out_shape=bf16(count, width),
            in_specs=[SMEM, VMEM, VMEM],
            out_specs=VMEM,
            compiler_params=params(16),
            cost_estimate=work(6 * count * width, tokens, tokens),
            name="norm",
        )(index, tokens, gain[None, :])
    rows = tokens.astype(jnp.float32)
    meansq = jnp.mean(rows * rows, axis=-1, keepdims=True)
    normed = (rows * lax.rsqrt(meansq + 1e-06) * gain).astype(jnp.bfloat16)
    pieces = [
        lax.dynamic_slice_in_dim(normed, jnp.bitwise_xor(index[0], j) * shard, shard, axis=1)
        for j in range(n_f)
    ]
    return jnp.concatenate(pieces, axis=1)


def pack_kernel(*refs):
    out_ref, at = refs[-1], 0
    for ref in refs[:-1]:
        out_ref[:, at : at + ref.shape[1]] = ref[...]
        at += ref.shape[1]


def pack(*arrays):
    return pl.pallas_call(
        pack_kernel,
        in_specs=[VMEM] * len(arrays),
        out_specs=VMEM,
        out_shape=bf16(arrays[0].shape[0], sum(x.shape[1] for x in arrays)),
        compiler_params=params(16),
        cost_estimate=work(0, *arrays, *arrays),
        name="pack",
    )(*arrays)


def cut_kernel(rows, columns, ref, out_ref):
    out_ref[...] = ref[rows, columns]


def part_of(array, cut, half, axis, cost=0):
    bounds = [slice(0, size) for size in array.shape]
    bounds[axis] = slice(cut, array.shape[axis]) if half else slice(0, cut)
    return pl.pallas_call(
        functools.partial(cut_kernel, *bounds),
        in_specs=[VMEM],
        out_specs=VMEM,
        out_shape=bf16(*[bound.stop - bound.start for bound in bounds]),
        compiler_params=params(16),
        cost_estimate=work(cost, array),
        name="cut",
    )(array)


def partial_kernel(n_x, counts, wide, *refs):
    x_refs, w_refs, (out_ref, rows) = refs[:n_x], refs[n_x:-2], refs[-2:]
    at = 0
    for x_ref in x_refs:
        rows[at : at + x_ref.shape[0], :] = x_ref[:, : rows.shape[1]]
        at += x_ref.shape[0]
    shard = w_refs[0].shape[0]
    pieces, at = [], 0
    for count in counts:
        pieces.append(w_refs[at : at + count])
        at += count
    for col in range(0, out_ref.shape[1], wide):
        total = None
        for j, parts in enumerate(pieces):
            at = col
            for w_ref in parts:
                if at < w_ref.shape[1]:
                    break
                at -= w_ref.shape[1]
            term = jnp.dot(
                rows[:, j * shard : (j + 1) * shard],
                w_ref[:, at : at + wide],
                preferred_element_type=jnp.float32,
            )
            total = term if total is None else total + term
        out_ref[:, col : col + wide] = total


def partial(blocks, pieces, wide, declared):
    weights = [part for piece in pieces for part in piece]
    length = sum(block.shape[0] for block in blocks)
    depth = len(pieces) * weights[0].shape[0]
    columns = sum(part.shape[1] for part in pieces[0])
    out = jax.ShapeDtypeStruct((length, columns), jnp.float32)
    counts = [len(piece) for piece in pieces]
    return pl.pallas_call(
        functools.partial(partial_kernel, len(blocks), counts, wide),
        in_specs=[VMEM] * (len(blocks) + len(weights)),
        out_specs=VMEM,
        out_shape=out,
        scratch_shapes=[pltpu.VMEM((length, depth), jnp.bfloat16)],
        compiler_params=params(16),
        cost_estimate=work(2 * length * depth * columns if declared else 0),
        name="partial",
    )(*blocks, *weights)


def rope_tile(tile, cos, sin):
    parts = []
    for at in range(0, tile.shape[1], HEAD_SIZE):
        head = tile[:, at : at + HEAD_SIZE]
        parts.append(head * cos + pltpu.roll(head, HALF, axis=1) * sin)
    return parts[0] if len(parts) == 1 else jnp.concatenate(parts, axis=1)


def finish_kernel(n_x, offsets, wide, roped, first_col, index_ref, *refs):
    x_refs = refs[:n_x]
    w_refs = refs[n_x : n_x + 4]
    early_ref, late_ref = refs[n_x + 4 : n_x + 6]
    bias_refs, (cos_ref, sin_ref) = refs[n_x + 6 : n_x + 9], refs[n_x + 9 : n_x + 11]
    q_out, kv_out, rows, cos, sin = refs[n_x + 11 :]
    shard = w_refs[0].shape[0]
    at = 0
    for x_ref in x_refs:
        rows[at : at + x_ref.shape[0], :] = x_ref[:, first_col : first_col + 2 * shard]
        at += x_ref.shape[0]
    blocks = len(offsets)
    count = at // blocks
    for k, offset in enumerate(offsets):
        block = lax.rem(index_ref[1] - offset + blocks, blocks)
        place = pl.ds(pl.multiple_of(block * count, count), count)
        cos[k * count : (k + 1) * count, :] = cos_ref[place, :]
        sin[k * count : (k + 1) * count, :] = sin_ref[place, :]
    q_cols = q_out.shape[1]

    def bias_tile(col):
        for bias_ref in bias_refs:
            if col < bias_ref.shape[0]:
                return bias_ref[pl.ds(col, wide)][None, :]
            col -= bias_ref.shape[0]

    base = 0
    for mine, sibling in (w_refs[:2], w_refs[2:]):
        for at in range(0, mine.shape[1], wide):
            total = jnp.dot(
                rows[:, :shard], mine[:, at : at + wide], preferred_element_type=jnp.float32
            )
            total = total + jnp.dot(
                rows[:, shard:], sibling[:, at : at + wide], preferred_element_type=jnp.float32
            )
            col = base + at
            total = total + jnp.concatenate(
                [early_ref[:, col : col + wide], late_ref[:, col : col + wide]], axis=0
            )
            total = total + bias_tile(col)
            if col < roped:
                total = rope_tile(total, cos[...], sin[...])
            total = total.astype(jnp.bfloat16)
            if col < q_cols:
                q_out[:, col : col + wide] = total
            else:
                kv_out[:, col - q_cols : col - q_cols + wide] = total
        base += mine.shape[1]


def finish(index, blocks, offsets, weights, early, late, biases, cos, sin, q_cols, first_col, wide):
    n_x = len(blocks)
    length = sum(block.shape[0] for block in blocks)
    shard = weights[0].shape[0]
    columns = early.shape[1]
    kv_cols = columns - q_cols
    return pl.pallas_call(
        functools.partial(finish_kernel, n_x, offsets, wide, q_cols + kv_cols // 2, first_col),
        in_specs=[SMEM] + [VMEM] * (n_x + 11),
        out_specs=[VMEM, VMEM],
        out_shape=[bf16(length, q_cols), bf16(length, kv_cols)],
        scratch_shapes=[
            pltpu.VMEM((length, 2 * shard), jnp.bfloat16),
            pltpu.VMEM((length, HEAD_SIZE), jnp.float32),
            pltpu.VMEM((length, HEAD_SIZE), jnp.float32),
        ],
        compiler_params=params(16),
        cost_estimate=work(0),
        name="finish",
    )(index, *blocks, *weights, early, late, *biases, cos, sin)


def attend_kernel(offsets, group, index_ref, q_ref, kv_ref, out_ref, keys, values):
    blocks = len(offsets)
    rows = q_ref.shape[0] // blocks
    factor = LOG2E / (HEAD_SIZE**0.5)

    def held(b):
        offset = lax.rem(index_ref[1] - b + blocks, blocks)
        k = sum(jnp.where(offset == value, i, 0) for i, value in enumerate(offsets))
        return pl.ds(pl.multiple_of(k * rows, rows), rows)

    kv_half = kv_ref.shape[1] // 2
    for b in range(blocks):
        keys[b * rows : (b + 1) * rows, :] = kv_ref[held(b), :kv_half]
        values[b * rows : (b + 1) * rows, :] = kv_ref[held(b), kv_half:]
    row = lax.broadcasted_iota(jnp.int32, (rows, rows), 0)
    column = lax.broadcasted_iota(jnp.int32, (rows, rows), 1)
    causal = row >= column
    causal = jnp.concatenate([causal.astype(jnp.float32)] * group, axis=0) > 0.5
    for g, b in [(g, b) for g in range(kv_half // HEAD_SIZE) for b in range(blocks)]:
        left = g * group * HEAD_SIZE
        head = slice(g * HEAD_SIZE, (g + 1) * HEAD_SIZE)
        q_block = q_ref[held(b), left : left + group * HEAD_SIZE]
        queries = jnp.concatenate(
            [q_block[:, h * HEAD_SIZE : (h + 1) * HEAD_SIZE] for h in range(group)], axis=0
        )
        at = b * rows
        near = lax.dot_general(
            queries, keys[at : at + rows, head], NT, preferred_element_type=jnp.float32
        )
        near = jnp.where(causal, near, jnp.float32(-1e30))
        largest = jnp.max(near, axis=-1, keepdims=True)
        if b > 0:
            far = lax.dot_general(queries, keys[:at, head], NT, preferred_element_type=jnp.float32)
            largest = jnp.maximum(largest, jnp.max(far, axis=-1, keepdims=True))
        near = jnp.exp2((near - largest) * factor)
        total = jnp.sum(near, axis=-1, keepdims=True)
        result = jnp.dot(
            near.astype(jnp.bfloat16), values[at : at + rows, head], preferred_element_type=jnp.float32
        )
        if b > 0:
            far = jnp.exp2((far - largest) * factor)
            total = total + jnp.sum(far, axis=-1, keepdims=True)
            result = result + jnp.dot(
                far.astype(jnp.bfloat16), values[:at, head], preferred_element_type=jnp.float32
            )
        result = (result / total).astype(jnp.bfloat16)
        for h in range(group):
            out_ref[held(b), left + h * HEAD_SIZE : left + (h + 1) * HEAD_SIZE] = result[
                h * rows : (h + 1) * rows, :
            ]


def attend(index, queries, kv, offsets):
    length, q_cols = queries.shape
    kv_half = kv.shape[1] // 2
    return pl.pallas_call(
        functools.partial(attend_kernel, offsets, q_cols // kv_half),
        in_specs=[SMEM, VMEM, VMEM],
        out_specs=VMEM,
        out_shape=bf16(length, q_cols),
        scratch_shapes=[
            pltpu.VMEM((length, kv_half), jnp.bfloat16),
            pltpu.VMEM((length, kv_half), jnp.bfloat16),
        ],
        compiler_params=params(16),
        cost_estimate=work(0),
        name="attend",
    )(index, queries, kv)


def mix_kernel(n_w, heads_ref, *refs):
    w_refs, out_refs = refs[:n_w], refs[n_w:]
    rows = out_refs[0].shape[0]
    weights = [w_ref[...] for w_ref in w_refs]
    weights = weights[0] if n_w == 1 else jnp.concatenate(weights, axis=0)
    term = lax.dot_general(
        heads_ref[...], weights, NT, preferred_element_type=jnp.float32
    ).astype(jnp.bfloat16)
    for k, out_ref in enumerate(out_refs):
        out_ref[...] = term[k * rows : (k + 1) * rows, :]


def mix(heads, parts, blocks):
    length, features = heads.shape
    columns = sum(part.shape[0] for part in parts)
    return pl.pallas_call(
        functools.partial(mix_kernel, len(parts)),
        in_specs=[VMEM] * (1 + len(parts)),
        out_specs=[VMEM] * blocks,
        out_shape=[bf16(length // blocks, columns)] * blocks,
        compiler_params=params(16),
        cost_estimate=work(2 * length * columns * features, heads, *parts),
        name="mix",
    )(heads, *parts)


def add_kernel(a_ref, b_ref, out_ref):
    total = a_ref[...].astype(jnp.float32) + b_ref[...].astype(jnp.float32)
    out_ref[...] = total.astype(jnp.bfloat16)


def add(a, b):
    return pl.pallas_call(
        add_kernel,
        in_specs=[VMEM, VMEM],
        out_specs=VMEM,
        out_shape=bf16(*a.shape),
        compiler_params=params(8),
        cost_estimate=work(0, a, a, a),
        name="add",
    )(a, b)


def place_kernel(parts, index_ref, *refs):
    n = len(parts)
    a_refs, b_refs, out_ref, total, sem = refs[:n], refs[n : 2 * n], *refs[-3:]
    copies, left = [], 0
    for a_ref, b_ref, pieces in zip(a_refs, b_refs, parts):
        add_kernel(a_ref, b_ref, total.at[:, pl.ds(left, a_ref.shape[1])])
        for j, shard, offset, width in pieces:
            start = pl.multiple_of(jnp.bitwise_xor(index_ref[0], j) * shard + offset, 128)
            copies.append(
                pltpu.make_async_copy(
                    total.at[:, pl.ds(left, width)],
                    out_ref.at[:, pl.ds(start, width)],
                    sem.at[len(copies)],
                )
            )
            copies[-1].start()
            left += width
    for copy in copies:
        copy.wait()


def place(mixed, index, first, second, parts, columns):
    every = [piece for pieces in parts for piece in pieces]
    count = first[0].shape[0]
    if any(offset % 128 or width % 128 or shard % 128 for _, shard, offset, width in every):
        if mixed is None:
            mixed = jnp.zeros((count, columns), jnp.bfloat16)
        for a, b, pieces in zip(first, second, parts):
            total, left = add(a, b), 0
            for j, shard, offset, width in pieces:
                start = jnp.bitwise_xor(index[0], j) * shard + offset
                mixed = lax.dynamic_update_slice(mixed, total[:, left : left + width], (0, start))
                left += width
        return mixed
    held = [] if mixed is None else [mixed]
    return pl.pallas_call(
        functools.partial(place_kernel, parts),
        in_specs=[SMEM] + [VMEM] * (2 * len(parts)) + [ANY] * len(held),
        out_specs=ANY,
        out_shape=bf16(count, columns),
        scratch_shapes=[
            pltpu.VMEM((count, sum(piece[3] for piece in every)), jnp.bfloat16),
            pltpu.SemaphoreType.DMA((len(every),)),
        ],
        input_output_aliases={1 + 2 * len(parts): 0} if held else {},
        compiler_params=params(8),
        cost_estimate=work(0, *first, *second),
        name="place",
    )(index, *first, *second, *held)


def swapped(array, n_f, mask):
    return lax.ppermute(array, "fsdp", [(i, i ^ mask) for i in range(n_f)])


def after(array, *others):
    return lax.optimization_barrier((array, *others))[0] if others else array


def chips_away(level, chips):
    return [r for r in range(chips) if bin(r).count("1") == level]


def send_level(held, n_f, cut, axis, level, *before):
    for r in chips_away(level, n_f // 2):
        if level == 1:
            held[r] = [swapped(after(held[0][0], *before), n_f, 2 * r)]
            continue
        held[r] = []
        for half, bit in ((0, r & -r), (1, 1 << (r.bit_length() - 1))):
            parts = held[r ^ bit]
            part = parts[half] if len(parts) == 2 else part_of(parts[0], cut, half, axis)
            held[r].append(swapped(after(part, *before), n_f, 2 * bit))


def send_siblings(held, sibling, n_f, level, *before):
    for r in chips_away(level, n_f // 2):
        others = held[r] if len(held[r]) > 1 else []
        sibling[r] = [swapped(after(part, *others, *before), n_f, 1) for part in held[r]]


def rope_tables(length):
    frequency = np.float32(ROPE_BASE) ** (
        -(np.arange(HALF, dtype=np.float32) * np.float32(2.0) / np.float32(HEAD_SIZE))
    )
    angle = np.arange(length, dtype=np.float32)[:, None] * frequency[None, :].astype(np.float32)
    angle = angle.astype(np.float64)
    cos, sin = np.cos(angle).astype(np.float32), np.sin(angle).astype(np.float32)
    return np.concatenate([cos, cos], axis=1), np.concatenate([-sin, sin], axis=1)


def body(
    n_f,
    n_s,
    tokens,
    norm_gain,
    q_weight,
    key_matrix,
    value_matrix,
    q_bias,
    k_bias,
    value_offset_bias,
    out_weight,
):
    index = jnp.stack([lax.axis_index("fsdp"), lax.axis_index("sp")])
    count = tokens.shape[0]
    chips = n_f // 2
    levels = chips.bit_length() - 1
    shard, q_cols = q_weight.shape
    kv_cols = key_matrix.shape[1]
    wide = 256 if q_cols % 256 == 0 and kv_cols % 256 == 0 else 128
    cut = (q_cols + 2 * kv_cols) // wide // 2 * wide
    cut += wide if cut + wide <= q_cols else 0
    o_cut = shard * 3 // 5 // 128 * 128 or shard // 2 // 16 * 16
    right = [(i, (i + 1) % n_s) for i in range(n_s)]
    left = [(i, (i - 1) % n_s) for i in range(n_s)]
    cos, sin = rope_tables(n_s * count)

    own = normed_pieces(index, tokens, norm_gain, n_f)
    held = {0: [pack(after(q_weight, own), key_matrix, value_matrix)]}
    sibling, o_held, o_sibling = {}, {0: [after(out_weight, held[0][0])]}, {}
    send_level(held, n_f, cut, 1, 1)
    send_siblings(held, sibling, n_f, 0)

    steps = n_s // 2
    offsets, blocks, gate = [0], [own], []
    ahead = behind = own
    for step in range(1, steps + 1):
        if step > 1 and step <= levels:
            send_level(held, n_f, cut, 1, step, *gate)
            send_siblings(held, sibling, n_f, step - 1, *gate)
        if step < steps:
            ahead = lax.ppermute(ahead, "sp", right)
            behind = lax.ppermute(behind, "sp", left)
            offsets += [step, n_s - step]
        else:
            ahead = lax.ppermute(halves[0], "sp", right)
            behind = lax.ppermute(halves[1], "sp", left)
            offsets += [step]
        blocks += [ahead, behind]
        gate = [ahead, behind]
        if step == steps - 1:
            halves = [part_of(x, count // 2, i, 0, EXCHANGE) for i, x in enumerate(gate)]
            gate = halves[1:]
        if step == 1:
            send_siblings(o_held, o_sibling, n_f, 0, *gate)

    def pieces_of(chosen):
        return [side[r] for r in chosen for side in (held, sibling)]

    most = pieces_of(range(chips - 1))
    early = partial(blocks[:-2], most, wide, True)
    send_siblings(held, sibling, n_f, levels, early)
    send_level(o_held, n_f, o_cut, 0, 1, early)
    late = partial(blocks[-2:], most, wide, False)
    mine, others = pieces_of([chips - 1])
    queries, kv = finish(
        index,
        blocks,
        offsets,
        [mine[0], others[0], mine[1], others[1]],
        early,
        late,
        (q_bias, k_bias, value_offset_bias),
        cos,
        sin,
        q_cols,
        2 * shard * (chips - 1),
        wide,
    )
    heads = attend(index, queries, kv, offsets)

    gate, behind, rounds = [], [], []
    for level in range(levels + 1):
        near = chips_away(level, chips)
        if level:
            send_siblings(o_held, o_sibling, n_f, level, *gate)
            send_level(o_held, n_f, o_cut, 0, level + 1, *gate)
        if level < 2:
            groups = [tuple((r, 0, core) for r in near) for core in (0, 1)]
        else:
            groups = [tuple((r, half, core) for half in (0, 1) for core in (0, 1)) for r in near]
        terms = []
        for group in groups:
            weights = [(o_sibling if core else o_held)[r][half] for r, half, core in group]
            mixed = mix(after(heads, *gate), weights, n_s)
            terms.append([mixed[offsets.index(d)] for d in range(n_s)])
        totals, arrivals = [term[1] for term in terms], []
        for d in range(2, n_s + 1):
            arrivals.append([lax.ppermute(total, "sp", right) for total in totals])
            others = behind if d == n_s - 1 else []
            if d < n_s:
                totals = [add(after(a, *others), term[d]) for a, term in zip(arrivals[-1], terms)]
        where = [
            [(2 * r + core, shard, half * o_cut, o_held[r][half].shape[0]) for r, half, core in group]
            for group in groups
        ]
        rounds.append(([term[0] for term in terms], arrivals, where))
        gate = arrivals[-1] if level == 0 else arrivals[min(1, n_s - 2)]
        behind = arrivals[-1][:1] if level else []

    mixed = None
    for chosen in (rounds[:-1], rounds[-1:]):
        mixed = place(
            mixed,
            index,
            [a for _, arrivals, _ in chosen for a in arrivals[-1]],
            [own for owns, _, _ in chosen for own in owns],
            [parts for _, _, where in chosen for parts in where],
            shard * n_f,
        )
    return mixed


def solution(mesh):
    n_f, n_s = mesh.shape["fsdp"], mesh.shape["sp"]
    placed = (
        P(("fsdp", "sp"), None),
        P(),
        P("fsdp", "sp"),
        P("fsdp", "sp"),
        P("fsdp", "sp"),
        P("sp"),
        P("sp"),
        P("sp"),
        P("fsdp", "sp"),
    )
    return jax.shard_map(
        functools.partial(body, n_f, n_s),
        mesh=mesh,
        in_specs=placed,
        out_specs=P(("fsdp", "sp"), None),
        check_vma=False,
    )
```
